32 devices in a mesh: dp: 8 (over y, x, core), section: 4 (over z).
Axes of the slice: x: 2, y: 2, z: 4, core: 2. Of those that a mesh axis runs over, the one named last changes fastest.
Arguments:
- encoder_input: bfloat16 [4, 8192, 768], P('section', 'dp'), may hold values from -6 to 6
- decoder_input: bfloat16 [4, 1024, 768], P('section', 'dp'), may hold values from -6 to 6
- cotangent: bfloat16 [4, 1024, 768], P('section', 'dp'), may hold values from -6 to 6
- pool_table: int32 [4, 8, 8, 256], P('section', 'dp'), may hold values from 0 to 1023, as said below
- retrieved: int32 [4, 1024, 1024], P('section', 'dp'), may hold values from 0 to 2047, as said below
- decoder_lengths: int32 [4, 8, 4], P('section', 'dp'), may hold values from 1 to 96, 128 in all within a row
- encoder_inward: bfloat16 [3, 768, 768], replicated, may hold values from -0.21875 to 0.21875
- encoder_outward: bfloat16 [768, 768], replicated, may hold values from -3.5 to 3.5
- encoder_biases: float32 [3, 768], replicated, may hold values from -3 to 3
- encoder_norms: float32 [2, 2, 768], replicated, may hold values from -3 to 3
- encoder_expand: bfloat16 [768, 3072], replicated, may hold values from -0.21875 to 0.21875
- encoder_expand_bias: float32 [3072], replicated, may hold values from -3 to 3
- encoder_shrink: bfloat16 [3072, 768], replicated, may hold values from -0.109375 to 0.109375
- encoder_shrink_bias: float32 [768], replicated, may hold values from -3 to 3
- self_inward: bfloat16 [3, 768, 768], replicated, may hold values from -0.21875 to 0.21875
- self_outward: bfloat16 [768, 768], replicated, may hold values from -0.625 to 0.625
- cross_inward: bfloat16 [3, 768, 768], replicated, may hold values from -0.21875 to 0.21875
- cross_outward: bfloat16 [768, 768], replicated, may hold values from -3.5 to 3.5
- decoder_biases: float32 [6, 768], replicated, may hold values from -3 to 3
- decoder_norms: float32 [3, 2, 768], replicated, may hold values from -3 to 3
- decoder_expand: bfloat16 [768, 3072], replicated, may hold values from -0.21875 to 0.21875
- decoder_expand_bias: float32 [3072], replicated, may hold values from -3 to 3
- decoder_shrink: bfloat16 [3072, 768], replicated, may hold values from -0.109375 to 0.109375
- decoder_shrink_bias: float32 [768], replicated, may hold values from -3 to 3
Outputs:
- decoder_output: bfloat16 [4, 1024, 768], P('section', 'dp')
- encoder_input_grad: float32 [4, 8192, 768], P('section', 'dp')
- decoder_input_grad: float32 [4, 1024, 768], P('section', 'dp')
- delta_encoder_inward: float32 [3, 768, 768], P(None, 'dp')
- delta_encoder_outward: float32 [768, 768], P('dp')
- delta_encoder_biases: float32 [3, 768], P(None, 'dp')
- delta_encoder_norms: float32 [2, 2, 768], P(None, None, 'dp')
- delta_encoder_expand: float32 [768, 3072], P('dp')
- delta_encoder_expand_bias: float32 [3072], P('dp')
- delta_encoder_shrink: float32 [3072, 768], P('dp')
- delta_encoder_shrink_bias: float32 [768], P('dp')
- delta_self_inward: float32 [3, 768, 768], P(None, 'dp')
- delta_self_outward: float32 [768, 768], P('dp')
- delta_cross_inward: float32 [3, 768, 768], P(None, 'dp')
- delta_cross_outward: float32 [768, 768], P('dp')
- delta_decoder_biases: float32 [6, 768], P(None, 'dp')
- delta_decoder_norms: float32 [3, 2, 768], P(None, None, 'dp')
- delta_decoder_expand: float32 [768, 3072], P('dp')
- delta_decoder_expand_bias: float32 [3072], P('dp')
- delta_decoder_shrink: float32 [3072, 768], P('dp')
- delta_decoder_shrink_bias: float32 [768], P('dp')
The draws below stay inside these ranges and needn't reach their ends.
Inputs may be any that keep to these rules, and one draw needn't show every extreme that they name: `pool_table`: within one block of 256 entries (one micro-batch, owner and requesting device) the rows are distinct. `retrieved`: A query's 1024 slots are distinct. For each micro-batch and requesting device, the slots of owner o that any query names lie among the first k_o of that owner's 256, with k_o from 128 to 256.
All inputs are finite; a program needn't handle non-finite values.
Results may differ from the reference program's by a relative error of at most 0.025.
Values may be sent and summed in bfloat16 or wider, within the bound.
A program may use at most 384 MiB of HBM per device.

```python
import math
import jax
import jax.numpy as jnp
import numpy as np
from jax import lax

D = 768
HEADS = 12
HEAD = 64
FF = 3072
SPAN = 1024
DEC_DEV = 128
NSEQ = 4
TOPK = 1024
CAP = 256
POOL = 2048
MICRO = 4
ETOK = 8192
DTOK = 1024
N_DP = 8


def draw_pool_table(key, part):
    key = jax.random.fold_in(key, 11)
    noise_draw = jax.random.randint(key, (MICRO, N_DP, N_DP, SPAN), 0, 65536)
    row_ids = jnp.arange(SPAN, dtype=jnp.int32)
    scores = noise_draw * SPAN + row_ids
    first_block = (jnp.arange(MICRO, dtype=jnp.int32)[:, None, None, None] == 0) & (jnp.arange(N_DP, dtype=jnp.int32)[None, :, None, None] == 0) & (jnp.arange(N_DP, dtype=jnp.int32)[None, None, :, None] == 0)
    scores = jnp.where(first_block & (row_ids == SPAN - 1)[None, None, None, :], -2, scores)
    scores = jnp.where(first_block & (row_ids == 0)[None, None, None, :], -1, scores)
    ordering = jnp.argsort(scores, axis=-1, stable=True)
    return ordering[..., :CAP].astype(jnp.int32)


def draw_retrieved(key, part):
    key = jax.random.fold_in(key, 23)

    def one_micro(micro_key):
        count_key, owner_key, score_key = jax.random.split(micro_key, 3)
        counts = jax.random.randint(count_key, (N_DP, N_DP), CAP // 2, CAP + 1)
        full_owner = jax.random.randint(owner_key, (N_DP, 1), 0, N_DP)
        requester_ids = jnp.arange(N_DP, dtype=jnp.int32)[:, None]
        full_owner = jnp.where(requester_ids == 0, N_DP - 1, full_owner)
        counts = jnp.where(jnp.arange(N_DP, dtype=jnp.int32)[None, :] == full_owner, CAP, counts)
        slot_index = jnp.arange(CAP, dtype=jnp.int32)
        used_slots = (slot_index[None, None, :] < counts[:, :, None]).reshape(N_DP, POOL)
        slot_ids = jnp.arange(POOL, dtype=jnp.int32)
        noise_draw = jax.random.randint(score_key, (N_DP, DEC_DEV, POOL), 0, 65536)
        scores = jnp.where(used_slots[:, None, :], noise_draw * POOL + slot_ids, -1 - slot_ids)
        forced = (jnp.arange(N_DP, dtype=jnp.int32)[:, None, None] == 0) & (jnp.arange(DEC_DEV, dtype=jnp.int32)[None, :, None] == 0) & ((slot_ids == POOL - 1) | (slot_ids == 0))[None, None, :]
        scores = jnp.where(forced, 65536 * POOL + slot_ids, scores)
        picked = lax.top_k(scores, TOPK)[1]
        return picked.reshape(N_DP * DEC_DEV, TOPK).astype(jnp.int32)
    return lax.map(one_micro, jax.random.split(key, MICRO))


def level_of(key, shape, pieces, smallest, high):
    def one(position, blocks):
        draws = jax.random.uniform(jax.random.fold_in(jax.random.fold_in(key, 6), position), (blocks,), jnp.float32, smallest / len(pieces), high / len(pieces))
        return jnp.repeat(jnp.exp(draws), shape[position] // blocks).reshape((-1,) + (1,) * (len(shape) - position - 1))

    level = one(*pieces[0])
    for cut in pieces[1:]:
        level = level * one(*cut)
    return level


def profile(count, total, most, skew):
    loads = [(1 << 20) // math.isqrt(grade ** skew) + 1 for grade in range(2, count + 1)]
    spare, holding = total - most - (count - 1), [1] * (count - 1)
    while spare > 0:
        candidates = [i for i in range(count - 1) if holding[i] < most]
        pool, remaining = sum([loads[i] for i in candidates]), spare
        for i in candidates:
            extra = min(most - holding[i], max(1, remaining * loads[i] // pool), spare)
            holding[i] = holding[i] + extra
            spare = spare - extra
    return np.array([most] + holding)


def ragged_sizes(rng, amount, total, reach, skew):
    if amount == 2:
        one = jax.random.randint(rng, (), max(1, total - reach), min(reach, total - 1) + 1)
        return jnp.stack([one, total - one])
    tallies = jnp.asarray(profile(amount, total, reach, skew), jnp.int32)
    twos = (amount - 1) // 2
    giver, receiver = tallies[1:1 + 2 * twos:2], tallies[2:2 + 2 * twos:2]
    slack = jnp.minimum(giver - 1, reach - receiver)
    moved = jax.random.randint(jax.random.fold_in(rng, 1), (twos,), 0, 1 << 20) % (slack + 1)
    tallies = tallies.at[1:1 + 2 * twos:2].set(giver - moved).at[2:2 + 2 * twos:2].set(receiver + moved)
    return tallies[jax.random.permutation(jax.random.fold_in(rng, 2), amount)]


def normal_values(stream_key, dims, scale, limit, shards=(), kind=jnp.bfloat16):
    entries = scale * jax.random.normal(stream_key, dims, jnp.float32)
    if shards:
        entries = entries * level_of(stream_key, dims, shards, -0.22, 0.18)
    return jnp.clip(entries, -limit, limit).astype(kind)


def setup_inputs(seed: int = 0) -> dict:
    key_list = jax.random.split(jax.random.key(seed), 25)
    return {
        "encoder_input": normal_values(key_list[0], (MICRO, ETOK, D), 1.0, 6.0, ((0, 4), (1, 8))),
        "decoder_input": normal_values(key_list[1], (MICRO, DTOK, D), 1.0, 6.0, ((0, 4), (1, 8))),
        "cotangent": normal_values(key_list[2], (MICRO, DTOK, D), 1.0, 6.0, ((0, 4), (1, 8))),
        "pool_table": draw_pool_table(jax.random.fold_in(key_list[24], 71), 0),
        "retrieved": draw_retrieved(jax.random.fold_in(key_list[24], 71), 0),
        "decoder_lengths": jax.vmap(lambda own: ragged_sizes(own, NSEQ, DEC_DEV, 3 * DEC_DEV // 4, 2))(jax.random.split(key_list[5], MICRO * N_DP)).reshape((MICRO, N_DP, NSEQ)).astype(jnp.int32),
        "encoder_inward": normal_values(key_list[6], (3, D, D), D ** -0.5, 0.21875),
        "encoder_outward": normal_values(key_list[7], (D, D), (max(1, 4 * D // SPAN)) ** -0.5, 3.5),
        "encoder_biases": normal_values(key_list[8], (3, D), 0.5, 3.0, (), jnp.float32),
        "encoder_norms": normal_values(key_list[9], (2, 2, D), 0.2, 3.0, (), jnp.float32),
        "encoder_expand": normal_values(key_list[10], (D, FF), D ** -0.5, 0.21875),
        "encoder_expand_bias": normal_values(key_list[11], (FF,), 0.5, 3.0, (), jnp.float32),
        "encoder_shrink": normal_values(key_list[12], (FF, D), FF ** -0.5, 0.109375),
        "encoder_shrink_bias": normal_values(key_list[13], (D,), 0.5, 3.0, (), jnp.float32),
        "self_inward": normal_values(key_list[14], (3, D, D), D ** -0.5, 0.21875),
        "self_outward": normal_values(key_list[15], (D, D), (max(1, 16 * D // DEC_DEV)) ** -0.5, 0.625),
        "cross_inward": normal_values(key_list[16], (3, D, D), D ** -0.5, 0.21875),
        "cross_outward": normal_values(key_list[17], (D, D), (max(1, 4 * D // TOPK)) ** -0.5, 3.5),
        "decoder_biases": normal_values(key_list[18], (6, D), 0.5, 3.0, (), jnp.float32),
        "decoder_norms": normal_values(key_list[19], (3, 2, D), 0.2, 3.0, (), jnp.float32),
        "decoder_expand": normal_values(key_list[20], (D, FF), D ** -0.5, 0.21875),
        "decoder_expand_bias": normal_values(key_list[21], (FF,), 0.5, 3.0, (), jnp.float32),
        "decoder_shrink": normal_values(key_list[22], (FF, D), FF ** -0.5, 0.109375),
        "decoder_shrink_bias": normal_values(key_list[23], (D,), 0.5, 3.0, (), jnp.float32),
    }


highest = lax.Precision.HIGHEST
norm_eps = 1e-05
scale_scores = 0.125

@jax.custom_vjp
def low(v):
    return lax.optimization_barrier(v.astype(jnp.bfloat16)).astype(jnp.float32)

@jax.custom_vjp
def low_back(v):
    return v

def low_keep(v):
    return (low(v), None)

def low_pass(kept, grad):
    return (grad,)

def back_keep(v):
    return (v, None)

def back_low(kept, grad):
    return (low(grad),)
low.defvjp(low_keep, low_pass)
low_back.defvjp(back_keep, back_low)

def rounded(values):
    return low_back(low(values))

def product(left, right):
    return jnp.dot(left, right, precision=highest)

def norm_apply(values, pair):
    centre = lax.optimization_barrier(jnp.mean(values, -1, keepdims=True))
    centred = values - centre
    spread = lax.optimization_barrier(jnp.mean(centred * centred, -1, keepdims=True))
    return centred * lax.rsqrt(spread + norm_eps) * (1.0 + pair[0]) + pair[1]

def split_heads(values):
    return values.reshape(values.shape[0], HEADS, HEAD).transpose(1, 0, 2)

def attend(query_rows, key_rows, value_rows, allowed):
    scores = low_back(jnp.einsum('hqe,hke->hqk', split_heads(query_rows), split_heads(key_rows), precision=highest) * scale_scores)
    if allowed is not None:
        scores = jnp.where(allowed[None], scores, -1e+30)
    row_max = lax.optimization_barrier(jnp.max(scores, -1, keepdims=True))
    exponent = jnp.exp(scores - row_max)
    weights_low = low(exponent / lax.optimization_barrier(jnp.sum(exponent, -1, keepdims=True)))
    context = jnp.einsum('hqk,hke->hqe', weights_low, split_heads(value_rows), precision=highest)
    return context.transpose(1, 0, 2).reshape(query_rows.shape[0], HEADS * HEAD)

def attention(source_query, source_keys, inward, outward, biases, allowed):
    query_rows = rounded(product(source_query, inward[0]) + biases[0])
    key_rows = rounded(product(source_keys, inward[1]))
    value_rows = rounded(product(source_keys, inward[2]) + biases[1])
    context = rounded(attend(query_rows, key_rows, value_rows, allowed))
    return low_back(product(context, outward) + biases[2])

def feed_forward(normed, expand, expand_bias, shrink, shrink_bias):
    before = low_back(product(low(normed), expand) + expand_bias)
    hidden = low(jax.nn.gelu(before, approximate=False))
    return low_back(product(hidden, shrink) + shrink_bias)

def encoder_unit(inputs, weight_set):
    inward, outward, biases, norms, expand, expand_bias, shrink, shrink_bias = weight_set
    first_norm = norm_apply(inputs + attention(inputs, inputs, inward, outward, biases, None), norms[0])
    return norm_apply(first_norm + feed_forward(first_norm, expand, expand_bias, shrink, shrink_bias), norms[1])

def decoder_unit(inputs, pooled, lengths, chosen_slots, weight_set):
    self_inward, self_outward, cross_inward, cross_outward, biases, norms, expand, expand_bias, shrink, shrink_bias = weight_set
    positions = jnp.arange(inputs.shape[0], dtype=jnp.int32)
    seq_ends = jnp.cumsum(lengths, dtype=jnp.int32)
    segment_id = lax.optimization_barrier(jnp.sum((positions[:, None] >= seq_ends[None, :-1]).astype(jnp.int32), 1))
    self_allowed = (segment_id[:, None] == segment_id[None, :]) & (positions[None, :] <= positions[:, None])
    cross_allowed = jnp.zeros((inputs.shape[0], pooled.shape[0]), jnp.bool_).at[positions[:, None], chosen_slots].set(True)
    first_norm = norm_apply(inputs + attention(inputs, inputs, self_inward, self_outward, biases[0:3], self_allowed), norms[0])
    second_norm = norm_apply(first_norm + attention(low(first_norm), pooled, cross_inward, cross_outward, biases[3:6], cross_allowed), norms[1])
    return norm_apply(second_norm + feed_forward(second_norm, expand, expand_bias, shrink, shrink_bias), norms[2])

def reference(encoder_input, decoder_input, cotangent, pool_table, retrieved, decoder_lengths, encoder_inward, encoder_outward, encoder_biases, encoder_norms, encoder_expand, encoder_expand_bias, encoder_shrink, encoder_shrink_bias, self_inward, self_outward, cross_inward, cross_outward, decoder_biases, decoder_norms, decoder_expand, decoder_expand_bias, decoder_shrink, decoder_shrink_bias):
    weight_set = jax.tree.map(lambda array: array.astype(jnp.float32), (encoder_inward, encoder_outward, encoder_biases, encoder_norms, encoder_expand, encoder_expand_bias, encoder_shrink, encoder_shrink_bias, self_inward, self_outward, cross_inward, cross_outward, decoder_biases, decoder_norms, decoder_expand, decoder_expand_bias, decoder_shrink, decoder_shrink_bias))
    partner = (jnp.arange(MICRO, dtype=jnp.int32) + MICRO // 2) % MICRO
    owner_base = (jnp.arange(N_DP, dtype=jnp.int32) * SPAN)[None, :, None, None]
    local_index = (pool_table + owner_base).transpose(0, 2, 1, 3).reshape(MICRO, N_DP, POOL)
    pool_index = (local_index + (partner * ETOK)[:, None, None]).reshape(MICRO * N_DP, POOL)
    lengths_flat = decoder_lengths.reshape(MICRO * N_DP, NSEQ)
    slots_flat = retrieved.reshape(MICRO * N_DP, DEC_DEV, TOPK)

    def forward(encoder_rows, decoder_rows, weight_args):
        encoder_weights = weight_args[:8]
        decoder_weights = weight_args[8:]

        def encode_span(span_rows):
            return encoder_unit(span_rows, encoder_weights)

        def decode_group(group_args):
            return decoder_unit(group_args[0], group_args[1], group_args[2], group_args[3], decoder_weights)
        states = lax.map(jax.checkpoint(encode_span), encoder_rows.reshape(MICRO * N_DP, SPAN, D))
        sent_states = rounded(states).reshape(MICRO * ETOK, D)
        pooled = low_back(jnp.take(sent_states, pool_index, axis=0))
        outputs = lax.map(jax.checkpoint(decode_group), (decoder_rows.reshape(MICRO * N_DP, DEC_DEV, D), pooled, lengths_flat, slots_flat))
        return outputs.reshape(MICRO, DTOK, D)
    primal, pull = jax.vjp(forward, encoder_input.astype(jnp.float32), decoder_input.astype(jnp.float32), weight_set)
    encoder_grad, decoder_grad, weight_grads = pull(cotangent.astype(jnp.float32))
    return (primal.astype(jnp.bfloat16), encoder_grad, decoder_grad, weight_grads[0], weight_grads[1], weight_grads[2], weight_grads[3], weight_grads[4], weight_grads[5], weight_grads[6], weight_grads[7], weight_grads[8], weight_grads[9], weight_grads[10], weight_grads[11], weight_grads[12], weight_grads[13], weight_grads[14], weight_grads[15], weight_grads[16], weight_grads[17])
```

```python
import jax
import jax.numpy as jnp
from jax import lax
from jax.experimental import pallas as pl
from jax.experimental.pallas import tpu as pltpu
from jax.sharding import PartitionSpec as P

HEAD = 64
WIDTH = 768


norm_eps = 1e-05
scale_scores = 0.125
low_type = jnp.bfloat16
wide_type = jnp.float32


def shifted(value, axis, by):
    length = lax.axis_size(axis)
    return lax.ppermute(value, axis, [(i, (i + by) % length) for i in range(length)])


def norm_apply(values, pair):
    centre = jnp.mean(values, -1, keepdims=True)
    centred = values - centre
    spread = jnp.mean(centred * centred, -1, keepdims=True)
    return centred * lax.rsqrt(spread + norm_eps) * (1.0 + pair[0]) + pair[1]


def norm_back(values, pair, incoming):
    return jax.vjp(norm_apply, values, pair)[1](incoming)


def gelu_exact(values):
    return jax.nn.gelu(values, approximate=False)


def project(left, right):
    return jnp.dot(left, right, preferred_element_type=wide_type)


def project_back(left, incoming):
    return lax.dot_general(
        left, incoming, (((0,), (0,)), ((), ())), preferred_element_type=wide_type
    )


def back_through(incoming, right):
    return lax.dot_general(
        incoming, right, (((1,), (1,)), ((), ())), preferred_element_type=wide_type
    )


def column_sum(values):
    return jnp.sum(values, 0, dtype=wide_type)


def split_heads(values):
    return values.reshape(values.shape[0], -1, HEAD).transpose(1, 0, 2)


def join_heads(values):
    return values.transpose(1, 0, 2).reshape(values.shape[1], -1)


def block_scores(query_heads, key_heads, allowed, row_start, block_rows):
    scores = (
        jnp.einsum(
            "hqe,hke->hqk",
            query_heads[:, row_start : row_start + block_rows],
            key_heads,
            preferred_element_type=wide_type,
        )
        * scale_scores
    )
    if allowed is not None:
        scores = jnp.where(allowed[None, row_start : row_start + block_rows], scores, -1e30)
    return scores


def attend_forward(query_heads, key_heads, value_heads, allowed):
    length = query_heads.shape[1]
    block_rows = min(512, length)
    contexts = []
    totals = []
    for row_start in range(0, length, block_rows):
        scores = block_scores(query_heads, key_heads, allowed, row_start, block_rows)
        row_max = jnp.max(scores, -1, keepdims=True)
        exponent = jnp.exp(scores - row_max)
        row_total = jnp.sum(exponent, -1, keepdims=True)
        weights_low = (exponent / row_total).astype(low_type)
        contexts.append(
            jnp.einsum("hqk,hke->hqe", weights_low, value_heads, preferred_element_type=wide_type)
        )
        totals.append(row_max + jnp.log(row_total))
    return (join_heads(jnp.concatenate(contexts, 1)), jnp.concatenate(totals, 1))


def attend_backward(query_heads, key_heads, value_heads, allowed, totals, context_grad):
    length = query_heads.shape[1]
    block_rows = min(512, length)
    query_grads = []
    key_grad = jnp.zeros(key_heads.shape, wide_type)
    value_grad = jnp.zeros(value_heads.shape, wide_type)
    for row_start in range(0, length, block_rows):
        scores = block_scores(query_heads, key_heads, allowed, row_start, block_rows)
        weights_full = jnp.exp(scores - totals[:, row_start : row_start + block_rows])
        grad_block = context_grad[:, row_start : row_start + block_rows]
        weights_grad = jnp.einsum(
            "hqe,hke->hqk", grad_block, value_heads, preferred_element_type=wide_type
        )
        inner = jnp.sum(weights_full * weights_grad, -1, keepdims=True)
        scores_grad = (weights_full * (weights_grad - inner)).astype(low_type)
        query_grads.append(
            jnp.einsum("hqk,hke->hqe", scores_grad, key_heads, preferred_element_type=wide_type)
            * scale_scores
        )
        key_grad = (
            key_grad
            + jnp.einsum(
                "hqk,hqe->hke",
                scores_grad,
                query_heads[:, row_start : row_start + block_rows],
                preferred_element_type=wide_type,
            )
            * scale_scores
        )
        value_grad = value_grad + jnp.einsum(
            "hqk,hqe->hke",
            weights_full.astype(low_type),
            grad_block,
            preferred_element_type=wide_type,
        )
    return (
        join_heads(jnp.concatenate(query_grads, 1)).astype(low_type),
        join_heads(key_grad).astype(low_type),
        join_heads(value_grad).astype(low_type),
    )


def attention_forward(source_query, source_keys, inward, outward, biases, allowed):
    query_rows = (project(source_query, inward[0]) + biases[0]).astype(low_type)
    key_rows = project(source_keys, inward[1]).astype(low_type)
    value_rows = (project(source_keys, inward[2]) + biases[1]).astype(low_type)
    context, totals = attend_forward(
        split_heads(query_rows), split_heads(key_rows), split_heads(value_rows), allowed
    )
    context = context.astype(low_type)
    return (
        project(context, outward) + biases[2],
        (query_rows, key_rows, value_rows, totals, context),
    )


def attention_backward(source_query, source_keys, inward, outward, allowed, saved_state, incoming):
    query_rows, key_rows, value_rows, totals, context = saved_state
    incoming_low = incoming.astype(low_type)
    context_grad = back_through(incoming_low, outward).astype(low_type)
    query_grad, key_grad, value_grad = attend_backward(
        split_heads(query_rows),
        split_heads(key_rows),
        split_heads(value_rows),
        allowed,
        totals,
        split_heads(context_grad),
    )
    inward_grad = jnp.stack(
        [
            project_back(source_query, query_grad),
            project_back(source_keys, key_grad),
            project_back(source_keys, value_grad),
        ]
    )
    bias_grad = jnp.stack(
        [column_sum(query_grad), column_sum(value_grad), column_sum(incoming_low)]
    )
    source_query_grad = back_through(query_grad, inward[0])
    source_keys_grad = back_through(key_grad, inward[1]) + back_through(value_grad, inward[2])
    return (
        source_query_grad,
        source_keys_grad,
        inward_grad,
        project_back(context, incoming_low),
        bias_grad,
    )


def feed_forward(normed, expand, expand_bias, shrink, shrink_bias):
    normed_low = normed.astype(low_type)
    before = project(normed_low, expand) + expand_bias
    hidden = gelu_exact(before).astype(low_type)
    return (project(hidden, shrink) + shrink_bias, (normed_low, before, hidden))


def feed_forward_back(expand, shrink, saved_state, incoming):
    normed_low, before, hidden = saved_state
    incoming_low = incoming.astype(low_type)
    hidden_grad = back_through(incoming_low, shrink)
    before_grad = jax.vjp(gelu_exact, before)[1](hidden_grad)[0].astype(low_type)
    return (
        back_through(before_grad, expand),
        project_back(normed_low, before_grad),
        column_sum(before_grad),
        project_back(hidden, incoming_low),
        column_sum(incoming_low),
    )


def encoder_pass(inputs, weight_set):
    inward, outward, biases, norms, expand, expand_bias, shrink, shrink_bias = weight_set
    branch, attention_saved = attention_forward(inputs, inputs, inward, outward, biases, None)
    mixed_rows = inputs.astype(wide_type) + branch
    first_norm = norm_apply(mixed_rows, norms[0])
    expand_out, feed_saved = feed_forward(first_norm, expand, expand_bias, shrink, shrink_bias)
    summed = first_norm + expand_out
    return (norm_apply(summed, norms[1]), (attention_saved, mixed_rows, feed_saved, summed))


def encoder_back(inputs, weight_set, saved_state, incoming):
    inward, outward, biases, norms, expand, expand_bias, shrink, shrink_bias = weight_set
    attention_saved, mixed_rows, feed_saved, summed = saved_state
    summed_grad, norm_two_grad = norm_back(summed, norms[1], incoming)
    first_grad, expand_grad, expand_bias_grad, shrink_grad, shrink_bias_grad = feed_forward_back(
        expand, shrink, feed_saved, summed_grad
    )
    mixed_grad, norm_one_grad = norm_back(mixed_rows, norms[0], first_grad + summed_grad)
    query_side, key_side, inward_grad, outward_grad, bias_grad = attention_backward(
        inputs, inputs, inward, outward, None, attention_saved, mixed_grad
    )
    return (
        mixed_grad + query_side + key_side,
        inward_grad,
        outward_grad,
        bias_grad,
        jnp.stack([norm_one_grad, norm_two_grad]),
        expand_grad,
        expand_bias_grad,
        shrink_grad,
        shrink_bias_grad,
    )


def decoder_pass(inputs, pooled, weight_set, self_allowed, cross_allowed):
    (
        self_inward,
        self_outward,
        cross_inward,
        cross_outward,
        biases,
        norms,
        expand,
        expand_bias,
        shrink,
        shrink_bias,
    ) = weight_set
    branch, self_saved = attention_forward(
        inputs, inputs, self_inward, self_outward, biases[0:3], self_allowed
    )
    mixed_rows = inputs.astype(wide_type) + branch
    first_norm = norm_apply(mixed_rows, norms[0])
    first_low = first_norm.astype(low_type)
    cross_out, cross_saved = attention_forward(
        first_low, pooled, cross_inward, cross_outward, biases[3:6], cross_allowed
    )
    joined = first_norm + cross_out
    second = norm_apply(joined, norms[1])
    expand_out, feed_saved = feed_forward(second, expand, expand_bias, shrink, shrink_bias)
    summed = second + expand_out
    return (
        norm_apply(summed, norms[2]),
        (self_saved, mixed_rows, first_low, cross_saved, joined, feed_saved, summed),
    )


def decoder_back(inputs, pooled, weight_set, self_allowed, cross_allowed, saved_state, incoming):
    (
        self_inward,
        self_outward,
        cross_inward,
        cross_outward,
        biases,
        norms,
        expand,
        expand_bias,
        shrink,
        shrink_bias,
    ) = weight_set
    self_saved, mixed_rows, first_low, cross_saved, joined, feed_saved, summed = saved_state
    summed_grad, norm_three_grad = norm_back(summed, norms[2], incoming)
    second_grad, expand_grad, expand_bias_grad, shrink_grad, shrink_bias_grad = feed_forward_back(
        expand, shrink, feed_saved, summed_grad
    )
    joined_grad, norm_two_grad = norm_back(joined, norms[1], second_grad + summed_grad)
    cross_query, pooled_grad, cross_inward_grad, cross_outward_grad, cross_bias_grad = (
        attention_backward(
            first_low, pooled, cross_inward, cross_outward, cross_allowed, cross_saved, joined_grad
        )
    )
    mixed_grad, norm_one_grad = norm_back(mixed_rows, norms[0], joined_grad + cross_query)
    query_side, key_side, self_inward_grad, self_outward_grad, self_bias_grad = attention_backward(
        inputs, inputs, self_inward, self_outward, self_allowed, self_saved, mixed_grad
    )
    return (
        mixed_grad + query_side + key_side,
        pooled_grad,
        self_inward_grad,
        self_outward_grad,
        cross_inward_grad,
        cross_outward_grad,
        jnp.concatenate([self_bias_grad, cross_bias_grad], 0),
        jnp.stack([norm_one_grad, norm_two_grad, norm_three_grad]),
        expand_grad,
        expand_bias_grad,
        shrink_grad,
        shrink_bias_grad,
    )


def mask_kernel(slots_ref, mask_ref):
    count, width = slots_ref.shape
    words = mask_ref.shape[0] // 32
    block = 16
    row = lax.broadcasted_iota(jnp.int32, (32, width), 0)
    for start in range(0, words, block):

        def step(i, totals):
            piece = slots_ref[pl.ds(pl.multiple_of(i * 8, 8), 8), :]
            word = lax.shift_right_logical(piece, 5)
            bit = jnp.left_shift(jnp.int32(1), piece & 31)
            return tuple(
                total | jnp.where(word == start + w, bit, 0) for w, total in enumerate(totals)
            )

        zero = jnp.zeros((8, width), jnp.int32)
        totals = lax.fori_loop(0, count // 8, step, (zero,) * block)
        for w, total in enumerate(totals):
            joined = total[0:1]
            for k in range(1, 8):
                joined = joined | total[k : k + 1]
            bits = lax.shift_right_logical(jnp.broadcast_to(joined, (32, width)), row) & 1
            at = (start + w) * 32
            mask_ref[at : at + 32, :] = bits.astype(jnp.float32).astype(mask_ref.dtype)


def slot_mask(slots, pool):
    return pl.pallas_call(
        mask_kernel,
        out_shape=jax.ShapeDtypeStruct((pool, slots.shape[0]), jnp.bfloat16),
        in_specs=[pl.BlockSpec(memory_space=pltpu.VMEM)],
        out_specs=pl.BlockSpec(memory_space=pltpu.VMEM),
        cost_estimate=pl.CostEstimate(flops=10**8, bytes_accessed=10**6, transcendentals=0),
    )(slots.T)


def rows_of(matrix, parts):
    lead = matrix.shape[:-2]
    rows, columns = matrix.shape[-2:]
    cut = matrix.reshape(-1, parts, rows // parts, columns // WIDTH, WIDTH)
    return cut.transpose(1, 0, 3, 2, 4).reshape(parts, -1, WIDTH)


def rows_back(shard, lead, rows, columns):
    cut = shard.reshape(-1, columns // WIDTH, rows, WIDTH)
    return cut.transpose(0, 2, 1, 3).reshape(lead + (rows, columns))


def sum_matrices(matrices):
    parts = lax.axis_size("dp")
    packed = jnp.concatenate([rows_of(m, parts).astype(low_type) for m in matrices], 1)
    shard = lax.psum_scatter(packed, "dp", scatter_dimension=0, tiled=True)[0]
    total = lax.psum(shard, "section").astype(wide_type)
    outs = []
    at = 0
    for m in matrices:
        size = m.size // parts // WIDTH
        outs.append(
            rows_back(total[at : at + size], m.shape[:-2], m.shape[-2] // parts, m.shape[-1])
        )
        at += size
    return outs


def sum_vectors(vectors):
    parts = lax.axis_size("dp")
    flat = jnp.concatenate([v.reshape(-1) for v in vectors])
    total = lax.psum(flat, ("dp", "section"))
    mine = lax.axis_index("dp")
    outs = []
    at = 0
    for v in vectors:
        whole = total[at : at + v.size].reshape(v.shape)
        at += v.size
        size = v.shape[-1] // parts
        outs.append(lax.dynamic_slice_in_dim(whole, mine * size, size, v.ndim - 1))
    return outs


def on_device(
    encoder_input,
    decoder_input,
    cotangent,
    pool_table,
    retrieved,
    decoder_lengths,
    encoder_inward,
    encoder_outward,
    encoder_biases,
    encoder_norms,
    encoder_expand,
    encoder_expand_bias,
    encoder_shrink,
    encoder_shrink_bias,
    self_inward,
    self_outward,
    cross_inward,
    cross_outward,
    decoder_biases,
    decoder_norms,
    decoder_expand,
    decoder_expand_bias,
    decoder_shrink,
    decoder_shrink_bias,
):
    encoder_weights = (
        encoder_inward,
        encoder_outward,
        encoder_biases,
        encoder_norms,
        encoder_expand,
        encoder_expand_bias,
        encoder_shrink,
        encoder_shrink_bias,
    )
    decoder_weights = (
        self_inward,
        self_outward,
        cross_inward,
        cross_outward,
        decoder_biases,
        decoder_norms,
        decoder_expand,
        decoder_expand_bias,
        decoder_shrink,
        decoder_shrink_bias,
    )
    encoder_rows = encoder_input[0]
    half_way = lax.axis_size("section") // 2
    queries, width = decoder_input.shape[1:]
    topk = retrieved.shape[2]
    rows_low = shifted(jnp.concatenate([decoder_input[0], cotangent[0]], 0), "section", -half_way)
    decoder_rows, cotangent_rows = rows_low[:queries], rows_low[queries:]
    lengths_row = jnp.pad(decoder_lengths[0], ((0, 0), (0, topk - decoder_lengths.shape[2])))
    integers = shifted(
        jnp.concatenate([retrieved[0], pool_table[0, 0].reshape(-1, topk), lengths_row], 0),
        "section",
        -half_way,
    )
    retrieved_rows = integers[:queries]
    owner_table = integers[queries:-1].reshape(pool_table.shape[2:])
    lengths = integers[-1, : decoder_lengths.shape[2]]
    encoder_final, encoder_saved = encoder_pass(encoder_rows, encoder_weights)
    states = encoder_final.astype(low_type)
    picked_rows = jnp.take(states, owner_table, axis=0)
    fetched = lax.all_to_all(picked_rows, "dp", split_axis=0, concat_axis=0, tiled=True)
    owners, slot_count, feature_count = fetched.shape
    pooled = fetched.reshape(owners * slot_count, feature_count)
    positions = jnp.arange(queries, dtype=jnp.int32)
    seq_ends = jnp.cumsum(lengths, dtype=jnp.int32)
    segment_id = jnp.sum((positions[:, None] >= seq_ends[None, :-1]).astype(jnp.int32), 1)
    self_allowed = (segment_id[:, None] == segment_id[None, :]) & (
        positions[None, :] <= positions[:, None]
    )
    cross_allowed = slot_mask(retrieved_rows, pooled.shape[0]).T > 0
    decoder_final, decoder_saved = decoder_pass(
        decoder_rows, pooled, decoder_weights, self_allowed, cross_allowed
    )
    (
        decoder_grad,
        pooled_grad,
        delta_self_inward,
        delta_self_outward,
        delta_cross_inward,
        delta_cross_outward,
        delta_decoder_biases,
        delta_decoder_norms,
        delta_decoder_expand,
        delta_decoder_expand_bias,
        delta_decoder_shrink,
        delta_decoder_shrink_bias,
    ) = decoder_back(
        decoder_rows,
        pooled,
        decoder_weights,
        self_allowed,
        cross_allowed,
        decoder_saved,
        cotangent_rows.astype(wide_type),
    )
    returned = lax.all_to_all(
        pooled_grad.astype(low_type).reshape(owners, slot_count, feature_count),
        "dp",
        split_axis=0,
        concat_axis=0,
        tiled=True,
    )
    spread = (
        jnp.arange(states.shape[0], dtype=jnp.int32)[:, None] == owner_table.reshape(1, -1)
    ).astype(low_type)
    state_grad = jnp.dot(
        spread, returned.reshape(-1, feature_count), preferred_element_type=wide_type
    )
    encoder_incoming = state_grad.astype(low_type).astype(wide_type)
    (
        encoder_grad,
        delta_encoder_inward,
        delta_encoder_outward,
        delta_encoder_biases,
        delta_encoder_norms,
        delta_encoder_expand,
        delta_encoder_expand_bias,
        delta_encoder_shrink,
        delta_encoder_shrink_bias,
    ) = encoder_back(encoder_rows, encoder_weights, encoder_saved, encoder_incoming)
    decoder_matrices = sum_matrices(
        [
            delta_self_inward,
            delta_self_outward,
            delta_cross_inward,
            delta_cross_outward,
            delta_decoder_expand,
            delta_decoder_shrink,
        ]
    )
    feed_matrices = sum_matrices([delta_encoder_expand, delta_encoder_shrink])
    attention_matrices = sum_matrices([delta_encoder_inward, delta_encoder_outward])
    vectors = sum_vectors(
        [
            delta_encoder_biases,
            delta_encoder_norms,
            delta_encoder_expand_bias,
            delta_encoder_shrink_bias,
            delta_decoder_biases,
            delta_decoder_norms,
            delta_decoder_expand_bias,
            delta_decoder_shrink_bias,
        ]
    )
    decoder_out = shifted(decoder_final.astype(low_type), "section", half_way)
    decoder_grad_out = shifted(decoder_grad, "section", half_way)
    return (
        decoder_out[None],
        encoder_grad[None],
        decoder_grad_out[None],
        attention_matrices[0],
        attention_matrices[1],
        vectors[0],
        vectors[1],
        feed_matrices[0],
        vectors[2],
        feed_matrices[1],
        vectors[3],
        decoder_matrices[0],
        decoder_matrices[1],
        decoder_matrices[2],
        decoder_matrices[3],
        vectors[4],
        vectors[5],
        decoder_matrices[4],
        vectors[6],
        decoder_matrices[5],
        vectors[7],
    )


def solution(mesh):
    in_specs = (
        P("section", "dp", None),
        P("section", "dp", None),
        P("section", "dp", None),
        P("section", "dp", None, None),
        P("section", "dp", None),
        P("section", "dp", None),
        P(),
        P(),
        P(),
        P(),
        P(),
        P(),
        P(),
        P(),
        P(),
        P(),
        P(),
        P(),
        P(),
        P(),
        P(),
        P(),
        P(),
        P(),
    )
    out_specs = (
        P("section", "dp", None),
        P("section", "dp", None),
        P("section", "dp", None),
        P(None, "dp", None),
        P("dp", None),
        P(None, "dp"),
        P(None, None, "dp"),
        P("dp", None),
        P("dp"),
        P("dp", None),
        P("dp"),
        P(None, "dp", None),
        P("dp", None),
        P(None, "dp", None),
        P("dp", None),
        P(None, "dp"),
        P(None, None, "dp"),
        P("dp", None),
        P("dp"),
        P("dp", None),
        P("dp"),
    )
    return jax.shard_map(
        on_device, mesh=mesh, in_specs=in_specs, out_specs=out_specs, check_vma=False
    )
```

```python
import functools

import jax
import jax.numpy as jnp
from jax import lax
from jax.experimental import pallas as pl
from jax.experimental.pallas import tpu as pltpu
from jax.sharding import PartitionSpec as P

HEAD = 64
WIDTH = 768


norm_eps = 1e-05
scale_scores = 0.125
low_type = jnp.bfloat16
wide_type = jnp.float32

NN = (((1,), (0,)), ((), ()))
NT = (((1,), (1,)), ((), ()))
TN = (((0,), (0,)), ((), ()))
GROUP = 256
VMEM = pltpu.VMEM


def dot(left, right, dims=NN):
    return lax.dot_general(left, right, dims, preferred_element_type=wide_type)


def low(value):
    return value.astype(low_type)


def wide(value):
    return value.astype(wide_type)


def head_lanes(dtype):
    lane = lax.broadcasted_iota(jnp.int32, (1, GROUP), 1) // HEAD
    return [(lane == h).astype(wide_type).astype(dtype) for h in range(GROUP // HEAD)]


def centred_of(values):
    centred = values - jnp.mean(values, -1, keepdims=True)
    spread = jnp.mean(centred * centred, -1, keepdims=True)
    return centred, lax.rsqrt(spread + norm_eps)


def norm_rows(values, gain, offset):
    centred, scale = centred_of(values)
    return centred * scale * (1.0 + gain) + offset


def norm_rows_back(values, gain, incoming):
    centred, scale = centred_of(values)
    unit = centred * scale
    inner = incoming * (1.0 + gain)
    mean_inner = jnp.mean(inner, -1, keepdims=True)
    mean_along = jnp.mean(inner * unit, -1, keepdims=True)
    return (
        scale * (inner - mean_inner - unit * mean_along),
        jnp.sum(incoming * unit, 0, keepdims=True),
        jnp.sum(incoming, 0, keepdims=True),
    )


def gelu_parts(u):
    size = jnp.abs(u) * 0.7071067811865476
    t = 1.0 / (1.0 + 0.3275911 * size)
    bell = jnp.exp(-0.5 * u * u)
    series = t * (
        0.254829592
        + t * (-0.284496736 + t * (1.421413741 + t * (-1.453152027 + t * 1.061405429)))
    )
    tail = 0.5 * series * bell
    share = jnp.where(u < 0.0, tail, 1.0 - tail)
    return u * share, share + u * (bell * 0.3989422804014327)


def params(limit=60, **rest):
    return pltpu.CompilerParams(vmem_limit_bytes=limit * 2**20, **rest)


def cost(flops, size, exps=0):
    return pl.CostEstimate(flops=int(flops), bytes_accessed=int(size), transcendentals=int(exps))


def full(*shape):
    return pl.BlockSpec(shape, lambda *_: (0,) * len(shape))


def like(shape, dtype):
    return jax.ShapeDtypeStruct(shape, dtype)


def paired():
    return lax.axis_size("dp") == 8


def grad_shapes(parts, rows, columns):
    if paired():
        return [like((4, parts * rows // 8, columns), low_type)] * 2
    return [like((parts, rows, columns), low_type)]


def grad_specs(parts, rows, columns, index=None):
    if paired():
        block, count = (4, parts * rows // 8, columns), 2
    else:
        block, count = (parts, rows, columns), 1
    return [pl.BlockSpec(block, index or (lambda *_: (0, 0, 0)))] * count


def emit(outs, part, hold):
    if len(outs) == 1:
        outs[0][part] = low(hold[...])
        return
    keep, send = outs
    me = lax.axis_index("dp")
    rows = hold.shape[0] // 8
    to = pl.ds(pl.multiple_of(part * rows, rows), rows)
    for at in range(4):
        mine = pl.multiple_of((me ^ (2 * at)) * rows, rows)
        other = pl.multiple_of((me ^ (2 * at + 1)) * rows, rows)
        keep[at, to, :] = low(hold[pl.ds(mine, rows), :])
        send[at, to, :] = low(hold[pl.ds(other, rows), :])


def emit_tall(outs, block, hold):
    if len(outs) == 1:
        size = hold.shape[0]
        outs[0][0, pl.ds(pl.multiple_of(block * size, size), size), :] = low(hold[...])
        return
    keep, send = outs
    me = lax.axis_index("dp")
    rows = hold.shape[0] // 2
    at = block ^ lax.shift_right_logical(me, 1)
    core = me & 1
    keep[at, 0:rows, :] = low(hold[pl.ds(pl.multiple_of(core * rows, rows), rows), :])
    send[at, 0:rows, :] = low(hold[pl.ds(pl.multiple_of((1 - core) * rows, rows), rows), :])


def thirds(items):
    third = len(items) // 3
    return items[:third], items[third : 2 * third], items[2 * third :]


def encoder_attend_kernel(
    x_ref, w_ref, wo_ref, bg_ref, b_ref, qkv_ref, c_ref, stat_ref, mixed_ref, stats
):
    group = pl.program_id(0)
    tokens = x_ref.shape[0]
    block = 256
    x = x_ref[...]
    qkv_ref[0] = low(dot(x, w_ref[0]) + bg_ref[0:1])
    qkv_ref[1] = low(dot(x, w_ref[1]))
    qkv_ref[2] = low(dot(x, w_ref[2]) + bg_ref[1:2])
    lanes_low, lanes = head_lanes(low_type), head_lanes(wide_type)
    lane = lax.broadcasted_iota(jnp.int32, (1, 128), 1)

    @pl.when(group == 0)
    def _():
        mixed_ref[...] = wide(x) + b_ref[2:3]

    def rows_step(i, carry):
        rows = pl.ds(pl.multiple_of(i * block, block), block)
        q = qkv_ref[0, rows, :] * jnp.asarray(scale_scores, low_type)
        context = jnp.zeros((block, GROUP), wide_type)
        stat = jnp.zeros((block, 128), wide_type)
        for h in range(GROUP // HEAD):
            scores = dot(q * lanes_low[h], qkv_ref[1], NT)
            top = jnp.max(scores, -1, keepdims=True)
            weights = jnp.exp(scores - top)
            total = jnp.sum(weights, -1, keepdims=True)
            context += dot(low(weights), qkv_ref[2]) * (lanes[h] * (1.0 / total))
            stat = jnp.where(lane == h, top + jnp.log(total), stat)
        c_ref[rows, :] = context
        stats[rows, :] = stat
        mixed_ref[rows, :] += dot(low(context), wo_ref[...])
        return carry

    lax.fori_loop(0, tokens // block, rows_step, 0)
    stat_ref[0] = stats[...].T[0:8]


def encoder_attend(x, inward, outward, biases):
    tokens, width = x.shape
    groups = width // GROUP
    return pl.pallas_call(
        encoder_attend_kernel,
        grid=(groups,),
        in_specs=[
            full(tokens, width),
            pl.BlockSpec((3, width, GROUP), lambda g: (0, 0, g)),
            pl.BlockSpec((GROUP, width), lambda g: (g, 0)),
            pl.BlockSpec((3, GROUP), lambda g: (0, g)),
            full(3, width),
        ],
        out_specs=[
            pl.BlockSpec((3, tokens, GROUP), lambda g: (0, 0, g)),
            pl.BlockSpec((tokens, GROUP), lambda g: (0, g)),
            pl.BlockSpec((1, 8, tokens), lambda g: (g, 0, 0)),
            full(tokens, width),
        ],
        out_shape=[
            like((3, tokens, width), low_type),
            like((tokens, width), wide_type),
            like((groups, 8, tokens), wide_type),
            like((tokens, width), wide_type),
        ],
        scratch_shapes=[VMEM((tokens, 128), wide_type)],
        compiler_params=params(),
        cost_estimate=cost(3e10, 2e7, 1.3e7),
        name="encoder_attend",
    )(x, inward, outward, biases, biases)


def encoder_feed_kernel(
    mixed_ref, n_ref, e_ref, eb_ref, s_ref, sb_ref, h_ref, d_ref, sum_ref, out_ref, a_low
):
    step = pl.program_id(0)
    tokens = mixed_ref.shape[0]
    block = 256

    @pl.when(step == 0)
    def _():
        first = norm_rows(mixed_ref[...], n_ref[0, 0:1], n_ref[0, 1:2])
        a_low[...] = low(first)
        sum_ref[...] = first + sb_ref[...]

    for i in range(tokens // block):
        rows = slice(i * block, (i + 1) * block)
        hidden, slope = gelu_parts(dot(a_low[rows, :], e_ref[...]) + eb_ref[...])
        h_ref[rows, :] = low(hidden)
        d_ref[rows, :] = low(slope)
        sum_ref[rows, :] += dot(low(hidden), s_ref[...])

    @pl.when(step == pl.num_programs(0) - 1)
    def _():
        out_ref[...] = low(norm_rows(sum_ref[...], n_ref[1, 0:1], n_ref[1, 1:2]))


def encoder_feed(mixed, norms, expand, expand_bias, shrink, shrink_bias):
    tokens, width = mixed.shape
    hidden = expand.shape[1]
    cut = hidden // 4
    return pl.pallas_call(
        encoder_feed_kernel,
        grid=(4,),
        in_specs=[
            full(tokens, width),
            full(2, 2, width),
            pl.BlockSpec((width, cut), lambda i: (0, i)),
            pl.BlockSpec((1, cut), lambda i: (0, i)),
            pl.BlockSpec((cut, width), lambda i: (i, 0)),
            full(1, width),
        ],
        out_specs=[
            pl.BlockSpec((tokens, cut), lambda i: (0, i)),
            pl.BlockSpec((tokens, cut), lambda i: (0, i)),
            full(tokens, width),
            full(tokens, width),
        ],
        out_shape=[
            like((tokens, hidden), low_type),
            like((tokens, hidden), low_type),
            like((tokens, width), wide_type),
            like((tokens, width), low_type),
        ],
        scratch_shapes=[VMEM((tokens, width), low_type)],
        compiler_params=params(),
        cost_estimate=cost(2e10, 3e7, 3e6),
        name="encoder_feed",
    )(mixed, norms, expand, expand_bias[None], shrink, shrink_bias[None])


def encoder_feed_back_kernel(
    g_ref, sum_ref, mixed_ref, h_ref, d_ref, c_ref, n_ref, e_ref, s_ref, *rest
):
    dmix_ref, vec_ref, eb_ref = rest[:3]
    back_low, a_turned, between, hold = rest[-4:]
    wide_outs, tall_outs, out_outs = thirds(rest[3:-4])
    step = pl.program_id(0)
    tokens = sum_ref.shape[0]
    block = 256

    @pl.when(step == 0)
    def _():
        grad, gain, offset = norm_rows_back(sum_ref[...], n_ref[1, 0:1], wide(g_ref[...]))
        dmix_ref[...] = grad
        back_low[...] = low(grad)
        vec_ref[...] = jnp.zeros(vec_ref.shape, wide_type)
        vec_ref[0:1] = gain
        vec_ref[1:2] = offset
        vec_ref[2:3] = jnp.sum(wide(back_low[...]), 0, keepdims=True)
        a_turned[...] = low(norm_rows(mixed_ref[...], n_ref[0, 0:1], n_ref[0, 1:2])).T

    column = jnp.zeros(eb_ref.shape, wide_type)
    for i in range(tokens // block):
        rows = slice(i * block, (i + 1) * block)
        before = low(dot(back_low[rows, :], s_ref[...], NT) * wide(d_ref[rows, :]))
        between[rows, :] = before
        column += jnp.sum(wide(before), 0, keepdims=True)
        dmix_ref[rows, :] += dot(before, e_ref[...], NT)
    eb_ref[...] = column
    hold[...] = dot(a_turned[...], between[...])
    emit(wide_outs, step, hold)
    hold[...] = dot(h_ref[...], back_low[...], TN)
    emit_tall(tall_outs, step, hold)

    @pl.when(step == pl.num_programs(0) - 1)
    def _():
        grad, gain, offset = norm_rows_back(mixed_ref[...], n_ref[0, 0:1], dmix_ref[...])
        dmix_ref[...] = grad
        back_low[...] = low(grad)
        vec_ref[3:4] = gain
        vec_ref[4:5] = offset
        vec_ref[5:6] = jnp.sum(wide(back_low[...]), 0, keepdims=True)
        hold[...] = dot(low(c_ref[...]), back_low[...], TN)
        emit(out_outs, 0, hold)


def encoder_feed_back(grad, summed, mixed, hidden, slope, context, norms, expand, shrink):
    tokens, width = mixed.shape
    total = expand.shape[1]
    cut = total // 4
    outs = pl.pallas_call(
        encoder_feed_back_kernel,
        grid=(4,),
        in_specs=[
            full(tokens, width),
            full(tokens, width),
            full(tokens, width),
            pl.BlockSpec((tokens, cut), lambda i: (0, i)),
            pl.BlockSpec((tokens, cut), lambda i: (0, i)),
            full(tokens, width),
            full(2, 2, width),
            pl.BlockSpec((width, cut), lambda i: (0, i)),
            pl.BlockSpec((cut, width), lambda i: (i, 0)),
        ],
        out_specs=[
            full(tokens, width),
            full(8, width),
            pl.BlockSpec((1, cut), lambda i: (0, i)),
            *grad_specs(4, width, width),
            *grad_specs(1, total, width),
            *grad_specs(1, width, width),
        ],
        out_shape=[
            like((tokens, width), wide_type),
            like((8, width), wide_type),
            like((1, total), wide_type),
            *grad_shapes(4, width, width),
            *grad_shapes(1, total, width),
            *grad_shapes(1, width, width),
        ],
        scratch_shapes=[
            VMEM((tokens, width), low_type),
            VMEM((width, tokens), low_type),
            VMEM((tokens, cut), low_type),
            VMEM((width, width), wide_type),
        ],
        compiler_params=params(),
        cost_estimate=cost(4e10, 5e7),
        name="encoder_feed_back",
    )(grad, summed, mixed, hidden, slope, context, norms, expand, shrink)
    return outs[:3], thirds(outs[3:])


def encoder_attend_back_kernel(
    dmix_ref, x_ref, qkv_ref, c_ref, stat_ref, w_ref, wo_ref, *rest
):
    dx_ref, vec_ref = rest[:2]
    outs, (dmix_low, x_turned, dc, weights, scores_back, dk, dv, dq_turned, hold) = (
        rest[2:-9],
        rest[-9:],
    )
    group = pl.program_id(0)
    tokens = x_ref.shape[0]
    block = 256
    heads = GROUP // HEAD

    @pl.when(group == 0)
    def _():
        dx_ref[...] = dmix_ref[...]
        dmix_low[...] = low(dmix_ref[...])
        x_turned[...] = x_ref[...].T

    dc[...] = low(dot(dmix_low[...], wo_ref[...], NT))
    lanes_low = head_lanes(low_type)
    eighth = jnp.asarray(scale_scores, low_type)
    pick = (
        lax.broadcasted_iota(jnp.int32, (8, GROUP), 1) // HEAD
        == lax.broadcasted_iota(jnp.int32, (8, GROUP), 0)
    ).astype(wide_type)
    pick = low(pick)
    product = wide(dc[...]) * c_ref[...]
    product_high = low(product)
    product_rest = low(product - wide(product_high))
    inner = dot(pick, product_high, NT) + dot(pick, product_rest, NT)
    k_turned = qkv_ref[1].T
    dk[...] = jnp.zeros(dk.shape, wide_type)
    dv[...] = jnp.zeros(dv.shape, wide_type)
    for i in range(tokens // block):
        rows = slice(i * block, (i + 1) * block)
        q = qkv_ref[0, rows, :] * eighth
        q_heads = jnp.concatenate([q * lanes_low[h] for h in range(heads)], 0)
        dc_heads = jnp.concatenate([dc[rows, :] * lanes_low[h] for h in range(heads)], 0)
        for h in range(heads):
            part = slice(h * block, (h + 1) * block)
            scores = dot(qkv_ref[1], q_heads[part], NT)
            weight = jnp.exp(scores - stat_ref[0, h : h + 1, rows])
            weight_back = dot(qkv_ref[2], dc_heads[part], NT)
            weights[:, part] = low(weight)
            back = low(weight * (weight_back - inner[h : h + 1, rows]))
            scores_back[:, part] = back
            dq_turned[h * HEAD : (h + 1) * HEAD, rows] = dot(
                k_turned[h * HEAD : (h + 1) * HEAD], back
            )
        dv[...] += dot(weights[...], dc_heads)
        dk[...] += dot(scores_back[...], q_heads)
    dq = low(dq_turned[...].T * scale_scores)
    dk_low, dv_low = low(dk[...]), low(dv[...])
    vec_ref[...] = jnp.zeros(vec_ref.shape, wide_type)
    vec_ref[0:1] = jnp.sum(wide(dq), 0, keepdims=True)
    vec_ref[1:2] = jnp.sum(wide(dv_low), 0, keepdims=True)
    dx_ref[...] += (
        dot(dq, w_ref[0], NT) + dot(dk_low, w_ref[1], NT) + dot(dv_low, w_ref[2], NT)
    )
    for part, grad in enumerate((dq, dk_low, dv_low)):
        hold[...] = dot(x_turned[...], grad)
        emit(outs, part, hold)


def encoder_attend_back(dmix, x, qkv, context, stats, inward, outward):
    tokens, width = x.shape
    groups = width // GROUP
    specs = grad_specs(3, width, GROUP, lambda g: (0, 0, g))
    outs = pl.pallas_call(
        encoder_attend_back_kernel,
        grid=(groups,),
        in_specs=[
            full(tokens, width),
            full(tokens, width),
            pl.BlockSpec((3, tokens, GROUP), lambda g: (0, 0, g)),
            pl.BlockSpec((tokens, GROUP), lambda g: (0, g)),
            pl.BlockSpec((1, 8, tokens), lambda g: (g, 0, 0)),
            pl.BlockSpec((3, width, GROUP), lambda g: (0, 0, g)),
            pl.BlockSpec((GROUP, width), lambda g: (g, 0)),
        ],
        out_specs=[
            full(tokens, width),
            pl.BlockSpec((8, GROUP), lambda g: (0, g)),
            *specs,
        ],
        out_shape=[
            like((tokens, width), wide_type),
            like((8, width), wide_type),
            *grad_shapes(3, width, width),
        ],
        scratch_shapes=[
            VMEM((tokens, width), low_type),
            VMEM((width, tokens), low_type),
            VMEM((tokens, GROUP), low_type),
            VMEM((tokens, 4 * 256), low_type),
            VMEM((tokens, 4 * 256), low_type),
            VMEM((tokens, GROUP), wide_type),
            VMEM((tokens, GROUP), wide_type),
            VMEM((GROUP, tokens), wide_type),
            VMEM((width, GROUP), wide_type),
        ],
        compiler_params=params(),
        cost_estimate=cost(5e10, 4e7, 1.3e7),
        name="encoder_attend_back",
    )(dmix, x, qkv, context, stats, inward, outward)
    return outs[:2], outs[2:]


def mask_kernel(slots_ref, across_ref, down_ref):
    count, width = slots_ref.shape
    words = down_ref.shape[0] // 32
    block = 32
    row = lax.broadcasted_iota(jnp.int32, (32, width), 0)
    for start in range(0, words, block):

        def step(i, totals):
            piece = slots_ref[pl.ds(pl.multiple_of(i * 8, 8), 8), :]
            word = lax.shift_right_logical(piece, 5)
            bit = jnp.left_shift(jnp.int32(1), piece & 31)
            return tuple(
                total | jnp.where(word == start + w, bit, 0) for w, total in enumerate(totals)
            )

        zero = jnp.zeros((8, width), jnp.int32)
        totals = lax.fori_loop(0, count // 8, step, (zero,) * block)
        for w, total in enumerate(totals):
            joined = total[0:1]
            for k in range(1, 8):
                joined = joined | total[k : k + 1]
            bits = lax.shift_right_logical(jnp.broadcast_to(joined, (32, width)), row) & 1
            at = (start + w) * 32
            down_ref[at : at + 32, :] = (wide(bits) - 1.0) * 1e30
    across_ref[...] = down_ref[...].T


def slot_mask(slots, pool):
    queries = slots.shape[0]
    return pl.pallas_call(
        mask_kernel,
        out_shape=[like((queries, pool), wide_type), like((pool, queries), wide_type)],
        in_specs=[pl.BlockSpec(memory_space=VMEM)],
        out_specs=[pl.BlockSpec(memory_space=VMEM)] * 2,
        compiler_params=params(24),
        cost_estimate=cost(1e10, 1e6),
        name="slot_mask",
    )(slots.T)


def pick_kernel(table_ref, states_ref, out_ref):
    spot = lax.broadcasted_iota(jnp.int32, (table_ref.shape[0], states_ref.shape[0]), 1)
    chosen = low((spot == table_ref[...]).astype(wide_type))
    out_ref[...] = low(dot(chosen, states_ref[...]))


def pick_rows(table, states):
    tokens, width = states.shape
    return pl.pallas_call(
        pick_kernel,
        grid=(table.size // 256,),
        in_specs=[pl.BlockSpec((256, 1), lambda i: (i, 0)), full(tokens, width)],
        out_specs=pl.BlockSpec((256, width), lambda i: (i, 0)),
        out_shape=like((table.size, width), low_type),
        compiler_params=params(24),
        cost_estimate=cost(4e9, 5e6),
        name="pick_rows",
    )(table.reshape(-1, 1), states)


def spread_kernel(table_ref, rows_ref, out_ref, total):
    step = pl.program_id(0)
    spot = lax.broadcasted_iota(jnp.int32, (out_ref.shape[0], table_ref.shape[1]), 0)
    chosen = low((spot == table_ref[...]).astype(wide_type))
    part = dot(chosen, rows_ref[...])

    @pl.when(step == 0)
    def _():
        total[...] = part

    @pl.when(step != 0)
    def _():
        total[...] += part

    @pl.when(step == pl.num_programs(0) - 1)
    def _():
        out_ref[...] = low(total[...])


def spread_rows(table, rows, tokens):
    width = rows.shape[1]
    return pl.pallas_call(
        spread_kernel,
        grid=(table.size // 512,),
        in_specs=[
            pl.BlockSpec((1, 512), lambda i: (0, i)),
            pl.BlockSpec((512, width), lambda i: (i, 0)),
        ],
        out_specs=full(tokens, width),
        out_shape=like((tokens, width), low_type),
        scratch_shapes=[VMEM((tokens, width), wide_type)],
        compiler_params=params(24),
        cost_estimate=cost(4e9, 5e6),
        name="spread_rows",
    )(table.reshape(1, -1), rows)


def by_head(value, lanes):
    return jnp.concatenate([value * lane for lane in lanes], 0)


def own_lanes(stacked, lanes):
    rows = stacked.shape[0] // len(lanes)
    return sum(stacked[h * rows : (h + 1) * rows] * lane for h, lane in enumerate(lanes))


def softmax_rows(scores):
    top = jnp.max(scores, -1, keepdims=True)
    weights = jnp.exp(scores - top)
    return weights * (1.0 / jnp.sum(weights, -1, keepdims=True))


def self_mask(lengths_ref, size):
    row = lax.broadcasted_iota(jnp.int32, (size, size), 0)
    column = lax.broadcasted_iota(jnp.int32, (size, size), 1)
    row_part, column_part = jnp.zeros_like(row), jnp.zeros_like(row)
    end = jnp.int32(0)
    for n in range(lengths_ref.shape[0] - 1):
        end = end + lengths_ref[n]
        row_part += (row >= end).astype(jnp.int32)
        column_part += (column >= end).astype(jnp.int32)
    allowed = (row_part == column_part) & (column <= row)
    added = jnp.where(allowed, 0.0, -1e30)
    return jnp.concatenate([added] * (GROUP // HEAD), 0)


def groups_of(width):
    return [slice(g, g + GROUP) for g in range(0, width, GROUP)]


def self_kernel(
    lengths_ref, y_ref, w_ref, wo_ref, b_ref, n_ref, cw_ref, qkv_ref, c_ref, mixed_ref, cq_ref
):
    y = y_ref[...]
    lanes_low, lanes = head_lanes(low_type), head_lanes(wide_type)
    mask = self_mask(lengths_ref, y.shape[0])
    qkv_ref[0] = low(dot(y, w_ref[0]) + b_ref[0:1])
    qkv_ref[1] = low(dot(y, w_ref[1]))
    qkv_ref[2] = low(dot(y, w_ref[2]) + b_ref[1:2])
    for part in groups_of(y.shape[1]):
        q = qkv_ref[0, :, part] * jnp.asarray(scale_scores, low_type)
        scores = dot(by_head(q, lanes_low), qkv_ref[1, :, part], NT) + mask
        weights = low(softmax_rows(scores))
        c_ref[:, part] = low(own_lanes(dot(weights, qkv_ref[2, :, part]), lanes))
    mixed = wide(y) + (dot(c_ref[...], wo_ref[...]) + b_ref[2:3])
    mixed_ref[...] = mixed
    first = low(norm_rows(mixed, n_ref[0, 0:1], n_ref[0, 1:2]))
    cq_ref[...] = low(dot(first, cw_ref[0]) + b_ref[3:4])


def self_forward(lengths, y, inward, outward, biases, norms, cross_inward):
    rows, width = y.shape
    return pl.pallas_call(
        self_kernel,
        grid=(1,),
        in_specs=[
            pl.BlockSpec(memory_space=pltpu.SMEM),
            full(rows, width),
            full(3, width, width),
            full(width, width),
            full(6, width),
            full(3, 2, width),
            full(1, width, width),
        ],
        out_specs=[
            full(3, rows, width),
            full(rows, width),
            full(rows, width),
            full(rows, width),
        ],
        out_shape=[
            like((3, rows, width), low_type),
            like((rows, width), low_type),
            like((rows, width), wide_type),
            like((rows, width), low_type),
        ],
        compiler_params=params(40),
        cost_estimate=cost(2e10, 7e6),
        name="self_forward",
    )(lengths, y, inward, outward, biases, norms, cross_inward)


def cross_kernel(pooled_ref, q_ref, mask_ref, w_ref, bg_ref, kv_ref, c_ref, stat_ref, scores, weights):
    rows = q_ref.shape[0]
    heads = GROUP // HEAD
    lanes_low, lanes = head_lanes(low_type), head_lanes(wide_type)
    kv_ref[0] = low(dot(pooled_ref[...], w_ref[1]))
    kv_ref[1] = low(dot(pooled_ref[...], w_ref[2]) + bg_ref[4:5])
    q = q_ref[...] * jnp.asarray(scale_scores, low_type)
    scores[...] = dot(by_head(q, lanes_low), kv_ref[0], NT)
    stats, scales = [], []
    for h in range(heads):
        part = slice(h * rows, (h + 1) * rows)
        masked = scores[part, :] + mask_ref[...]
        top = jnp.max(masked, -1, keepdims=True)
        weight = jnp.exp(masked - top)
        total = jnp.sum(weight, -1, keepdims=True)
        weights[part, :] = low(weight)
        stats.append(top + jnp.log(total))
        scales.append(lanes[h] * (1.0 / total))
    mixed = dot(weights[...], kv_ref[1])
    c_ref[...] = sum(mixed[h * rows : (h + 1) * rows] * scales[h] for h in range(heads))
    column = jnp.concatenate(stats, 0)
    stat_ref[0] = jnp.broadcast_to(column, (heads * rows, 128)).T[0:8]


def cross_forward(pooled, q, mask, inward, biases):
    slots, width = pooled.shape
    rows = q.shape[0]
    groups = width // GROUP
    stacked = rows * (GROUP // HEAD)
    return pl.pallas_call(
        cross_kernel,
        grid=(groups,),
        in_specs=[
            full(slots, width),
            pl.BlockSpec((rows, GROUP), lambda g: (0, g)),
            full(rows, slots),
            pl.BlockSpec((3, width, GROUP), lambda g: (0, 0, g)),
            pl.BlockSpec((6, GROUP), lambda g: (0, g)),
        ],
        out_specs=[
            pl.BlockSpec((2, slots, GROUP), lambda g: (0, 0, g)),
            pl.BlockSpec((rows, GROUP), lambda g: (0, g)),
            pl.BlockSpec((1, 8, stacked), lambda g: (g, 0, 0)),
        ],
        out_shape=[
            like((2, slots, width), low_type),
            like((rows, width), wide_type),
            like((groups, 8, stacked), wide_type),
        ],
        scratch_shapes=[VMEM((stacked, slots), wide_type), VMEM((stacked, slots), low_type)],
        compiler_params=params(),
        cost_estimate=cost(2e10, 1.2e7, 3e6),
        name="cross_forward",
    )(pooled, q, mask, inward, biases)


def middle_kernel(
    mixed_ref, c_ref, co_ref, b_ref, n_ref, e_ref, eb_ref, s_ref, sb_ref, grad_ref, *rest
):
    out_ref, joined_back_ref, dc_ref, vec_ref, deb_ref = rest[:5]
    hidden, slope, between, hold = rest[-4:]
    wide_outs, tall_outs, out_outs = thirds(rest[5:-4])
    width = mixed_ref.shape[1]
    blocks = [slice(i * width, (i + 1) * width) for i in range(e_ref.shape[1] // width)]
    first = norm_rows(mixed_ref[...], n_ref[0, 0:1], n_ref[0, 1:2])
    context = low(c_ref[...])
    joined = first + (dot(context, co_ref[...]) + b_ref[5:6])
    second = norm_rows(joined, n_ref[1, 0:1], n_ref[1, 1:2])
    second_low = low(second)
    total = jnp.zeros(joined.shape, wide_type)
    for part in blocks:
        value, rate = gelu_parts(dot(second_low, e_ref[:, part]) + eb_ref[:, part])
        hidden[:, part] = low(value)
        slope[:, part] = rate
        total += dot(hidden[:, part], s_ref[part, :])
    summed = second + (total + sb_ref[...])
    out_ref[...] = low(norm_rows(summed, n_ref[2, 0:1], n_ref[2, 1:2]))
    summed_back, gain, offset = norm_rows_back(summed, n_ref[2, 0:1], wide(grad_ref[...]))
    summed_low = low(summed_back)
    vec_ref[...] = jnp.zeros(vec_ref.shape, wide_type)
    vec_ref[0:1] = gain
    vec_ref[1:2] = offset
    vec_ref[2:3] = jnp.sum(wide(summed_low), 0, keepdims=True)
    second_back = summed_back
    for part in blocks:
        before = low(dot(summed_low, s_ref[part, :], NT) * slope[:, part])
        between[:, part] = before
        deb_ref[:, part] = jnp.sum(wide(before), 0, keepdims=True)
        second_back += dot(before, e_ref[:, part], NT)
    joined_back, gain, offset = norm_rows_back(joined, n_ref[1, 0:1], second_back)
    joined_low = low(joined_back)
    joined_back_ref[...] = joined_back
    vec_ref[3:4] = gain
    vec_ref[4:5] = offset
    vec_ref[5:6] = jnp.sum(wide(joined_low), 0, keepdims=True)
    dc_ref[...] = low(dot(joined_low, co_ref[...], NT))
    for i, part in enumerate(blocks):
        hold[...] = dot(second_low, between[:, part], TN)
        emit(wide_outs, i, hold)
        hold[...] = dot(hidden[:, part], summed_low, TN)
        emit_tall(tall_outs, i, hold)
    hold[...] = dot(context, joined_low, TN)
    emit(out_outs, 0, hold)


def middle(mixed, context, outward, biases, norms, expand, expand_bias, shrink, shrink_bias, grad):
    rows, width = mixed.shape
    total = expand.shape[1]
    ins = (
        mixed,
        context,
        outward,
        biases,
        norms,
        expand,
        expand_bias[None],
        shrink,
        shrink_bias[None],
        grad,
    )
    outs = pl.pallas_call(
        middle_kernel,
        grid=(1,),
        in_specs=[full(*value.shape) for value in ins],
        out_specs=[
            full(rows, width),
            full(rows, width),
            full(rows, width),
            full(8, width),
            full(1, total),
            *grad_specs(4, width, width),
            *grad_specs(1, total, width),
            *grad_specs(1, width, width),
        ],
        out_shape=[
            like((rows, width), low_type),
            like((rows, width), wide_type),
            like((rows, width), low_type),
            like((8, width), wide_type),
            like((1, total), wide_type),
            *grad_shapes(4, width, width),
            *grad_shapes(1, total, width),
            *grad_shapes(1, width, width),
        ],
        scratch_shapes=[
            VMEM((rows, total), low_type),
            VMEM((rows, total), wide_type),
            VMEM((rows, total), low_type),
            VMEM((width, width), wide_type),
        ],
        compiler_params=params(),
        cost_estimate=cost(2e10, 2.2e7),
        name="middle",
    )(*ins)
    return outs[:5], thirds(outs[5:])


def cross_back_kernel(
    kv_ref, q_ref, c_ref, dc_ref, stat_ref, mask_ref, w_ref, dkv_ref, dq_ref, vec_ref, dpool_ref,
    total, weights, scores_back
):
    group = pl.program_id(0)
    rows = q_ref.shape[0]
    heads = GROUP // HEAD
    lanes_low, lanes = head_lanes(low_type), head_lanes(wide_type)
    q_heads = by_head(q_ref[...] * jnp.asarray(scale_scores, low_type), lanes_low)
    dc_heads = by_head(dc_ref[...], lanes_low)
    product = wide(dc_heads) * jnp.concatenate([c_ref[...]] * heads, 0)
    column = jnp.sum(product, -1, keepdims=True)
    inner = jnp.broadcast_to(column, (heads * rows, 128)).T[0:1]
    stat = stat_ref[0, 0:1]
    for h in range(heads):
        part = slice(h * rows, (h + 1) * rows)
        weight = jnp.exp(dot(kv_ref[0], q_heads[part], NT) + mask_ref[...] - stat[:, part])
        weight_back = dot(kv_ref[1], dc_heads[part], NT)
        weights[:, part] = low(weight)
        scores_back[:, part] = low(weight * (weight_back - inner[:, part]))
    dk = low(dot(scores_back[...], q_heads))
    dv = low(dot(weights[...], dc_heads))
    dkv_ref[0] = dk
    dkv_ref[1] = dv
    dq = low(own_lanes(dot(scores_back[...], kv_ref[0], TN), lanes) * scale_scores)
    dq_ref[...] = dq
    vec_ref[...] = jnp.zeros(vec_ref.shape, wide_type)
    vec_ref[0:1] = jnp.sum(wide(dq), 0, keepdims=True)
    vec_ref[1:2] = jnp.sum(wide(dv), 0, keepdims=True)
    part = dot(dk, w_ref[1], NT) + dot(dv, w_ref[2], NT)

    @pl.when(group == 0)
    def _():
        total[...] = part

    @pl.when(group != 0)
    def _():
        total[...] += part

    @pl.when(group == pl.num_programs(0) - 1)
    def _():
        dpool_ref[...] = low(total[...])


def cross_back(kv, q, context, dc, stats, mask, inward):
    slots, width = kv.shape[1:]
    rows = q.shape[0]
    groups = width // GROUP
    stacked = rows * (GROUP // HEAD)
    column = pl.BlockSpec((rows, GROUP), lambda g: (0, g))
    return pl.pallas_call(
        cross_back_kernel,
        grid=(groups,),
        in_specs=[
            pl.BlockSpec((2, slots, GROUP), lambda g: (0, 0, g)),
            column,
            column,
            column,
            pl.BlockSpec((1, 8, stacked), lambda g: (g, 0, 0)),
            full(slots, rows),
            pl.BlockSpec((3, width, GROUP), lambda g: (0, 0, g)),
        ],
        out_specs=[
            pl.BlockSpec((2, slots, GROUP), lambda g: (0, 0, g)),
            column,
            pl.BlockSpec((8, GROUP), lambda g: (0, g)),
            full(slots, width),
        ],
        out_shape=[
            like((2, slots, width), low_type),
            like((rows, width), low_type),
            like((8, width), wide_type),
            like((slots, width), low_type),
        ],
        scratch_shapes=[
            VMEM((slots, width), wide_type),
            VMEM((slots, stacked), low_type),
            VMEM((slots, stacked), low_type),
        ],
        compiler_params=params(),
        cost_estimate=cost(3e10, 2.2e7, 3e6),
        name="cross_back",
    )(kv, q, context, dc, stats, mask, inward)


def cross_grads_kernel(pooled_ref, dkv_ref, mixed_ref, dq_ref, n_ref, *rest):
    outs, (turned, hold) = rest[:-2], rest[-2:]

    @pl.when(pl.program_id(0) == 0)
    def _():
        turned[...] = pooled_ref[...].T

    first = low(norm_rows(mixed_ref[...], n_ref[0, 0:1], n_ref[0, 1:2]))
    hold[...] = dot(first, dq_ref[...], TN)
    emit(outs, 0, hold)
    hold[...] = dot(turned[...], dkv_ref[0])
    emit(outs, 1, hold)
    hold[...] = dot(turned[...], dkv_ref[1])
    emit(outs, 2, hold)


def cross_grads(pooled, dkv, mixed, dq, norms):
    slots, width = pooled.shape
    rows = mixed.shape[0]
    return pl.pallas_call(
        cross_grads_kernel,
        grid=(width // GROUP,),
        in_specs=[
            full(slots, width),
            pl.BlockSpec((2, slots, GROUP), lambda g: (0, 0, g)),
            full(rows, width),
            pl.BlockSpec((rows, GROUP), lambda g: (0, g)),
            full(3, 2, width),
        ],
        out_specs=grad_specs(3, width, GROUP, lambda g: (0, 0, g)),
        out_shape=grad_shapes(3, width, width),
        scratch_shapes=[VMEM((width, slots), low_type), VMEM((width, GROUP), wide_type)],
        compiler_params=params(48),
        cost_estimate=cost(1e10, 1.5e7),
        name="cross_grads",
    )(pooled, dkv, mixed, dq, norms)


def self_back_kernel(
    lengths_ref, y_ref, mixed_ref, jb_ref, cdq_ref, qkv_ref, c_ref, w_ref, wo_ref, cw_ref, n_ref,
    dy_ref, vec_ref, *rest
):
    outs, (dqkv, hold) = rest[:-2], rest[-2:]
    width = y_ref.shape[1]
    y = y_ref[...]
    lanes_low, lanes = head_lanes(low_type), head_lanes(wide_type)
    mask = self_mask(lengths_ref, y.shape[0])
    first_back = jb_ref[...] + dot(cdq_ref[...], cw_ref[0], NT)
    mixed_back, gain, offset = norm_rows_back(mixed_ref[...], n_ref[0, 0:1], first_back)
    mixed_low = low(mixed_back)
    vec_ref[...] = jnp.zeros(vec_ref.shape, wide_type)
    vec_ref[0:1] = gain
    vec_ref[1:2] = offset
    vec_ref[2:3] = jnp.sum(wide(mixed_low), 0, keepdims=True)
    dc = low(dot(mixed_low, wo_ref[...], NT))
    for part in groups_of(width):
        q_heads = by_head(qkv_ref[0, :, part] * jnp.asarray(scale_scores, low_type), lanes_low)
        dc_heads = by_head(dc[:, part], lanes_low)
        weights = softmax_rows(dot(q_heads, qkv_ref[1, :, part], NT) + mask)
        weights_back = dot(dc_heads, qkv_ref[2, :, part], NT)
        inner = jnp.sum(weights * weights_back, -1, keepdims=True)
        scores_back = low(weights * (weights_back - inner))
        dq = own_lanes(dot(scores_back, qkv_ref[1, :, part]), lanes) * scale_scores
        dqkv[0, :, part] = low(dq)
        dqkv[1, :, part] = low(dot(scores_back, q_heads, TN))
        dqkv[2, :, part] = low(dot(low(weights), dc_heads, TN))
    vec_ref[3:4] = jnp.sum(wide(dqkv[0]), 0, keepdims=True)
    vec_ref[4:5] = jnp.sum(wide(dqkv[2]), 0, keepdims=True)
    dy_ref[...] = (
        mixed_back
        + dot(dqkv[0], w_ref[0], NT)
        + (dot(dqkv[1], w_ref[1], NT) + dot(dqkv[2], w_ref[2], NT))
    )
    for part in range(3):
        hold[...] = dot(y, dqkv[part], TN)
        emit(outs, part, hold)
    hold[...] = dot(c_ref[...], mixed_low, TN)
    emit(outs, 3, hold)


def self_back(lengths, y, mixed, joined_back, dq, qkv, context, inward, outward, cross_inward, norms):
    rows, width = y.shape
    ins = (y, mixed, joined_back, dq, qkv, context, inward, outward)
    outs = pl.pallas_call(
        self_back_kernel,
        grid=(1,),
        in_specs=[
            pl.BlockSpec(memory_space=pltpu.SMEM),
            *[full(*value.shape) for value in ins],
            full(1, width, width),
            full(3, 2, width),
        ],
        out_specs=[full(rows, width), full(8, width), *grad_specs(4, width, width)],
        out_shape=[
            like((rows, width), wide_type),
            like((8, width), wide_type),
            *grad_shapes(4, width, width),
        ],
        scratch_shapes=[VMEM((3, rows, width), low_type), VMEM((width, width), wide_type)],
        compiler_params=params(48),
        cost_estimate=cost(2e10, 1.5e7),
        name="self_back",
    )(lengths, *ins, cross_inward, norms)
    return outs[:2], outs[2:]


def shifted(value, axis, by):
    length = lax.axis_size(axis)
    return lax.ppermute(value, axis, [(i, (i + by) % length) for i in range(length)])


COUNT = 7
ROWS = 384
HALF = ROWS // 2
QUARTER = ROWS // 4
VEC_ROWS = 32


def add_rows(to, other, rows):
    def step(i, carry):
        at = pl.ds(pl.multiple_of(i * 32, 32), 32)
        to[at, :] = low(wide(to[at, :]) + wide(other[at, :]))
        return carry

    lax.fori_loop(0, rows // 32, step, 0)


def partners():
    me, section = lax.axis_index("dp"), lax.axis_index("section")
    return (
        {"dp": me + 1 - 2 * (me % 2)},
        {"dp": me + 2 - 4 * ((me // 2) % 2)},
        {"dp": me + 4 - 8 * (me // 4)},
        {"section": section + 1 - 2 * (section % 2)},
        {"section": section + 2 - 4 * (section // 2)},
    )


def greet():
    barrier = pltpu.get_barrier_semaphore()
    for partner in partners():
        pl.semaphore_signal(barrier, 1, device_id=partner, device_id_type=pl.DeviceIdType.MESH)
    pl.semaphore_wait(barrier, 5)


def sum_kernel(sources, *refs):
    count = len(sources)
    keeps, sends, vec_ref = refs[:count], refs[count : 2 * count], refs[2 * count]
    out_ref, vec_out = refs[2 * count + 1 : 2 * count + 3]
    own, from_core, from_one, from_two, from_three, from_four, whole, vec_in = refs[
        2 * count + 3 : 2 * count + 11
    ]
    load_sems, core_send, core_recv, send_sems, recv_sems, vec_send, vec_recv, out_sems = refs[
        2 * count + 11 :
    ]
    core, over_x, over_y, near, far = partners()
    section = lax.axis_index("section")
    side = section % 2
    far_side = section // 2
    half_at = pl.multiple_of(side * HALF, HALF)
    half_other = pl.multiple_of((1 - side) * HALF, HALF)
    quarter_at = pl.multiple_of(side * HALF + far_side * QUARTER, QUARTER)
    quarter_other = pl.multiple_of(side * HALF + (1 - far_side) * QUARTER, QUARTER)
    upper, lower = pl.ds(0, HALF), pl.ds(HALF, HALF)

    def remote(source, to, send, recv, partner):
        return pltpu.make_async_remote_copy(
            src_ref=source,
            dst_ref=to,
            send_sem=send,
            recv_sem=recv,
            device_id=partner,
            device_id_type=pl.DeviceIdType.MESH,
        )

    loads, first = [], []
    for n, (chunk, row) in enumerate(sources):
        rows = pl.ds(row, keeps[n].shape[1])
        loads.append(
            pltpu.make_async_copy(
                keeps[n], own.at[chunk, :, rows], load_sems.at[n]
            )
        )
        first.append(
            remote(sends[n], from_core.at[chunk, :, rows], core_send.at[n], core_recv.at[n], core)
        )

    def pairs(stage, c):
        total = own.at[c, 0]
        if stage == 1:
            return (
                (own.at[c, pl.ds(1, 1), upper], from_one.at[c, 0, pl.ds(0, 1)], over_x),
                (own.at[c, pl.ds(3, 1), upper], from_one.at[c, 0, pl.ds(1, 1)], over_x),
                (own.at[c, pl.ds(2, 2), lower], from_one.at[c, 1], over_y),
            )
        if stage == 2:
            return (
                (own.at[c, 2, upper], from_two.at[c, 0], over_y),
                (own.at[c, 1, lower], from_two.at[c, 1], over_x),
            )
        if stage == 3:
            return ((total.at[pl.ds(half_other, HALF)], from_three.at[c], near),)
        if stage == 4:
            return ((total.at[pl.ds(quarter_other, QUARTER)], from_four.at[c], far),)
        if stage == 5:
            rows = pl.ds(quarter_at, QUARTER)
            return ((whole.at[c, rows], whole.at[c, rows], far),)
        rows = pl.ds(half_at, HALF)
        return ((whole.at[c, rows], whole.at[c, rows], near),)

    def copies(stage, c):
        return [
            remote(source, to, send_sems.at[stage, c, k], recv_sems.at[stage, c, k], partner)
            for k, (source, to, partner) in enumerate(pairs(stage, c))
        ]

    def start(stage, c):
        for copy in copies(stage, c):
            copy.start()

    def land(stage, c):
        for copy in copies(stage, c):
            copy.wait_recv()

    def out_copy(c):
        return pltpu.make_async_copy(whole.at[c], out_ref.at[c], out_sems.at[c])

    def vec_copy(stage):
        return remote(
            vec_out, vec_in.at[stage], vec_send.at[stage], vec_recv.at[stage], partners()[stage]
        )

    def vec_step(stage):
        if stage:
            vec_copy(stage - 1).wait()
            vec_out[...] += vec_in[stage - 1]
        else:
            vec_out[...] = vec_ref[...]
        if stage < 5:
            vec_copy(stage).start()

    def step(stage, c):
        if stage == 0:
            for n, (chunk, _) in enumerate(sources):
                if chunk == c:
                    loads[n].wait()
                    first[n].wait_recv()
            for at in range(4):
                add_rows(own.at[c, at], from_core.at[c, at], ROWS)
            start(1, c)
            return
        land(stage, c)
        if stage == 1:
            for k in range(2):
                add_rows(own.at[c, 2 * k, upper], from_one.at[c, 0, k], HALF)
                add_rows(own.at[c, k, lower], from_one.at[c, 1, k], HALF)
        elif stage == 2:
            add_rows(own.at[c, 0, upper], from_two.at[c, 0], HALF)
            add_rows(own.at[c, 0, lower], from_two.at[c, 1], HALF)
        elif stage == 3:
            add_rows(own.at[c, 0, pl.ds(half_at, HALF)], from_three.at[c], HALF)
        elif stage == 4:
            rows = pl.ds(quarter_at, QUARTER)
            whole[c, rows, :] = low(wide(own[c, 0, rows, :]) + wide(from_four[c]))
        if stage < 6:
            start(stage + 1, c)
        else:
            out_copy(c).start()

    greet()
    for n in range(count):
        first[n].start()
        loads[n].start()
    vec_step(0)
    for time in range(COUNT + 6):
        for stage in reversed(range(7)):
            if 0 <= time - stage < COUNT:
                step(stage, time - stage)
        if 1 <= time + 1 <= 5:
            vec_step(time + 1)
    for n in range(count):
        first[n].wait_send()
    for c in range(COUNT):
        for stage in range(1, 7):
            for copy in copies(stage, c):
                copy.wait_send()
        out_copy(c).wait()


def sum_pairs(pairs, sources, vector):
    count = len(pairs)
    width = pairs[0][0].shape[2]
    anywhere = pl.BlockSpec(memory_space=pl.ANY)
    here = pl.BlockSpec(memory_space=VMEM)
    dma = pltpu.SemaphoreType.DMA
    return pl.pallas_call(
        functools.partial(sum_kernel, sources),
        in_specs=[anywhere] * (2 * count) + [here],
        out_specs=[anywhere, here],
        out_shape=[
            like((COUNT, ROWS, width), low_type),
            like((VEC_ROWS, width), wide_type),
        ],
        scratch_shapes=[
            VMEM((COUNT, 4, ROWS, width), low_type),
            VMEM((COUNT, 4, ROWS, width), low_type),
            VMEM((COUNT, 2, 2, HALF, width), low_type),
            VMEM((COUNT, 2, HALF, width), low_type),
            VMEM((COUNT, HALF, width), low_type),
            VMEM((COUNT, QUARTER, width), low_type),
            VMEM((COUNT, ROWS, width), low_type),
            VMEM((5, VEC_ROWS, width), wide_type),
            dma((count,)),
            dma((count,)),
            dma((count,)),
            dma((7, COUNT, 3)),
            dma((7, COUNT, 3)),
            dma((5,)),
            dma((5,)),
            dma((COUNT,)),
        ],
        compiler_params=params(60, collective_id=1, has_side_effects=True),
        cost_estimate=cost(1e8, 1e8),
        name="sum_pairs",
    )(*[p[0] for p in pairs], *[p[1] for p in pairs], vector)


def sum_whole(grads):
    parts = lax.axis_size("dp")
    packed = []
    for grad in grads:
        count, rows, columns = grad.shape
        cut = grad.reshape(count, parts, rows // parts, columns // WIDTH, WIDTH)
        packed.append(cut.transpose(1, 0, 3, 2, 4).reshape(parts, -1, WIDTH))
    shard = lax.psum_scatter(jnp.concatenate(packed, 1), "dp", scatter_dimension=0, tiled=True)[0]
    total = wide(lax.psum(shard, "section"))
    outs, at = [], 0
    for grad in grads:
        count, rows, columns = grad.shape
        size = grad.size // parts // WIDTH
        cut = total[at : at + size].reshape(count, columns // WIDTH, rows // parts, WIDTH)
        outs.append(cut.transpose(0, 2, 1, 3).reshape(count * rows // parts, columns))
        at += size
    return outs


def sum_all(grads, vectors):
    flat = jnp.concatenate([v.reshape(-1) for v in vectors])
    if paired():
        sources = ((0, 0), (1, 0), (2, 0), (2, 288), (3, 0), (4, 0), (5, 0), (6, 0), (6, 288))
        rows = [grad[0].shape[1] for grad in grads]
        padded = jnp.pad(flat, (0, VEC_ROWS * WIDTH - flat.size)).reshape(VEC_ROWS, WIDTH)
        total, flat = sum_pairs(grads, sources, padded)
        flat = flat.reshape(-1)
        shards = [
            wide(total[chunk, row : row + size]) for (chunk, row), size in zip(sources, rows)
        ]
    else:
        shards = sum_whole([grad[0] for grad in grads])
        flat = lax.psum(flat, ("dp", "section"))
    parts, mine = lax.axis_size("dp"), lax.axis_index("dp")
    outs, at = [], 0
    for v in vectors:
        whole = flat[at : at + v.size].reshape(v.shape)
        at += v.size
        size = v.shape[-1] // parts
        outs.append(lax.dynamic_slice_in_dim(whole, mine * size, size, v.ndim - 1))
    return shards, outs


def beside(shard):
    rows = shard.shape[0] // 4
    return shard.reshape(4, rows, WIDTH).transpose(1, 0, 2).reshape(rows, 4 * WIDTH)


def on_device(
    encoder_input,
    decoder_input,
    cotangent,
    pool_table,
    retrieved,
    decoder_lengths,
    encoder_inward,
    encoder_outward,
    encoder_biases,
    encoder_norms,
    encoder_expand,
    encoder_expand_bias,
    encoder_shrink,
    encoder_shrink_bias,
    self_inward,
    self_outward,
    cross_inward,
    cross_outward,
    decoder_biases,
    decoder_norms,
    decoder_expand,
    decoder_expand_bias,
    decoder_shrink,
    decoder_shrink_bias,
):
    x = encoder_input[0]
    half_way = lax.axis_size("section") // 2
    queries = decoder_input.shape[1]
    topk = retrieved.shape[2]
    rows_low = shifted(jnp.concatenate([decoder_input[0], cotangent[0]], 0), "section", -half_way)
    y, grad = rows_low[:queries], rows_low[queries:]
    lengths_row = jnp.pad(decoder_lengths[0], ((0, 0), (0, topk - decoder_lengths.shape[2])))
    integers = shifted(
        jnp.concatenate([retrieved[0], pool_table[0, 0].reshape(-1, topk), lengths_row], 0),
        "section",
        -half_way,
    )
    slots = integers[:queries]
    table = integers[queries:-1].reshape(-1)
    lengths = integers[-1, : decoder_lengths.shape[2]]
    owners = pool_table.shape[2]

    qkv, context, stats, mixed = encoder_attend(
        x, encoder_inward, encoder_outward, encoder_biases
    )
    hidden, slope, summed, states = encoder_feed(
        mixed,
        encoder_norms,
        encoder_expand,
        encoder_expand_bias,
        encoder_shrink,
        encoder_shrink_bias,
    )
    picked = pick_rows(table, states).reshape(owners, -1, WIDTH)
    pooled = lax.all_to_all(picked, "dp", split_axis=0, concat_axis=0, tiled=True)
    pooled = pooled.reshape(-1, WIDTH)

    mask_across, mask_down = slot_mask(slots, pooled.shape[0])
    self_qkv, self_context, self_mixed, cross_q = self_forward(
        lengths, y, self_inward, self_outward, decoder_biases, decoder_norms, cross_inward
    )
    kv, cross_context, cross_stats = cross_forward(
        pooled, cross_q, mask_across, cross_inward, decoder_biases
    )
    (out, joined_back, dc, mid_vec, mid_expand), (d_expand, d_shrink, d_cross_out) = middle(
        self_mixed,
        cross_context,
        cross_outward,
        decoder_biases,
        decoder_norms,
        decoder_expand,
        decoder_expand_bias,
        decoder_shrink,
        decoder_shrink_bias,
        grad,
    )
    dkv, dq, cross_vec, dpool = cross_back(
        kv, cross_q, cross_context, dc, cross_stats, mask_down, cross_inward
    )
    returned = lax.all_to_all(
        dpool.reshape(owners, -1, WIDTH), "dp", split_axis=0, concat_axis=0, tiled=True
    )
    d_cross_in = cross_grads(pooled, dkv, self_mixed, dq, decoder_norms)
    (dy, self_vec), d_self = self_back(
        lengths,
        y,
        self_mixed,
        joined_back,
        dq,
        self_qkv,
        self_context,
        self_inward,
        self_outward,
        cross_inward,
        decoder_norms,
    )
    decoder_out = shifted(out, "section", half_way)
    decoder_grad = shifted(dy, "section", half_way)
    states_back = spread_rows(table, returned.reshape(-1, WIDTH), x.shape[0])

    (dmix, feed_vec, feed_expand), (e_expand, e_shrink, e_out) = encoder_feed_back(
        states_back,
        summed,
        mixed,
        hidden,
        slope,
        context,
        encoder_norms,
        encoder_expand,
        encoder_shrink,
    )
    (dx, attend_vec), e_in = encoder_attend_back(
        dmix, x, qkv, context, stats, encoder_inward, encoder_outward
    )

    shards, vectors = sum_all(
        [d_expand, d_shrink, d_cross_in, d_cross_out, d_self, e_expand, e_shrink, e_in, e_out],
        [
            jnp.concatenate([attend_vec[0:2], feed_vec[5:6]], 0),
            jnp.stack([feed_vec[3:5], feed_vec[0:2]]),
            feed_expand[0],
            feed_vec[2],
            jnp.concatenate([self_vec[3:5], self_vec[2:3], cross_vec[0:2], mid_vec[5:6]], 0),
            jnp.stack([self_vec[0:2], mid_vec[3:5], mid_vec[0:2]]),
            mid_expand[0],
            mid_vec[2],
        ],
    )
    d_expand, d_shrink, d_cross_in, d_cross_out, d_self, e_expand, e_shrink, e_in, e_out = shards
    rows = WIDTH // lax.axis_size("dp")
    return (
        decoder_out[None],
        dx[None],
        decoder_grad[None],
        e_in.reshape(3, rows, WIDTH),
        e_out,
        vectors[0],
        vectors[1],
        beside(e_expand),
        vectors[2],
        e_shrink,
        vectors[3],
        d_self[: 3 * rows].reshape(3, rows, WIDTH),
        d_self[3 * rows :],
        d_cross_in.reshape(3, rows, WIDTH),
        d_cross_out,
        vectors[4],
        vectors[5],
        beside(d_expand),
        vectors[6],
        d_shrink,
        vectors[7],
    )


def solution(mesh):
    in_specs = (
        P("section", "dp", None),
        P("section", "dp", None),
        P("section", "dp", None),
        P("section", "dp", None, None),
        P("section", "dp", None),
        P("section", "dp", None),
        P(),
        P(),
        P(),
        P(),
        P(),
        P(),
        P(),
        P(),
        P(),
        P(),
        P(),
        P(),
        P(),
        P(),
        P(),
        P(),
        P(),
        P(),
    )
    out_specs = (
        P("section", "dp", None),
        P("section", "dp", None),
        P("section", "dp", None),
        P(None, "dp", None),
        P("dp", None),
        P(None, "dp"),
        P(None, None, "dp"),
        P("dp", None),
        P("dp"),
        P("dp", None),
        P("dp"),
        P(None, "dp", None),
        P("dp", None),
        P(None, "dp", None),
        P("dp", None),
        P(None, "dp"),
        P(None, None, "dp"),
        P("dp", None),
        P("dp"),
        P("dp", None),
        P("dp"),
    )
    return jax.shard_map(
        on_device, mesh=mesh, in_specs=in_specs, out_specs=out_specs, check_vma=False
    )
```

```python
import functools

import jax
import jax.numpy as jnp
from jax import lax
from jax.experimental import pallas as pl
from jax.experimental.pallas import tpu as pltpu
from jax.sharding import PartitionSpec as P

HEAD = 64
WIDTH = 768


norm_eps = 1e-05
scale_scores = 0.125
low_type = jnp.bfloat16
wide_type = jnp.float32

NN = (((1,), (0,)), ((), ()))
NT = (((1,), (1,)), ((), ()))
TN = (((0,), (0,)), ((), ()))
GROUP = 256
VMEM = pltpu.VMEM


def dot(left, right, dims=NN):
    return lax.dot_general(left, right, dims, preferred_element_type=wide_type)


def low(value):
    return value.astype(low_type)


def wide(value):
    return value.astype(wide_type)


def head_lanes(dtype):
    lane = lax.broadcasted_iota(jnp.int32, (1, GROUP), 1) // HEAD
    return [(lane == h).astype(wide_type).astype(dtype) for h in range(GROUP // HEAD)]


def centred_of(values):
    centred = values - jnp.mean(values, -1, keepdims=True)
    spread = jnp.mean(centred * centred, -1, keepdims=True)
    return centred, lax.rsqrt(spread + norm_eps)


def norm_rows(values, gain, offset):
    centred, scale = centred_of(values)
    return centred * scale * (1.0 + gain) + offset


def norm_rows_back(values, gain, incoming):
    centred, scale = centred_of(values)
    unit = centred * scale
    inner = incoming * (1.0 + gain)
    mean_inner = jnp.mean(inner, -1, keepdims=True)
    mean_along = jnp.mean(inner * unit, -1, keepdims=True)
    return (
        scale * (inner - mean_inner - unit * mean_along),
        jnp.sum(incoming * unit, 0, keepdims=True),
        jnp.sum(incoming, 0, keepdims=True),
    )


def gelu_parts(u):
    size = jnp.abs(u) * 0.7071067811865476
    t = 1.0 / (1.0 + 0.3275911 * size)
    bell = jnp.exp(-0.5 * u * u)
    series = t * (
        0.254829592
        + t * (-0.284496736 + t * (1.421413741 + t * (-1.453152027 + t * 1.061405429)))
    )
    tail = 0.5 * series * bell
    share = jnp.where(u < 0.0, tail, 1.0 - tail)
    return u * share, share + u * (bell * 0.3989422804014327)


def params(limit=60, **rest):
    return pltpu.CompilerParams(vmem_limit_bytes=limit * 2**20, **rest)


def host_params(plan):
    if plan:
        return params(62, collective_id=plan.collective_id, has_side_effects=True)
    return params()


def cost(flops, size, exps=0):
    return pl.CostEstimate(flops=int(flops), bytes_accessed=int(size), transcendentals=int(exps))


def full(*shape):
    return pl.BlockSpec(shape, lambda *_: (0,) * len(shape))


def once(*shape):
    return pl.BlockSpec(shape, lambda *_: (0,) * len(shape), pipeline_mode=pl.Buffered(1))


def like(shape, dtype):
    return jax.ShapeDtypeStruct(shape, dtype)


def paired():
    return lax.axis_size("dp") == 8


def grad_shapes(parts, rows, columns):
    if paired():
        return [like((4, parts * rows // 8, columns), low_type)] * 2
    return [like((parts, rows, columns), low_type)]


def grad_specs(parts, rows, columns, index=None):
    if paired():
        block, count = (4, parts * rows // 8, columns), 2
    else:
        block, count = (parts, rows, columns), 1
    return [pl.BlockSpec(block, index or (lambda *_: (0, 0, 0)))] * count


def emit(outs, part, hold):
    if len(outs) == 1:
        outs[0][part] = low(hold[...])
        return
    keep, send = outs
    me = lax.axis_index("dp")
    rows = hold.shape[0] // 8
    to = pl.ds(pl.multiple_of(part * rows, rows), rows)
    for at in range(4):
        mine = pl.multiple_of((me ^ (2 * at)) * rows, rows)
        other = pl.multiple_of((me ^ (2 * at + 1)) * rows, rows)
        keep[at, to, :] = low(hold[pl.ds(mine, rows), :])
        send[at, to, :] = low(hold[pl.ds(other, rows), :])


def emit_tall(outs, block, hold):
    if len(outs) == 1:
        size = hold.shape[0]
        outs[0][0, pl.ds(pl.multiple_of(block * size, size), size), :] = low(hold[...])
        return
    keep, send = outs
    me = lax.axis_index("dp")
    rows = hold.shape[0] // 2
    at = block ^ lax.shift_right_logical(me, 1)
    core = me & 1
    keep[at, 0:rows, :] = low(hold[pl.ds(pl.multiple_of(core * rows, rows), rows), :])
    send[at, 0:rows, :] = low(hold[pl.ds(pl.multiple_of((1 - core) * rows, rows), rows), :])


def thirds(items):
    third = len(items) // 3
    return items[:third], items[third : 2 * third], items[2 * third :]


def encoder_attend_kernel(
    x_ref, w_ref, wo_ref, bg_ref, b_ref, qkv_ref, c_ref, cl_ref, stat_ref, mixed_ref, stats
):
    group = pl.program_id(0)
    tokens = x_ref.shape[0]
    block = 256
    x = x_ref[...]
    qkv_ref[0] = low(dot(x, w_ref[0]) + bg_ref[0:1])
    qkv_ref[1] = low(dot(x, w_ref[1]))
    qkv_ref[2] = low(dot(x, w_ref[2]) + bg_ref[1:2])
    lanes_low, lanes = head_lanes(low_type), head_lanes(wide_type)
    lane = lax.broadcasted_iota(jnp.int32, (1, 128), 1)

    @pl.when(group == 0)
    def _():
        mixed_ref[...] = wide(x) + b_ref[2:3]

    def rows_step(i, carry):
        rows = pl.ds(pl.multiple_of(i * block, block), block)
        q = qkv_ref[0, rows, :] * jnp.asarray(scale_scores, low_type)
        context = jnp.zeros((block, GROUP), wide_type)
        stat = jnp.zeros((block, 128), wide_type)
        for h in range(GROUP // HEAD):
            scores = dot(q * lanes_low[h], qkv_ref[1], NT)
            top = jnp.max(scores, -1, keepdims=True)
            weights = jnp.exp(scores - top)
            total = jnp.sum(weights, -1, keepdims=True)
            context += dot(low(weights), qkv_ref[2]) * (lanes[h] * (1.0 / total))
            stat = jnp.where(lane == h, top + jnp.log(total), stat)
        c_ref[rows, :] = context
        cl_ref[rows, :] = low(context)
        stats[rows, :] = stat
        mixed_ref[rows, :] += dot(low(context), wo_ref[...])
        return carry

    lax.fori_loop(0, tokens // block, rows_step, 0)
    stat_ref[0] = stats[...].T[0:8]


def encoder_attend(x, inward, outward, biases):
    tokens, width = x.shape
    groups = width // GROUP
    return pl.pallas_call(
        encoder_attend_kernel,
        grid=(groups,),
        in_specs=[
            full(tokens, width),
            pl.BlockSpec((3, width, GROUP), lambda g: (0, 0, g)),
            pl.BlockSpec((GROUP, width), lambda g: (g, 0)),
            pl.BlockSpec((3, GROUP), lambda g: (0, g)),
            full(3, width),
        ],
        out_specs=[
            pl.BlockSpec((3, tokens, GROUP), lambda g: (0, 0, g)),
            pl.BlockSpec((tokens, GROUP), lambda g: (0, g)),
            pl.BlockSpec((tokens, GROUP), lambda g: (0, g)),
            pl.BlockSpec((1, 8, tokens), lambda g: (g, 0, 0)),
            full(tokens, width),
        ],
        out_shape=[
            like((3, tokens, width), low_type),
            like((tokens, width), wide_type),
            like((tokens, width), low_type),
            like((groups, 8, tokens), wide_type),
            like((tokens, width), wide_type),
        ],
        scratch_shapes=[VMEM((tokens, 128), wide_type)],
        compiler_params=params(),
        cost_estimate=cost(3e10, 2e7, 1.3e7),
        name="encoder_attend",
    )(x, inward, outward, biases, biases)


def encoder_feed_kernel(
    mixed_ref, n_ref, e_ref, eb_ref, s_ref, sb_ref, h_ref, d_ref, sum_ref, out_ref, a_low
):
    step = pl.program_id(0)
    tokens = mixed_ref.shape[0]
    block = 256

    @pl.when(step == 0)
    def _():
        def rows_step(i, carry):
            rows = pl.ds(pl.multiple_of(i * 128, 128), 128)
            first = norm_rows(mixed_ref[rows, :], n_ref[0, 0:1], n_ref[0, 1:2])
            a_low[rows, :] = low(first)
            sum_ref[rows, :] = first + sb_ref[...]
            return carry

        lax.fori_loop(0, tokens // 128, rows_step, 0)

    for i in range(tokens // block):
        rows = slice(i * block, (i + 1) * block)
        hidden, slope = gelu_parts(dot(a_low[rows, :], e_ref[...]) + eb_ref[...])
        h_ref[rows, :] = low(hidden)
        d_ref[rows, :] = low(slope)
        sum_ref[rows, :] += dot(low(hidden), s_ref[...])

    @pl.when(step == pl.num_programs(0) - 1)
    def _():
        def rows_step(i, carry):
            rows = pl.ds(pl.multiple_of(i * 128, 128), 128)
            out_ref[rows, :] = low(norm_rows(sum_ref[rows, :], n_ref[1, 0:1], n_ref[1, 1:2]))
            return carry

        lax.fori_loop(0, tokens // 128, rows_step, 0)


def encoder_feed(mixed, norms, expand, expand_bias, shrink, shrink_bias):
    tokens, width = mixed.shape
    hidden = expand.shape[1]
    cut = hidden // 4
    return pl.pallas_call(
        encoder_feed_kernel,
        grid=(4,),
        in_specs=[
            full(tokens, width),
            full(2, 2, width),
            pl.BlockSpec((width, cut), lambda i: (0, i)),
            pl.BlockSpec((1, cut), lambda i: (0, i)),
            pl.BlockSpec((cut, width), lambda i: (i, 0)),
            full(1, width),
        ],
        out_specs=[
            pl.BlockSpec((tokens, cut), lambda i: (0, i)),
            pl.BlockSpec((tokens, cut), lambda i: (0, i)),
            full(tokens, width),
            full(tokens, width),
        ],
        out_shape=[
            like((tokens, hidden), low_type),
            like((tokens, hidden), low_type),
            like((tokens, width), wide_type),
            like((tokens, width), low_type),
        ],
        scratch_shapes=[VMEM((tokens, width), low_type)],
        compiler_params=params(),
        cost_estimate=cost(2e10, 3e7, 3e6),
        name="encoder_feed",
    )(mixed, norms, expand, expand_bias[None], shrink, shrink_bias[None])


def split_refs(refs, *counts):
    out, at = [], 0
    for count in counts:
        out.append(refs[at : at + count])
        at += count
    return out + [refs[at:]]


def hosting(plan):
    return (plan.ins, len(plan.outs())) if plan else (0, 0)


def encoder_feed_back_kernel(plan, *refs):
    grads = 6 if paired() else 3
    host_ins, host_outs = hosting(plan)
    main, guests, outs, guest_outs, scratch, guest_scratch = split_refs(
        refs, 9, host_ins, 3 + grads, host_outs, 4
    )
    g_ref, sum_ref, mixed_ref, h_ref, d_ref, c_ref, n_ref, e_ref, s_ref = main
    dmix_ref, vec_ref, eb_ref = outs[:3]
    wide_outs, tall_outs, out_outs = thirds(outs[3:])
    back_low, a_turned, between, hold = scratch
    step = pl.program_id(0)
    sums = plan.open(guests, guest_outs, guest_scratch) if plan else None

    def place(n):
        if sums:
            sums.slot(step, 4, 3, n)

    place(0)
    tokens = sum_ref.shape[0]
    block = 256

    @pl.when(step == 0)
    def _():
        vec_ref[...] = jnp.zeros(vec_ref.shape, wide_type)

        def rows_step(i, carry):
            rows = pl.ds(pl.multiple_of(i * 128, 128), 128)
            grad, gain, offset = norm_rows_back(
                sum_ref[rows, :], n_ref[1, 0:1], wide(g_ref[rows, :])
            )
            dmix_ref[rows, :] = grad
            back_low[rows, :] = low(grad)
            vec_ref[0:1] += gain
            vec_ref[1:2] += offset
            vec_ref[2:3] += jnp.sum(wide(low(grad)), 0, keepdims=True)
            first = norm_rows(mixed_ref[rows, :], n_ref[0, 0:1], n_ref[0, 1:2])
            a_turned[:, rows] = low(first).T
            return carry

        lax.fori_loop(0, tokens // 128, rows_step, 0)

    column = jnp.zeros(eb_ref.shape, wide_type)
    for i in range(tokens // block):
        rows = slice(i * block, (i + 1) * block)
        before = low(dot(back_low[rows, :], s_ref[...], NT) * wide(d_ref[rows, :]))
        between[rows, :] = before
        column += jnp.sum(wide(before), 0, keepdims=True)
        dmix_ref[rows, :] += dot(before, e_ref[...], NT)
        if i == 1:
            place(1)
    eb_ref[...] = column
    hold[...] = dot(a_turned[...], between[...])
    emit(wide_outs, step, hold)
    hold[...] = dot(h_ref[...], back_low[...], TN)
    emit_tall(tall_outs, step, hold)

    @pl.when(step == pl.num_programs(0) - 1)
    def _():

        def rows_step(i, carry):
            rows = pl.ds(pl.multiple_of(i * 128, 128), 128)
            grad, gain, offset = norm_rows_back(
                mixed_ref[rows, :], n_ref[0, 0:1], dmix_ref[rows, :]
            )
            dmix_ref[rows, :] = grad
            back_low[rows, :] = low(grad)
            vec_ref[3:4] += gain
            vec_ref[4:5] += offset
            vec_ref[5:6] += jnp.sum(wide(low(grad)), 0, keepdims=True)
            return carry

        lax.fori_loop(0, tokens // 128, rows_step, 0)
        hold[...] = dot(c_ref[...], back_low[...], TN)
        emit(out_outs, 0, hold)

    place(2)


def encoder_feed_back(
    grad, summed, mixed, hidden, slope, context, norms, expand, shrink, plan=None, guests=()
):
    tokens, width = mixed.shape
    total = expand.shape[1]
    cut = total // 4
    guest_outs = plan.outs() if plan else []
    outs = pl.pallas_call(
        functools.partial(encoder_feed_back_kernel, plan),
        grid=(4,),
        in_specs=[
            once(tokens, width),
            once(tokens, width),
            once(tokens, width),
            pl.BlockSpec((tokens, cut), lambda i: (0, i)),
            pl.BlockSpec((tokens, cut), lambda i: (0, i)),
            once(tokens, width),
            full(2, 2, width),
            pl.BlockSpec((width, cut), lambda i: (0, i)),
            pl.BlockSpec((cut, width), lambda i: (i, 0)),
            *(plan.in_specs() if plan else []),
        ],
        out_specs=[
            full(tokens, width),
            full(8, width),
            pl.BlockSpec((1, cut), lambda i: (0, i)),
            *grad_specs(4, width, width),
            *grad_specs(1, total, width),
            *grad_specs(1, width, width),
            *[spec for spec, _ in guest_outs],
        ],
        out_shape=[
            like((tokens, width), wide_type),
            like((8, width), wide_type),
            like((1, total), wide_type),
            *grad_shapes(4, width, width),
            *grad_shapes(1, total, width),
            *grad_shapes(1, width, width),
            *[shape for _, shape in guest_outs],
        ],
        scratch_shapes=[
            VMEM((tokens, width), low_type),
            VMEM((width, tokens), low_type),
            VMEM((tokens, cut), low_type),
            VMEM((width, width), wide_type),
            *(plan.scratch() if plan else []),
        ],
        compiler_params=host_params(plan),
        cost_estimate=cost(4e10, 5e7),
        name="encoder_feed_back",
    )(grad, summed, mixed, hidden, slope, context, norms, expand, shrink, *guests)
    main = len(outs) - len(guest_outs)
    return outs[:3], thirds(outs[3:main]), outs[main:]


def encoder_attend_back_kernel(plan, *refs):
    host_ins, host_outs = hosting(plan)
    main, guests, (dx_ref, vec_ref), outs, guest_outs, scratch, guest_scratch = split_refs(
        refs, 7, host_ins, 2, 2 if paired() else 1, host_outs, 9
    )
    dmix_ref, x_ref, qkv_ref, c_ref, stat_ref, w_ref, wo_ref = main
    dmix_low, x_turned, dc, weights, scores_back, dk, dv, dq_turned, hold = scratch
    group = pl.program_id(0)
    sums = plan.open(guests, guest_outs, guest_scratch) if plan else None

    def place(n):
        if sums:
            sums.slot(group, 3, 3, n)

    place(0)
    tokens = x_ref.shape[0]
    block = 256
    heads = GROUP // HEAD

    @pl.when(group == 0)
    def _():
        dx_ref[...] = dmix_ref[...]
        dmix_low[...] = low(dmix_ref[...])
        x_turned[...] = x_ref[...].T

    dc[...] = low(dot(dmix_low[...], wo_ref[...], NT))
    lanes_low = head_lanes(low_type)
    eighth = jnp.asarray(scale_scores, low_type)
    pick = (
        lax.broadcasted_iota(jnp.int32, (8, GROUP), 1) // HEAD
        == lax.broadcasted_iota(jnp.int32, (8, GROUP), 0)
    ).astype(wide_type)
    pick = low(pick)
    product = wide(dc[...]) * c_ref[...]
    product_high = low(product)
    product_rest = low(product - wide(product_high))
    inner = dot(pick, product_high, NT) + dot(pick, product_rest, NT)
    k_turned = qkv_ref[1].T
    dk[...] = jnp.zeros(dk.shape, wide_type)
    dv[...] = jnp.zeros(dv.shape, wide_type)
    for i in range(tokens // block):
        rows = slice(i * block, (i + 1) * block)
        q = qkv_ref[0, rows, :] * eighth
        q_heads = jnp.concatenate([q * lanes_low[h] for h in range(heads)], 0)
        dc_heads = jnp.concatenate([dc[rows, :] * lanes_low[h] for h in range(heads)], 0)
        for h in range(heads):
            part = slice(h * block, (h + 1) * block)
            scores = dot(qkv_ref[1], q_heads[part], NT)
            weight = jnp.exp(scores - stat_ref[0, h : h + 1, rows])
            weight_back = dot(qkv_ref[2], dc_heads[part], NT)
            weights[:, part] = low(weight)
            back = low(weight * (weight_back - inner[h : h + 1, rows]))
            scores_back[:, part] = back
            dq_turned[h * HEAD : (h + 1) * HEAD, rows] = dot(
                k_turned[h * HEAD : (h + 1) * HEAD], back
            )
        dv[...] += dot(weights[...], dc_heads)
        dk[...] += dot(scores_back[...], q_heads)
        if i == 1:
            place(1)
    dq = low(dq_turned[...].T * scale_scores)
    dk_low, dv_low = low(dk[...]), low(dv[...])
    vec_ref[...] = jnp.zeros(vec_ref.shape, wide_type)
    vec_ref[0:1] = jnp.sum(wide(dq), 0, keepdims=True)
    vec_ref[1:2] = jnp.sum(wide(dv_low), 0, keepdims=True)
    dx_ref[...] += (
        dot(dq, w_ref[0], NT) + dot(dk_low, w_ref[1], NT) + dot(dv_low, w_ref[2], NT)
    )
    for part, grad in enumerate((dq, dk_low, dv_low)):
        hold[...] = dot(x_turned[...], grad)
        emit(outs, part, hold)
    place(2)


def encoder_attend_back(
    dmix, x, qkv, context, stats, inward, outward, plan=None, guests=()
):
    tokens, width = x.shape
    groups = width // GROUP
    specs = grad_specs(3, width, GROUP, lambda g: (0, 0, g))
    guest_outs = plan.outs() if plan else []
    outs = pl.pallas_call(
        functools.partial(encoder_attend_back_kernel, plan),
        grid=(groups,),
        in_specs=[
            once(tokens, width),
            once(tokens, width),
            pl.BlockSpec((3, tokens, GROUP), lambda g: (0, 0, g)),
            pl.BlockSpec((tokens, GROUP), lambda g: (0, g)),
            pl.BlockSpec((1, 8, tokens), lambda g: (g, 0, 0)),
            pl.BlockSpec((3, width, GROUP), lambda g: (0, 0, g)),
            pl.BlockSpec((GROUP, width), lambda g: (g, 0)),
            *(plan.in_specs() if plan else []),
        ],
        out_specs=[
            full(tokens, width),
            pl.BlockSpec((8, GROUP), lambda g: (0, g)),
            *specs,
            *[spec for spec, _ in guest_outs],
        ],
        out_shape=[
            like((tokens, width), wide_type),
            like((8, width), wide_type),
            *grad_shapes(3, width, width),
            *[shape for _, shape in guest_outs],
        ],
        scratch_shapes=[
            VMEM((tokens, width), low_type),
            VMEM((width, tokens), low_type),
            VMEM((tokens, GROUP), low_type),
            VMEM((tokens, 4 * 256), low_type),
            VMEM((tokens, 4 * 256), low_type),
            VMEM((tokens, GROUP), wide_type),
            VMEM((tokens, GROUP), wide_type),
            VMEM((GROUP, tokens), wide_type),
            VMEM((width, GROUP), wide_type),
            *(plan.scratch() if plan else []),
        ],
        compiler_params=host_params(plan),
        cost_estimate=cost(5e10, 4e7, 1.3e7),
        name="encoder_attend_back",
    )(dmix, x, qkv, context, stats, inward, outward, *guests)
    main = len(outs) - len(guest_outs)
    return outs[:2], outs[2:main], outs[main:]


def mask_kernel(slots_ref, across_ref, down_ref):
    count, width = slots_ref.shape
    words = down_ref.shape[0] // 32
    block = 32
    row = lax.broadcasted_iota(jnp.int32, (32, width), 0)
    for start in range(0, words, block):

        def step(i, totals):
            piece = slots_ref[pl.ds(pl.multiple_of(i * 8, 8), 8), :]
            word = lax.shift_right_logical(piece, 5)
            bit = jnp.left_shift(jnp.int32(1), piece & 31)
            return tuple(
                total | jnp.where(word == start + w, bit, 0) for w, total in enumerate(totals)
            )

        zero = jnp.zeros((8, width), jnp.int32)
        totals = lax.fori_loop(0, count // 8, step, (zero,) * block)
        for w, total in enumerate(totals):
            joined = total[0:1]
            for k in range(1, 8):
                joined = joined | total[k : k + 1]
            bits = lax.shift_right_logical(jnp.broadcast_to(joined, (32, width)), row) & 1
            at = (start + w) * 32
            down_ref[at : at + 32, :] = (wide(bits) - 1.0) * 1e30
    across_ref[...] = down_ref[...].T


def slot_mask(slots, pool):
    queries = slots.shape[0]
    return pl.pallas_call(
        mask_kernel,
        out_shape=[like((queries, pool), wide_type), like((pool, queries), wide_type)],
        in_specs=[pl.BlockSpec(memory_space=VMEM)],
        out_specs=[pl.BlockSpec(memory_space=VMEM)] * 2,
        compiler_params=params(24),
        cost_estimate=cost(1e10, 1e6),
        name="slot_mask",
    )(slots.T)


def pick_kernel(table_ref, states_ref, out_ref):
    spot = lax.broadcasted_iota(jnp.int32, (table_ref.shape[0], states_ref.shape[0]), 1)
    chosen = low((spot == table_ref[...]).astype(wide_type))
    out_ref[...] = low(dot(chosen, states_ref[...]))


def pick_rows(table, states):
    tokens, width = states.shape
    return pl.pallas_call(
        pick_kernel,
        grid=(table.size // 256,),
        in_specs=[pl.BlockSpec((256, 1), lambda i: (i, 0)), full(tokens, width)],
        out_specs=pl.BlockSpec((256, width), lambda i: (i, 0)),
        out_shape=like((table.size, width), low_type),
        compiler_params=params(24),
        cost_estimate=cost(4e9, 5e6),
        name="pick_rows",
    )(table.reshape(-1, 1), states)


def spread_kernel(table_ref, rows_ref, out_ref, total):
    step = pl.program_id(0)
    spot = lax.broadcasted_iota(jnp.int32, (out_ref.shape[0], table_ref.shape[1]), 0)
    chosen = low((spot == table_ref[...]).astype(wide_type))
    part = dot(chosen, rows_ref[...])

    @pl.when(step == 0)
    def _():
        total[...] = part

    @pl.when(step != 0)
    def _():
        total[...] += part

    @pl.when(step == pl.num_programs(0) - 1)
    def _():
        out_ref[...] = low(total[...])


def spread_rows(table, rows, tokens):
    width = rows.shape[1]
    return pl.pallas_call(
        spread_kernel,
        grid=(table.size // 512,),
        in_specs=[
            pl.BlockSpec((1, 512), lambda i: (0, i)),
            pl.BlockSpec((512, width), lambda i: (i, 0)),
        ],
        out_specs=full(tokens, width),
        out_shape=like((tokens, width), low_type),
        scratch_shapes=[VMEM((tokens, width), wide_type)],
        compiler_params=params(24),
        cost_estimate=cost(4e9, 5e6),
        name="spread_rows",
    )(table.reshape(1, -1), rows)


def by_head(value, lanes):
    return jnp.concatenate([value * lane for lane in lanes], 0)


def own_lanes(stacked, lanes):
    rows = stacked.shape[0] // len(lanes)
    return sum(stacked[h * rows : (h + 1) * rows] * lane for h, lane in enumerate(lanes))


def softmax_rows(scores):
    top = jnp.max(scores, -1, keepdims=True)
    weights = jnp.exp(scores - top)
    return weights * (1.0 / jnp.sum(weights, -1, keepdims=True))


def self_mask(lengths_ref, size):
    row = lax.broadcasted_iota(jnp.int32, (size, size), 0)
    column = lax.broadcasted_iota(jnp.int32, (size, size), 1)
    row_part, column_part = jnp.zeros_like(row), jnp.zeros_like(row)
    end = jnp.int32(0)
    for n in range(lengths_ref.shape[0] - 1):
        end = end + lengths_ref[n]
        row_part += (row >= end).astype(jnp.int32)
        column_part += (column >= end).astype(jnp.int32)
    allowed = (row_part == column_part) & (column <= row)
    added = jnp.where(allowed, 0.0, -1e30)
    return jnp.concatenate([added] * (GROUP // HEAD), 0)


def groups_of(width):
    return [slice(g, g + GROUP) for g in range(0, width, GROUP)]


def self_kernel(
    lengths_ref, y_ref, w_ref, wo_ref, b_ref, n_ref, cw_ref, qkv_ref, c_ref, mixed_ref, cq_ref
):
    y = y_ref[...]
    lanes_low, lanes = head_lanes(low_type), head_lanes(wide_type)
    mask = self_mask(lengths_ref, y.shape[0])
    qkv_ref[0] = low(dot(y, w_ref[0]) + b_ref[0:1])
    qkv_ref[1] = low(dot(y, w_ref[1]))
    qkv_ref[2] = low(dot(y, w_ref[2]) + b_ref[1:2])
    for part in groups_of(y.shape[1]):
        q = qkv_ref[0, :, part] * jnp.asarray(scale_scores, low_type)
        scores = dot(by_head(q, lanes_low), qkv_ref[1, :, part], NT) + mask
        weights = low(softmax_rows(scores))
        c_ref[:, part] = low(own_lanes(dot(weights, qkv_ref[2, :, part]), lanes))
    mixed = wide(y) + (dot(c_ref[...], wo_ref[...]) + b_ref[2:3])
    mixed_ref[...] = mixed
    first = low(norm_rows(mixed, n_ref[0, 0:1], n_ref[0, 1:2]))
    cq_ref[...] = low(dot(first, cw_ref[0]) + b_ref[3:4])


def self_forward(lengths, y, inward, outward, biases, norms, cross_inward):
    rows, width = y.shape
    return pl.pallas_call(
        self_kernel,
        grid=(1,),
        in_specs=[
            pl.BlockSpec(memory_space=pltpu.SMEM),
            full(rows, width),
            full(3, width, width),
            full(width, width),
            full(6, width),
            full(3, 2, width),
            full(1, width, width),
        ],
        out_specs=[
            full(3, rows, width),
            full(rows, width),
            full(rows, width),
            full(rows, width),
        ],
        out_shape=[
            like((3, rows, width), low_type),
            like((rows, width), low_type),
            like((rows, width), wide_type),
            like((rows, width), low_type),
        ],
        compiler_params=params(40),
        cost_estimate=cost(2e10, 7e6),
        name="self_forward",
    )(lengths, y, inward, outward, biases, norms, cross_inward)


def cross_kernel(pooled_ref, q_ref, mask_ref, w_ref, bg_ref, kv_ref, c_ref, stat_ref, scores, weights):
    rows = q_ref.shape[0]
    heads = GROUP // HEAD
    lanes_low, lanes = head_lanes(low_type), head_lanes(wide_type)
    kv_ref[0] = low(dot(pooled_ref[...], w_ref[1]))
    kv_ref[1] = low(dot(pooled_ref[...], w_ref[2]) + bg_ref[4:5])
    q = q_ref[...] * jnp.asarray(scale_scores, low_type)
    scores[...] = dot(by_head(q, lanes_low), kv_ref[0], NT)
    stats, scales = [], []
    for h in range(heads):
        part = slice(h * rows, (h + 1) * rows)
        masked = scores[part, :] + mask_ref[...]
        top = jnp.max(masked, -1, keepdims=True)
        weight = jnp.exp(masked - top)
        total = jnp.sum(weight, -1, keepdims=True)
        weights[part, :] = low(weight)
        stats.append(top + jnp.log(total))
        scales.append(lanes[h] * (1.0 / total))
    mixed = dot(weights[...], kv_ref[1])
    c_ref[...] = sum(mixed[h * rows : (h + 1) * rows] * scales[h] for h in range(heads))
    column = jnp.concatenate(stats, 0)
    stat_ref[0] = jnp.broadcast_to(column, (heads * rows, 128)).T[0:8]


def cross_forward(pooled, q, mask, inward, biases):
    slots, width = pooled.shape
    rows = q.shape[0]
    groups = width // GROUP
    stacked = rows * (GROUP // HEAD)
    return pl.pallas_call(
        cross_kernel,
        grid=(groups,),
        in_specs=[
            full(slots, width),
            pl.BlockSpec((rows, GROUP), lambda g: (0, g)),
            full(rows, slots),
            pl.BlockSpec((3, width, GROUP), lambda g: (0, 0, g)),
            pl.BlockSpec((6, GROUP), lambda g: (0, g)),
        ],
        out_specs=[
            pl.BlockSpec((2, slots, GROUP), lambda g: (0, 0, g)),
            pl.BlockSpec((rows, GROUP), lambda g: (0, g)),
            pl.BlockSpec((1, 8, stacked), lambda g: (g, 0, 0)),
        ],
        out_shape=[
            like((2, slots, width), low_type),
            like((rows, width), wide_type),
            like((groups, 8, stacked), wide_type),
        ],
        scratch_shapes=[VMEM((stacked, slots), wide_type), VMEM((stacked, slots), low_type)],
        compiler_params=params(),
        cost_estimate=cost(2e10, 1.2e7, 3e6),
        name="cross_forward",
    )(pooled, q, mask, inward, biases)


def middle_kernel(
    mixed_ref, c_ref, co_ref, b_ref, n_ref, e_ref, eb_ref, s_ref, sb_ref, grad_ref, *rest
):
    out_ref, joined_back_ref, dc_ref, vec_ref, deb_ref = rest[:5]
    hidden, slope, between, hold = rest[-4:]
    feed_ref, out_outs = rest[5], rest[6:-4]
    parts = feed_ref.shape[0]
    width = mixed_ref.shape[1]
    blocks = [slice(i * width, (i + 1) * width) for i in range(e_ref.shape[1] // width)]
    first = norm_rows(mixed_ref[...], n_ref[0, 0:1], n_ref[0, 1:2])
    context = low(c_ref[...])
    joined = first + (dot(context, co_ref[...]) + b_ref[5:6])
    second = norm_rows(joined, n_ref[1, 0:1], n_ref[1, 1:2])
    second_low = low(second)
    total = jnp.zeros(joined.shape, wide_type)
    for part in blocks:
        value, rate = gelu_parts(dot(second_low, e_ref[:, part]) + eb_ref[:, part])
        hidden[:, part] = low(value)
        slope[:, part] = rate
        total += dot(hidden[:, part], s_ref[part, :])
    summed = second + (total + sb_ref[...])
    out_ref[...] = low(norm_rows(summed, n_ref[2, 0:1], n_ref[2, 1:2]))
    summed_back, gain, offset = norm_rows_back(summed, n_ref[2, 0:1], wide(grad_ref[...]))
    summed_low = low(summed_back)
    vec_ref[...] = jnp.zeros(vec_ref.shape, wide_type)
    vec_ref[0:1] = gain
    vec_ref[1:2] = offset
    vec_ref[2:3] = jnp.sum(wide(summed_low), 0, keepdims=True)
    second_back = summed_back
    for part in blocks:
        before = low(dot(summed_low, s_ref[part, :], NT) * slope[:, part])
        between[:, part] = before
        deb_ref[:, part] = jnp.sum(wide(before), 0, keepdims=True)
        second_back += dot(before, e_ref[:, part], NT)
    joined_back, gain, offset = norm_rows_back(joined, n_ref[1, 0:1], second_back)
    joined_low = low(joined_back)
    joined_back_ref[...] = joined_back
    vec_ref[3:4] = gain
    vec_ref[4:5] = offset
    vec_ref[5:6] = jnp.sum(wide(joined_low), 0, keepdims=True)
    dc_ref[...] = low(dot(joined_low, co_ref[...], NT))
    for i, part in enumerate(blocks):
        rows = width // parts
        grad = low(dot(second_low, between[:, part], TN))
        for n in range(parts):
            feed_ref[n, i * rows : (i + 1) * rows, :] = grad[n * rows : (n + 1) * rows]
        grad = low(dot(hidden[:, part], summed_low, TN))
        rows, first = 4 * rows, i * parts // 4
        for n in range(parts // 4):
            feed_ref[first + n, rows:, :] = grad[n * rows : (n + 1) * rows]
    hold[...] = dot(context, joined_low, TN)
    emit(out_outs, 0, hold)


def middle(mixed, context, outward, biases, norms, expand, expand_bias, shrink, shrink_bias, grad):
    rows, width = mixed.shape
    total = expand.shape[1]
    parts = lax.axis_size("dp")
    ins = (
        mixed,
        context,
        outward,
        biases,
        norms,
        expand,
        expand_bias[None],
        shrink,
        shrink_bias[None],
        grad,
    )
    outs = pl.pallas_call(
        middle_kernel,
        grid=(1,),
        in_specs=[full(*value.shape) for value in ins],
        out_specs=[
            full(rows, width),
            full(rows, width),
            full(rows, width),
            full(8, width),
            full(1, total),
            full(parts, 2 * total // parts, width),
            *grad_specs(1, width, width),
        ],
        out_shape=[
            like((rows, width), low_type),
            like((rows, width), wide_type),
            like((rows, width), low_type),
            like((8, width), wide_type),
            like((1, total), wide_type),
            like((parts, 2 * total // parts, width), low_type),
            *grad_shapes(1, width, width),
        ],
        scratch_shapes=[
            VMEM((rows, total), low_type),
            VMEM((rows, total), wide_type),
            VMEM((rows, total), low_type),
            VMEM((width, width), wide_type),
        ],
        compiler_params=params(),
        cost_estimate=cost(2e10, 2.2e7),
        name="middle",
    )(*ins)
    return outs[:5], outs[5], outs[6:]


def cross_back_kernel(
    kv_ref, q_ref, c_ref, dc_ref, stat_ref, mask_ref, w_ref, dkv_ref, dq_ref, vec_ref, dpool_ref,
    total, weights, scores_back
):
    group = pl.program_id(0)
    rows = q_ref.shape[0]
    heads = GROUP // HEAD
    lanes_low, lanes = head_lanes(low_type), head_lanes(wide_type)
    q_heads = by_head(q_ref[...] * jnp.asarray(scale_scores, low_type), lanes_low)
    dc_heads = by_head(dc_ref[...], lanes_low)
    product = wide(dc_heads) * jnp.concatenate([c_ref[...]] * heads, 0)
    column = jnp.sum(product, -1, keepdims=True)
    inner = jnp.broadcast_to(column, (heads * rows, 128)).T[0:1]
    stat = stat_ref[0, 0:1]
    for h in range(heads):
        part = slice(h * rows, (h + 1) * rows)
        weight = jnp.exp(dot(kv_ref[0], q_heads[part], NT) + mask_ref[...] - stat[:, part])
        weight_back = dot(kv_ref[1], dc_heads[part], NT)
        weights[:, part] = low(weight)
        scores_back[:, part] = low(weight * (weight_back - inner[:, part]))
    dk = low(dot(scores_back[...], q_heads))
    dv = low(dot(weights[...], dc_heads))
    dkv_ref[0] = dk
    dkv_ref[1] = dv
    dq = low(own_lanes(dot(scores_back[...], kv_ref[0], TN), lanes) * scale_scores)
    dq_ref[...] = dq
    vec_ref[...] = jnp.zeros(vec_ref.shape, wide_type)
    vec_ref[0:1] = jnp.sum(wide(dq), 0, keepdims=True)
    vec_ref[1:2] = jnp.sum(wide(dv), 0, keepdims=True)
    part = dot(dk, w_ref[1], NT) + dot(dv, w_ref[2], NT)

    @pl.when(group == 0)
    def _():
        total[...] = part

    @pl.when(group != 0)
    def _():
        total[...] += part

    @pl.when(group == pl.num_programs(0) - 1)
    def _():
        dpool_ref[...] = low(total[...])


def cross_back(kv, q, context, dc, stats, mask, inward):
    slots, width = kv.shape[1:]
    rows = q.shape[0]
    groups = width // GROUP
    stacked = rows * (GROUP // HEAD)
    column = pl.BlockSpec((rows, GROUP), lambda g: (0, g))
    return pl.pallas_call(
        cross_back_kernel,
        grid=(groups,),
        in_specs=[
            pl.BlockSpec((2, slots, GROUP), lambda g: (0, 0, g)),
            column,
            column,
            column,
            pl.BlockSpec((1, 8, stacked), lambda g: (g, 0, 0)),
            full(slots, rows),
            pl.BlockSpec((3, width, GROUP), lambda g: (0, 0, g)),
        ],
        out_specs=[
            pl.BlockSpec((2, slots, GROUP), lambda g: (0, 0, g)),
            column,
            pl.BlockSpec((8, GROUP), lambda g: (0, g)),
            full(slots, width),
        ],
        out_shape=[
            like((2, slots, width), low_type),
            like((rows, width), low_type),
            like((8, width), wide_type),
            like((slots, width), low_type),
        ],
        scratch_shapes=[
            VMEM((slots, width), wide_type),
            VMEM((slots, stacked), low_type),
            VMEM((slots, stacked), low_type),
        ],
        compiler_params=params(),
        cost_estimate=cost(3e10, 2.2e7, 3e6),
        name="cross_back",
    )(kv, q, context, dc, stats, mask, inward)


def cross_grads_kernel(pooled_ref, dkv_ref, mixed_ref, dq_ref, n_ref, *rest):
    outs, (turned, hold) = rest[:-2], rest[-2:]

    @pl.when(pl.program_id(0) == 0)
    def _():
        turned[...] = pooled_ref[...].T

    first = low(norm_rows(mixed_ref[...], n_ref[0, 0:1], n_ref[0, 1:2]))
    hold[...] = dot(first, dq_ref[...], TN)
    emit(outs, 0, hold)
    hold[...] = dot(turned[...], dkv_ref[0])
    emit(outs, 1, hold)
    hold[...] = dot(turned[...], dkv_ref[1])
    emit(outs, 2, hold)


def cross_grads(pooled, dkv, mixed, dq, norms):
    slots, width = pooled.shape
    rows = mixed.shape[0]
    return pl.pallas_call(
        cross_grads_kernel,
        grid=(width // GROUP,),
        in_specs=[
            full(slots, width),
            pl.BlockSpec((2, slots, GROUP), lambda g: (0, 0, g)),
            full(rows, width),
            pl.BlockSpec((rows, GROUP), lambda g: (0, g)),
            full(3, 2, width),
        ],
        out_specs=grad_specs(3, width, GROUP, lambda g: (0, 0, g)),
        out_shape=grad_shapes(3, width, width),
        scratch_shapes=[VMEM((width, slots), low_type), VMEM((width, GROUP), wide_type)],
        compiler_params=params(48),
        cost_estimate=cost(1e10, 1.5e7),
        name="cross_grads",
    )(pooled, dkv, mixed, dq, norms)


def self_back_kernel(
    lengths_ref, y_ref, mixed_ref, jb_ref, cdq_ref, qkv_ref, c_ref, w_ref, wo_ref, cw_ref, n_ref,
    dy_ref, vec_ref, *rest
):
    outs, (dqkv, hold) = rest[:-2], rest[-2:]
    width = y_ref.shape[1]
    y = y_ref[...]
    lanes_low, lanes = head_lanes(low_type), head_lanes(wide_type)
    mask = self_mask(lengths_ref, y.shape[0])
    first_back = jb_ref[...] + dot(cdq_ref[...], cw_ref[0], NT)
    mixed_back, gain, offset = norm_rows_back(mixed_ref[...], n_ref[0, 0:1], first_back)
    mixed_low = low(mixed_back)
    vec_ref[...] = jnp.zeros(vec_ref.shape, wide_type)
    vec_ref[0:1] = gain
    vec_ref[1:2] = offset
    vec_ref[2:3] = jnp.sum(wide(mixed_low), 0, keepdims=True)
    dc = low(dot(mixed_low, wo_ref[...], NT))
    for part in groups_of(width):
        q_heads = by_head(qkv_ref[0, :, part] * jnp.asarray(scale_scores, low_type), lanes_low)
        dc_heads = by_head(dc[:, part], lanes_low)
        weights = softmax_rows(dot(q_heads, qkv_ref[1, :, part], NT) + mask)
        weights_back = dot(dc_heads, qkv_ref[2, :, part], NT)
        inner = jnp.sum(weights * weights_back, -1, keepdims=True)
        scores_back = low(weights * (weights_back - inner))
        dq = own_lanes(dot(scores_back, qkv_ref[1, :, part]), lanes) * scale_scores
        dqkv[0, :, part] = low(dq)
        dqkv[1, :, part] = low(dot(scores_back, q_heads, TN))
        dqkv[2, :, part] = low(dot(low(weights), dc_heads, TN))
    vec_ref[3:4] = jnp.sum(wide(dqkv[0]), 0, keepdims=True)
    vec_ref[4:5] = jnp.sum(wide(dqkv[2]), 0, keepdims=True)
    dy_ref[...] = (
        mixed_back
        + dot(dqkv[0], w_ref[0], NT)
        + (dot(dqkv[1], w_ref[1], NT) + dot(dqkv[2], w_ref[2], NT))
    )
    for part in range(3):
        hold[...] = dot(y, dqkv[part], TN)
        emit(outs, part, hold)
    hold[...] = dot(c_ref[...], mixed_low, TN)
    emit(outs, 3, hold)


def self_back(lengths, y, mixed, joined_back, dq, qkv, context, inward, outward, cross_inward, norms):
    rows, width = y.shape
    ins = (y, mixed, joined_back, dq, qkv, context, inward, outward)
    outs = pl.pallas_call(
        self_back_kernel,
        grid=(1,),
        in_specs=[
            pl.BlockSpec(memory_space=pltpu.SMEM),
            *[full(*value.shape) for value in ins],
            full(1, width, width),
            full(3, 2, width),
        ],
        out_specs=[full(rows, width), full(8, width), *grad_specs(4, width, width)],
        out_shape=[
            like((rows, width), wide_type),
            like((8, width), wide_type),
            *grad_shapes(4, width, width),
        ],
        scratch_shapes=[VMEM((3, rows, width), low_type), VMEM((width, width), wide_type)],
        compiler_params=params(48),
        cost_estimate=cost(2e10, 1.5e7),
        name="self_back",
    )(lengths, *ins, cross_inward, norms)
    return outs[:2], outs[2:]


CUT = 192
HALF = CUT // 2
QUARTER = CUT // 4
VEC_ROWS = 32
MESH = pl.DeviceIdType.MESH


def shifted(value, axis, by):
    length = lax.axis_size(axis)
    return lax.ppermute(value, axis, [(i, (i + by) % length) for i in range(length)])


def add_rows(to, other, rows):
    def step(i, carry):
        at = pl.ds(pl.multiple_of(i * 32, 32), 32)
        to[at, :] = low(wide(to[at, :]) + wide(other[at, :]))
        return carry

    lax.fori_loop(0, rows // 32, step, 0)


def partners():
    me, section = lax.axis_index("dp"), lax.axis_index("section")
    return (
        {"dp": me + 1 - 2 * (me % 2)},
        {"dp": me + 2 - 4 * ((me // 2) % 2)},
        {"dp": me + 4 - 8 * (me // 4)},
        {"section": section + 1 - 2 * (section % 2)},
        {"section": section + 2 - 4 * (section // 2)},
    )


def greet():
    barrier = pltpu.get_barrier_semaphore()
    for partner in partners():
        pl.semaphore_signal(barrier, 1, device_id=partner, device_id_type=MESH)
    pl.semaphore_wait(barrier, 5)


def laid_out(pieces):
    out, at = [], 0
    for n, first, size in pieces:
        row = first
        while row < first + size:
            rows = min(CUT - at % CUT, first + size - row)
            out.append((n, row, rows, at // CUT, at % CUT))
            row, at = row + rows, at + rows
    return tuple(out), at // CUT


class Plan:
    def __init__(self, pieces, arrived, schedule, collective_id, onward=False, vector=False):
        self.arrays = 1 + max(piece[0] for piece in pieces)
        self.schedule, self.collective_id = schedule, collective_id
        self.sources, self.fresh = laid_out(pieces)
        self.from_kernels = tuple(arrived)
        arrived = sum(self.from_kernels)
        self.arrived, self.onward, self.vector = arrived, onward, vector
        self.late = arrived + (self.fresh if onward else 0)
        self.ins = 2 * self.arrays + len(self.from_kernels) + (1 if vector else 0)

    def in_specs(self):
        anywhere = pl.BlockSpec(memory_space=pl.ANY)
        count = self.ins - (1 if self.vector else 0)
        return [anywhere] * count + ([pl.BlockSpec(memory_space=VMEM)] if self.vector else [])

    def outs(self):
        out = []
        if not self.onward:
            out.append((pl.BlockSpec(memory_space=pl.ANY), like((self.fresh * CUT, WIDTH), low_type)))
        if self.late:
            out.append((pl.BlockSpec(memory_space=pl.ANY), like((self.late * CUT, WIDTH), low_type)))
        if self.vector:
            out.append((pl.BlockSpec(memory_space=VMEM), like((VEC_ROWS, WIDTH), wide_type)))
        return out

    def scratch(self):
        dma = pltpu.SemaphoreType.DMA
        fresh, late, arrived = self.fresh, max(self.late, 1), max(self.arrived, 1)
        most = max(fresh, late)
        count = len(self.sources)
        return [
            VMEM((fresh, 4, CUT, WIDTH), low_type),
            VMEM((fresh, 4, CUT, WIDTH), low_type),
            VMEM((fresh, 2, 2, HALF, WIDTH), low_type),
            VMEM((fresh, 2, HALF, WIDTH), low_type),
            VMEM((arrived, CUT, WIDTH if self.late else 128), low_type),
            VMEM((late, HALF, WIDTH if self.late else 128), low_type),
            VMEM((late, QUARTER, WIDTH if self.late else 128), low_type),
            VMEM((late, CUT, WIDTH if self.late else 128), low_type),
            VMEM((5, VEC_ROWS if self.vector else 8, WIDTH), wide_type),
            dma((count,)),
            dma((count,)),
            dma((count,)),
            dma((3, fresh, 3)),
            dma((3, fresh, 3)),
            dma((late, 4)),
            dma((late, 4)),
            dma((arrived,)),
            dma((2, most)),
            dma((5,)),
            dma((5,)),
        ]

    def open(self, ins, outs, scratch):
        return Sums(self, ins, outs, scratch)


class Sums:
    def __init__(self, plan, ins, outs, scratch):
        count = plan.arrays
        outs, ins = list(outs), list(ins)
        self.plan = plan
        self.keeps, self.sends = ins[:count], ins[count : 2 * count]
        ins = ins[2 * count :]
        self.arrived = [ins.pop(0) for _ in plan.from_kernels]
        self.vec_ref = ins.pop(0) if plan.vector else None
        self.shard_out = None if plan.onward else outs.pop(0)
        self.late_out = outs.pop(0) if plan.late else None
        self.vec_out = outs.pop(0) if plan.vector else None
        (
            self.own,
            self.from_core,
            self.from_one,
            self.from_two,
            self.waiting,
            self.from_three,
            self.from_four,
            self.whole,
            self.vec_in,
            self.load_sems,
            self.core_send,
            self.core_recv,
            self.send_sems,
            self.recv_sems,
            self.line_send,
            self.line_recv,
            self.arrive_sems,
            self.out_sems,
            self.vec_send,
            self.vec_recv,
        ) = scratch
        self.core, self.over_x, self.over_y, self.near, self.far = partners()
        section = lax.axis_index("section")
        side, far_side = section % 2, section // 2
        self.half_at = pl.multiple_of(side * HALF, HALF)
        self.half_other = pl.multiple_of((1 - side) * HALF, HALF)
        self.quarter_at = pl.multiple_of(side * HALF + far_side * QUARTER, QUARTER)
        self.quarter_other = pl.multiple_of(side * HALF + (1 - far_side) * QUARTER, QUARTER)

    def remote(self, source, to, send, recv, partner):
        return pltpu.make_async_remote_copy(
            src_ref=source,
            dst_ref=to,
            send_sem=send,
            recv_sem=recv,
            device_id=partner,
            device_id_type=MESH,
        )

    def load(self, s):
        n, row, rows, chunk, at = self.plan.sources[s]
        return pltpu.make_async_copy(
            self.keeps[n].at[:, pl.ds(row, rows)],
            self.own.at[chunk, :, pl.ds(at, rows)],
            self.load_sems.at[s],
        )

    def cross(self, s):
        n, row, rows, chunk, at = self.plan.sources[s]
        return self.remote(
            self.sends[n].at[:, pl.ds(row, rows)],
            self.from_core.at[chunk, :, pl.ds(at, rows)],
            self.core_send.at[s],
            self.core_recv.at[s],
            self.core,
        )

    def arrive(self, k):
        at, source = k, 0
        while at >= self.plan.from_kernels[source]:
            at, source = at - self.plan.from_kernels[source], source + 1
        return pltpu.make_async_copy(
            self.arrived[source].at[pl.ds(at * CUT, CUT)],
            self.waiting.at[k],
            self.arrive_sems.at[k],
        )

    def summed(self, k):
        if k < self.plan.arrived:
            return self.waiting.at[k]
        return self.own.at[k - self.plan.arrived, 0]

    def pairs(self, stage, c):
        own, upper, lower = self.own, pl.ds(0, HALF), pl.ds(HALF, HALF)
        if stage == 1:
            return (
                (own.at[c, 1, upper], self.from_one.at[c, 0, 0], self.over_x),
                (own.at[c, 3, upper], self.from_one.at[c, 0, 1], self.over_x),
                (own.at[c, pl.ds(2, 2), lower], self.from_one.at[c, 1], self.over_y),
            )
        return (
            (own.at[c, 2, upper], self.from_two.at[c, 0], self.over_y),
            (own.at[c, 1, lower], self.from_two.at[c, 1], self.over_x),
        )

    def copies(self, stage, c):
        return [
            self.remote(
                source, to, self.send_sems.at[stage, c, k], self.recv_sems.at[stage, c, k], partner
            )
            for k, (source, to, partner) in enumerate(self.pairs(stage, c))
        ]

    def start(self, stage, c):
        for copy in self.copies(stage, c):
            copy.start()

    def across(self, stage, k):
        half = self.summed(k).at[pl.ds(self.half_other, HALF)]
        quarter = self.summed(k).at[pl.ds(self.quarter_other, QUARTER)]
        mine = self.whole.at[k, pl.ds(self.quarter_at, QUARTER)]
        ours = self.whole.at[k, pl.ds(self.half_at, HALF)]
        source, to, partner = (
            (half, self.from_three.at[k], self.near),
            (quarter, self.from_four.at[k], self.far),
            (mine, mine, self.far),
            (ours, ours, self.near),
        )[stage - 3]
        n = stage - 3
        return self.remote(source, to, self.line_send.at[k, n], self.line_recv.at[k, n], partner)

    def line(self, stage, k):
        if stage == "go":
            self.across(3, k).start()
            return
        self.across(stage, k).wait_recv()
        if stage == 3:
            add_rows(self.summed(k).at[pl.ds(self.half_at, HALF)], self.from_three.at[k], HALF)
        elif stage == 4:
            rows = pl.ds(self.quarter_at, QUARTER)
            self.whole[k, rows, :] = low(wide(self.summed(k)[rows, :]) + wide(self.from_four[k]))
        if stage < 6:
            self.across(stage + 1, k).start()
        else:
            self.late_copy(k).start()

    def shard_copy(self, c):
        return pltpu.make_async_copy(
            self.own.at[c, 0], self.shard_out.at[pl.ds(c * CUT, CUT)], self.out_sems.at[0, c]
        )

    def late_copy(self, k):
        return pltpu.make_async_copy(
            self.whole.at[k], self.late_out.at[pl.ds(k * CUT, CUT)], self.out_sems.at[1, k]
        )

    def vec_copy(self, stage):
        return self.remote(
            self.vec_out,
            self.vec_in.at[stage],
            self.vec_send.at[stage],
            self.vec_recv.at[stage],
            partners()[stage],
        )

    def vec_step(self, stage):
        if stage:
            self.vec_copy(stage - 1).wait()
            self.vec_out[...] += self.vec_in[stage - 1]
        else:
            self.vec_out[...] = self.vec_ref[...]
        if stage < 5:
            self.vec_copy(stage).start()

    def begin(self):
        greet()
        for s in range(len(self.plan.sources)):
            self.cross(s).start()
            self.load(s).start()
        for k in range(self.plan.arrived):
            self.arrive(k).start()

    def step(self, stage, c):
        if stage == "vec":
            self.vec_step(c)
            return
        if stage == "go":
            self.arrive(c).wait()
            self.line("go", c)
            return
        if stage > 2:
            self.line(stage, c)
            return
        if stage == 0:
            for s, source in enumerate(self.plan.sources):
                if source[3] == c:
                    self.load(s).wait()
                    self.cross(s).wait_recv()
            for at in range(4):
                add_rows(self.own.at[c, at], self.from_core.at[c, at], CUT)
            self.start(1, c)
            return
        for copy in self.copies(stage, c):
            copy.wait_recv()
        upper, lower = pl.ds(0, HALF), pl.ds(HALF, HALF)
        if stage == 1:
            for k in range(2):
                add_rows(self.own.at[c, 2 * k, upper], self.from_one.at[c, 0, k], HALF)
                add_rows(self.own.at[c, k, lower], self.from_one.at[c, 1, k], HALF)
            self.start(2, c)
        else:
            add_rows(self.own.at[c, 0, upper], self.from_two.at[c, 0], HALF)
            add_rows(self.own.at[c, 0, lower], self.from_two.at[c, 1], HALF)
            if self.plan.onward:
                self.line("go", self.plan.arrived + c)
            else:
                self.shard_copy(c).start()

    def finish(self):
        for s in range(len(self.plan.sources)):
            self.cross(s).wait_send()
        for c in range(self.plan.fresh):
            for stage in (1, 2):
                for copy in self.copies(stage, c):
                    copy.wait_send()
            if not self.plan.onward:
                self.shard_copy(c).wait()
        for k in range(self.plan.late):
            for stage in (3, 4, 5, 6):
                self.across(stage, k).wait_send()
            self.late_copy(k).wait()

    def slot(self, grid_step, steps, slots, slot):
        for n in range(steps):
            wanted = self.plan.schedule.get(n * slots + slot, ())
            if not wanted:
                continue

            @pl.when(grid_step == n)
            def _(wanted=wanted):
                for stage, c in wanted:
                    if stage == "begin":
                        self.begin()
                    elif stage == "finish":
                        self.finish()
                    else:
                        self.step(stage, c)


def last_sums_kernel(plan, *refs):
    ins, rest = refs[: plan.ins], refs[plan.ins :]
    count = len(plan.outs())
    sums = plan.open(ins, rest[:count], rest[count:])
    sums.begin()
    for stage, c in plan.schedule:
        sums.step(stage, c)
    sums.finish()


def last_sums(plan, pairs, arrived, vector):
    outs = plan.outs()
    return pl.pallas_call(
        functools.partial(last_sums_kernel, plan),
        in_specs=plan.in_specs(),
        out_specs=[spec for spec, _ in outs],
        out_shape=[shape for _, shape in outs],
        scratch_shapes=plan.scratch(),
        compiler_params=params(60, collective_id=plan.collective_id, has_side_effects=True),
        cost_estimate=cost(1e8, 1e8),
        name="last_sums",
    )(*[p[0] for p in pairs], *[p[1] for p in pairs], *arrived, vector)


def landing_order(fresh, arrived, onward, vector=False, first=0.0):
    free = {}
    events, steps = [], []

    def send(time, takes, *links):
        begin = max([time] + [free.get(link, 0.0) for link in links])
        for link in links:
            free[link] = begin + takes
        return begin + takes + 1.5

    def push(time, stage, c):
        events.append((time, len(steps) + len(events), stage, c))

    for c in range(fresh):
        push(first + 4.0 + 2.2 * c, 0, c)
    for k in range(arrived):
        push(first + 3.0 + 0.3 * k, "go", k)
    if vector:
        push(first, "vec", 0)
    while events:
        event = min(events)
        events.remove(event)
        time, _, stage, c = event
        steps.append((time, stage, c))
        if stage == "vec":
            if c < 5:
                push(time + 5.0, "vec", c + 1)
        elif stage == 0:
            if free.get("xy", 0.0) > time + 2.5:
                steps.pop()
                push(free["xy"] - 2.0, 0, c)
            else:
                push(send(time, 6.6, "xy"), 1, c)
        elif stage == 1:
            push(send(time, 3.3, "xy"), 2, c)
        elif stage == 2 and not onward:
            pass
        elif stage in ("go", 2):
            push(send(time, 3.3, "out"), 3, c + (arrived if stage == 2 else 0))
        elif stage == 3:
            push(send(time, 3.3, "mid", "out"), 4, c)
        elif stage == 4:
            push(send(time, 3.3, "mid", "out"), 5, c)
        elif stage == 5:
            push(send(time, 3.3, "out"), 6, c)
    return steps


def feed_plan():
    schedule = {
        0: [("begin", 0)],
        1: [(0, 0), (0, 1), (0, 2)],
        9: [(1, 0), (1, 1), (1, 2)],
        11: [(2, 0), (2, 1), (2, 2), ("finish", 0)],
    }
    return Plan(((0, 0, 288), (1, 0, 96), (2, 0, 192)), (), schedule, 1)


def attend_plan():
    schedule = {
        0: [("begin", 0)],
        1: [(0, 0), (0, 1), (0, 2), (0, 3), (0, 4)],
        6: [(1, 0), (1, 1), (1, 2)],
        7: [(1, 3), (1, 4), (2, 0), (2, 1)],
        8: [(2, 2), (2, 3), (2, 4), ("finish", 0)],
    }
    return Plan(((0, 192, 192), (1, 0, 384), (2, 0, 384)), (), schedule, 2)


def last_plan():
    order = [step[1:] for step in landing_order(2, 5, True, True)]
    return Plan(((0, 0, 288), (1, 0, 96)), (5,), order, 3, onward=True, vector=True)


def unpack_kernel(first_ref, last_ref, vec_ref, *outs):
    (
        e_in, e_out, e_bias, e_norm, e_expand, e_expand_bias, e_shrink, e_shrink_bias,
        s_in, s_out, c_in, c_out, d_bias, d_norm, d_expand, d_expand_bias, d_shrink, d_shrink_bias,
    ) = outs
    rows = e_out.shape[0]

    def rows_of(ref, at, count=1):
        return wide(ref[at * rows : (at + count) * rows, :])

    for i in range(4):
        part = slice(i * WIDTH, (i + 1) * WIDTH)
        d_expand[:, part] = rows_of(first_ref, i)
        e_expand[:, part] = rows_of(last_ref, 2 + i)
    d_shrink[...] = rows_of(first_ref, 4, 4)
    for i in range(3):
        c_in[i] = rows_of(first_ref, 8 + i)
        e_in[i] = rows_of(last_ref, 10 + i)
    c_out[...] = rows_of(first_ref, 11)
    s_in[0] = rows_of(first_ref, 12)
    s_in[1] = rows_of(first_ref, 13)
    s_in[2] = rows_of(last_ref, 0)
    s_out[...] = rows_of(last_ref, 1)
    e_shrink[...] = rows_of(last_ref, 6, 4)
    e_out[...] = rows_of(last_ref, 13)
    me = lax.axis_index("dp")
    mine = pltpu.roll(vec_ref[...], WIDTH - me * rows, 1)
    e_bias[...] = mine[0:3, 0:rows]
    e_norm[0] = mine[3:5, 0:rows]
    e_norm[1] = mine[5:7, 0:rows]
    e_shrink_bias[...] = mine[11:12, 0:rows]
    d_bias[...] = mine[12:18, 0:rows]
    for i in range(3):
        d_norm[i] = mine[18 + 2 * i : 20 + 2 * i, 0:rows]
    d_shrink_bias[...] = mine[28:29, 0:rows]
    for at, to in ((7, e_expand_bias), (24, d_expand_bias)):
        row = jnp.zeros((1, WIDTH), wide_type)
        for i in range(4):
            row = jnp.where(me // 2 == i, vec_ref[at + i : at + i + 1, :], row)
        to[...] = jnp.where(me % 2 == 0, row[:, : WIDTH // 2], row[:, WIDTH // 2 :])


def unpack(first, last, vector):
    rows, width = WIDTH // 8, WIDTH
    square, cube = (rows, width), (3, rows, width)
    wide_one, tall_one = (rows, 4 * width), (4 * rows, width)
    shapes = [
        cube, square, (3, rows), (2, 2, rows), wide_one, (1, 4 * rows), tall_one, (1, rows),
        cube, square, cube, square, (6, rows), (3, 2, rows), wide_one, (1, 4 * rows), tall_one,
        (1, rows),
    ]
    here = pl.BlockSpec(memory_space=VMEM)
    return pl.pallas_call(
        unpack_kernel,
        in_specs=[here] * 3,
        out_specs=[here] * len(shapes),
        out_shape=[like(shape, wide_type) for shape in shapes],
        compiler_params=params(40),
        cost_estimate=cost(1e7, 1.3e7),
        name="unpack",
    )(first, last, vector)


def sum_whole(grads):
    parts = lax.axis_size("dp")
    packed = []
    for grad in grads:
        count, rows, columns = grad.shape
        cut = grad.reshape(count, parts, rows // parts, columns // WIDTH, WIDTH)
        packed.append(cut.transpose(1, 0, 3, 2, 4).reshape(parts, -1, WIDTH))
    shard = lax.psum_scatter(jnp.concatenate(packed, 1), "dp", scatter_dimension=0, tiled=True)[0]
    total = wide(lax.psum(shard, "section"))
    outs, at = [], 0
    for grad in grads:
        count, rows, columns = grad.shape
        size = grad.size // parts // WIDTH
        cut = total[at : at + size].reshape(count, columns // WIDTH, rows // parts, WIDTH)
        outs.append(cut.transpose(0, 2, 1, 3).reshape(count * rows // parts, columns))
        at += size
    return outs


def beside(shard):
    rows = shard.shape[0] // 4
    return shard.reshape(4, rows, WIDTH).transpose(1, 0, 2).reshape(rows, 4 * WIDTH)


def sum_any(grads, d_feed, vectors):
    e_in, e_out, e_expand, e_shrink, s_all, c_in, c_out = sum_whole([grad[0] for grad in grads])
    d_feed = wide(lax.psum(d_feed, "section"))
    d_expand, d_shrink = d_feed[: d_feed.shape[0] // 2], d_feed[d_feed.shape[0] // 2 :]
    flat = lax.psum(jnp.concatenate([v.reshape(-1) for v in vectors]), ("dp", "section"))
    parts, mine = lax.axis_size("dp"), lax.axis_index("dp")
    outs, at = [], 0
    for v in vectors:
        whole = flat[at : at + v.size].reshape(v.shape)
        at += v.size
        size = v.shape[-1] // parts
        outs.append(lax.dynamic_slice_in_dim(whole, mine * size, size, v.ndim - 1))
    rows = WIDTH // parts
    return (
        e_in.reshape(3, rows, WIDTH),
        e_out,
        outs[0],
        outs[1],
        beside(e_expand),
        outs[2],
        e_shrink,
        outs[3],
        s_all[: 3 * rows].reshape(3, rows, WIDTH),
        s_all[3 * rows :],
        c_in.reshape(3, rows, WIDTH),
        c_out,
        outs[4],
        outs[5],
        beside(d_expand),
        outs[6],
        d_shrink,
        outs[7],
    )


def on_device(
    encoder_input,
    decoder_input,
    cotangent,
    pool_table,
    retrieved,
    decoder_lengths,
    encoder_inward,
    encoder_outward,
    encoder_biases,
    encoder_norms,
    encoder_expand,
    encoder_expand_bias,
    encoder_shrink,
    encoder_shrink_bias,
    self_inward,
    self_outward,
    cross_inward,
    cross_outward,
    decoder_biases,
    decoder_norms,
    decoder_expand,
    decoder_expand_bias,
    decoder_shrink,
    decoder_shrink_bias,
):
    x = encoder_input[0]
    half_way = lax.axis_size("section") // 2
    queries = decoder_input.shape[1]
    topk = retrieved.shape[2]
    rows_low = shifted(jnp.concatenate([decoder_input[0], cotangent[0]], 0), "section", -half_way)
    y, grad = rows_low[:queries], rows_low[queries:]
    lengths_row = jnp.pad(decoder_lengths[0], ((0, 0), (0, topk - decoder_lengths.shape[2])))
    integers = shifted(
        jnp.concatenate([retrieved[0], pool_table[0, 0].reshape(-1, topk), lengths_row], 0),
        "section",
        -half_way,
    )
    slots = integers[:queries]
    table = integers[queries:-1].reshape(-1)
    lengths = integers[-1, : decoder_lengths.shape[2]]
    owners = pool_table.shape[2]

    qkv, context, context_low, stats, mixed = encoder_attend(
        x, encoder_inward, encoder_outward, encoder_biases
    )
    hidden, slope, summed, states = encoder_feed(
        mixed,
        encoder_norms,
        encoder_expand,
        encoder_expand_bias,
        encoder_shrink,
        encoder_shrink_bias,
    )
    picked = pick_rows(table, states).reshape(owners, -1, WIDTH)
    pooled = lax.all_to_all(picked, "dp", split_axis=0, concat_axis=0, tiled=True)
    pooled = pooled.reshape(-1, WIDTH)

    mask_across, mask_down = slot_mask(slots, pooled.shape[0])
    self_qkv, self_context, self_mixed, cross_q = self_forward(
        lengths, y, self_inward, self_outward, decoder_biases, decoder_norms, cross_inward
    )
    kv, cross_context, cross_stats = cross_forward(
        pooled, cross_q, mask_across, cross_inward, decoder_biases
    )
    (out, joined_back, dc, mid_vec, mid_expand), d_feed, d_cross_out = middle(
        self_mixed,
        cross_context,
        cross_outward,
        decoder_biases,
        decoder_norms,
        decoder_expand,
        decoder_expand_bias,
        decoder_shrink,
        decoder_shrink_bias,
        grad,
    )
    d_feed = lax.psum_scatter(d_feed, "dp", scatter_dimension=0, tiled=True)[0]
    dkv, dq, cross_vec, dpool = cross_back(
        kv, cross_q, cross_context, dc, cross_stats, mask_down, cross_inward
    )
    returned = lax.all_to_all(
        dpool.reshape(owners, -1, WIDTH), "dp", split_axis=0, concat_axis=0, tiled=True
    )
    d_cross_in = cross_grads(pooled, dkv, self_mixed, dq, decoder_norms)
    (dy, self_vec), d_self = self_back(
        lengths,
        y,
        self_mixed,
        joined_back,
        dq,
        self_qkv,
        self_context,
        self_inward,
        self_outward,
        cross_inward,
        decoder_norms,
    )
    decoder_out = shifted(out, "section", half_way)
    decoder_grad = shifted(dy, "section", half_way)
    states_back = spread_rows(table, returned.reshape(-1, WIDTH), x.shape[0])

    hosts = paired()
    plan = feed_plan() if hosts else None
    guests = [pair[k] for k in range(2) for pair in (d_cross_in, d_cross_out, d_self)] if hosts else []
    (dmix, feed_vec, feed_expand), (e_expand, e_shrink, e_out), from_feed = encoder_feed_back(
        states_back,
        summed,
        mixed,
        hidden,
        slope,
        context_low,
        encoder_norms,
        encoder_expand,
        encoder_shrink,
        plan,
        guests,
    )
    plan = attend_plan() if hosts else None
    if hosts:
        guests = [pair[k] for k in range(2) for pair in (d_self, e_expand, e_shrink)]
        early = jnp.concatenate([d_feed, from_feed[0]], 0)
        early, dmix = lax.optimization_barrier((early, dmix))
        early = lax.psum(early, "section")
    (dx, attend_vec), e_in, from_attend = encoder_attend_back(
        dmix, x, qkv, context, stats, encoder_inward, encoder_outward, plan, guests
    )
    vectors = [
        jnp.concatenate([attend_vec[0:2], feed_vec[5:6]], 0),
        jnp.stack([feed_vec[3:5], feed_vec[0:2]]),
        feed_expand[0],
        feed_vec[2],
        jnp.concatenate([self_vec[3:5], self_vec[2:3], cross_vec[0:2], mid_vec[5:6]], 0),
        jnp.stack([self_vec[0:2], mid_vec[3:5], mid_vec[0:2]]),
        mid_expand[0],
        mid_vec[2],
    ]
    if hosts:
        flat = jnp.concatenate([v.reshape(-1) for v in vectors])
        flat = jnp.pad(flat, (0, VEC_ROWS * WIDTH - flat.size)).reshape(VEC_ROWS, WIDTH)
        last, vector = last_sums(last_plan(), (e_in, e_out), from_attend, flat)
        results = unpack(early, last, vector)
        results = [r[0] if n in (5, 7, 15, 17) else r for n, r in enumerate(results)]
    else:
        results = sum_any(
            [e_in, e_out, e_expand, e_shrink, d_self, d_cross_in, d_cross_out], d_feed, vectors
        )
    return (decoder_out[None], dx[None], decoder_grad[None], *results)


def solution(mesh):
    in_specs = (
        P("section", "dp", None),
        P("section", "dp", None),
        P("section", "dp", None),
        P("section", "dp", None, None),
        P("section", "dp", None),
        P("section", "dp", None),
        P(),
        P(),
        P(),
        P(),
        P(),
        P(),
        P(),
        P(),
        P(),
        P(),
        P(),
        P(),
        P(),
        P(),
        P(),
        P(),
        P(),
        P(),
    )
    out_specs = (
        P("section", "dp", None),
        P("section", "dp", None),
        P("section", "dp", None),
        P(None, "dp", None),
        P("dp", None),
        P(None, "dp"),
        P(None, None, "dp"),
        P("dp", None),
        P("dp"),
        P("dp", None),
        P("dp"),
        P(None, "dp", None),
        P("dp", None),
        P(None, "dp", None),
        P("dp", None),
        P(None, "dp"),
        P(None, None, "dp"),
        P("dp", None),
        P("dp"),
        P("dp", None),
        P("dp"),
    )
    return jax.shard_map(
        on_device, mesh=mesh, in_specs=in_specs, out_specs=out_specs, check_vma=False
    )
```

```python
import functools

import jax
import jax.numpy as jnp
from jax import lax
from jax.experimental import pallas as pl
from jax.experimental.pallas import tpu as pltpu
from jax.sharding import PartitionSpec as P

HEAD = 64
WIDTH = 768


norm_eps = 1e-05
scale_scores = 0.125
low_type = jnp.bfloat16
wide_type = jnp.float32

NN = (((1,), (0,)), ((), ()))
NT = (((1,), (1,)), ((), ()))
TN = (((0,), (0,)), ((), ()))
GROUP = 256
VMEM = pltpu.VMEM


def dot(left, right, dims=NN):
    return lax.dot_general(left, right, dims, preferred_element_type=wide_type)


def low(value):
    return value.astype(low_type)


def wide(value):
    return value.astype(wide_type)


def head_lanes(dtype):
    lane = lax.broadcasted_iota(jnp.int32, (1, GROUP), 1) // HEAD
    return [(lane == h).astype(wide_type).astype(dtype) for h in range(GROUP // HEAD)]


def centred_of(values):
    centred = values - jnp.mean(values, -1, keepdims=True)
    spread = jnp.mean(centred * centred, -1, keepdims=True)
    return centred, lax.rsqrt(spread + norm_eps)


def norm_rows(values, gain, offset):
    centred, scale = centred_of(values)
    return centred * scale * (1.0 + gain) + offset


def norm_rows_back(values, gain, incoming):
    centred, scale = centred_of(values)
    unit = centred * scale
    inner = incoming * (1.0 + gain)
    mean_inner = jnp.mean(inner, -1, keepdims=True)
    mean_along = jnp.mean(inner * unit, -1, keepdims=True)
    return (
        scale * (inner - mean_inner - unit * mean_along),
        jnp.sum(incoming * unit, 0, keepdims=True),
        jnp.sum(incoming, 0, keepdims=True),
    )


def gelu_parts(u):
    size = jnp.abs(u) * 0.7071067811865476
    t = 1.0 / (1.0 + 0.3275911 * size)
    bell = jnp.exp(-0.5 * u * u)
    series = t * (
        0.254829592
        + t * (-0.284496736 + t * (1.421413741 + t * (-1.453152027 + t * 1.061405429)))
    )
    tail = 0.5 * series * bell
    share = jnp.where(u < 0.0, tail, 1.0 - tail)
    return u * share, share + u * (bell * 0.3989422804014327)


def params(limit=60, **rest):
    return pltpu.CompilerParams(vmem_limit_bytes=limit * 2**20, **rest)


def host_params(plan):
    if plan:
        return params(62, collective_id=plan.collective_id, has_side_effects=True)
    return params()


def cost(flops, size, exps=0):
    return pl.CostEstimate(flops=int(flops), bytes_accessed=int(size), transcendentals=int(exps))


def full(*shape):
    return pl.BlockSpec(shape, lambda *_: (0,) * len(shape))


def once(*shape):
    return pl.BlockSpec(shape, lambda *_: (0,) * len(shape), pipeline_mode=pl.Buffered(1))


def like(shape, dtype):
    return jax.ShapeDtypeStruct(shape, dtype)


def paired():
    return lax.axis_size("dp") == 8


def grad_shapes(parts, rows, columns):
    if paired():
        return [like((4, parts * rows // 8, columns), low_type)] * 2
    return [like((parts, rows, columns), low_type)]


def grad_specs(parts, rows, columns, index=None):
    if paired():
        block, count = (4, parts * rows // 8, columns), 2
    else:
        block, count = (parts, rows, columns), 1
    return [pl.BlockSpec(block, index or (lambda *_: (0, 0, 0)))] * count


def emit(outs, part, hold):
    if len(outs) == 1:
        outs[0][part] = low(hold[...])
        return
    keep, send = outs
    me = lax.axis_index("dp")
    rows = hold.shape[0] // 8
    to = pl.ds(pl.multiple_of(part * rows, rows), rows)
    for at in range(4):
        mine = pl.multiple_of((me ^ (2 * at)) * rows, rows)
        other = pl.multiple_of((me ^ (2 * at + 1)) * rows, rows)
        keep[at, to, :] = low(hold[pl.ds(mine, rows), :])
        send[at, to, :] = low(hold[pl.ds(other, rows), :])


def emit_tall(outs, block, hold):
    if len(outs) == 1:
        size = hold.shape[0]
        outs[0][0, pl.ds(pl.multiple_of(block * size, size), size), :] = low(hold[...])
        return
    keep, send = outs
    me = lax.axis_index("dp")
    rows = hold.shape[0] // 2
    at = block ^ lax.shift_right_logical(me, 1)
    core = me & 1
    keep[at, 0:rows, :] = low(hold[pl.ds(pl.multiple_of(core * rows, rows), rows), :])
    send[at, 0:rows, :] = low(hold[pl.ds(pl.multiple_of((1 - core) * rows, rows), rows), :])


def thirds(items):
    third = len(items) // 3
    return items[:third], items[third : 2 * third], items[2 * third :]


def encoder_attend_kernel(
    x_ref, w_ref, wo_ref, bg_ref, b_ref, qkv_ref, c_ref, cl_ref, stat_ref, mixed_ref, stats
):
    group = pl.program_id(0)
    tokens = x_ref.shape[0]
    block = 512
    x = x_ref[...]
    qkv_ref[0] = low(dot(x, w_ref[0]) + bg_ref[0:1])
    qkv_ref[1] = low(dot(x, w_ref[1]))
    qkv_ref[2] = low(dot(x, w_ref[2]) + bg_ref[1:2])
    lanes_low, lanes = head_lanes(low_type), head_lanes(wide_type)
    lane = lax.broadcasted_iota(jnp.int32, (1, 128), 1)

    @pl.when(group == 0)
    def _():
        mixed_ref[...] = wide(x) + b_ref[2:3]

    def rows_step(i, carry):
        rows = pl.ds(pl.multiple_of(i * block, block), block)
        q = qkv_ref[0, rows, :] * jnp.asarray(scale_scores, low_type)
        context = jnp.zeros((block, GROUP), wide_type)
        stat = jnp.zeros((block, 128), wide_type)
        for h in range(GROUP // HEAD):
            scores = dot(q * lanes_low[h], qkv_ref[1], NT)
            top = jnp.max(scores, -1, keepdims=True)
            weights = jnp.exp(scores - top)
            total = jnp.sum(weights, -1, keepdims=True)
            context += dot(low(weights), qkv_ref[2]) * (lanes[h] * (1.0 / total))
            stat = jnp.where(lane == h, top + jnp.log(total), stat)
        c_ref[rows, :] = context
        cl_ref[rows, :] = low(context)
        stats[rows, :] = stat
        mixed_ref[rows, :] += dot(low(context), wo_ref[...])
        return carry

    lax.fori_loop(0, tokens // block, rows_step, 0)
    stat_ref[0] = stats[...].T[0:8]


def encoder_attend(x, inward, outward, biases):
    tokens, width = x.shape
    groups = width // GROUP
    return pl.pallas_call(
        encoder_attend_kernel,
        grid=(groups,),
        in_specs=[
            full(tokens, width),
            pl.BlockSpec((3, width, GROUP), lambda g: (0, 0, g)),
            pl.BlockSpec((GROUP, width), lambda g: (g, 0)),
            pl.BlockSpec((3, GROUP), lambda g: (0, g)),
            full(3, width),
        ],
        out_specs=[
            pl.BlockSpec((3, tokens, GROUP), lambda g: (0, 0, g)),
            pl.BlockSpec((tokens, GROUP), lambda g: (0, g)),
            pl.BlockSpec((tokens, GROUP), lambda g: (0, g)),
            pl.BlockSpec((1, 8, tokens), lambda g: (g, 0, 0)),
            full(tokens, width),
        ],
        out_shape=[
            like((3, tokens, width), low_type),
            like((tokens, width), wide_type),
            like((tokens, width), low_type),
            like((groups, 8, tokens), wide_type),
            like((tokens, width), wide_type),
        ],
        scratch_shapes=[VMEM((tokens, 128), wide_type)],
        compiler_params=params(),
        cost_estimate=cost(3e10, 2e7, 1.3e7),
        name="encoder_attend",
    )(x, inward, outward, biases, biases)


def encoder_feed_kernel(
    mixed_ref, n_ref, e_ref, eb_ref, s_ref, sb_ref, h_ref, d_ref, sum_ref, out_ref, a_low
):
    step = pl.program_id(0)
    tokens = mixed_ref.shape[0]
    block = 256

    @pl.when(step == 0)
    def _():
        def rows_step(i, carry):
            rows = pl.ds(pl.multiple_of(i * 256, 256), 256)
            first = norm_rows(mixed_ref[rows, :], n_ref[0, 0:1], n_ref[0, 1:2])
            a_low[rows, :] = low(first)
            sum_ref[rows, :] = first + sb_ref[...]
            return carry

        lax.fori_loop(0, tokens // 256, rows_step, 0)

    for i in range(tokens // block):
        rows = slice(i * block, (i + 1) * block)
        hidden, slope = gelu_parts(dot(a_low[rows, :], e_ref[...]) + eb_ref[...])
        h_ref[rows, :] = low(hidden)
        d_ref[rows, :] = low(slope)
        sum_ref[rows, :] += dot(low(hidden), s_ref[...])

    @pl.when(step == pl.num_programs(0) - 1)
    def _():
        def rows_step(i, carry):
            rows = pl.ds(pl.multiple_of(i * 256, 256), 256)
            out_ref[rows, :] = low(norm_rows(sum_ref[rows, :], n_ref[1, 0:1], n_ref[1, 1:2]))
            return carry

        lax.fori_loop(0, tokens // 256, rows_step, 0)


def encoder_feed(mixed, norms, expand, expand_bias, shrink, shrink_bias):
    tokens, width = mixed.shape
    hidden = expand.shape[1]
    cut = hidden // 4
    return pl.pallas_call(
        encoder_feed_kernel,
        grid=(4,),
        in_specs=[
            full(tokens, width),
            full(2, 2, width),
            pl.BlockSpec((width, cut), lambda i: (0, i)),
            pl.BlockSpec((1, cut), lambda i: (0, i)),
            pl.BlockSpec((cut, width), lambda i: (i, 0)),
            full(1, width),
        ],
        out_specs=[
            pl.BlockSpec((tokens, cut), lambda i: (0, i)),
            pl.BlockSpec((tokens, cut), lambda i: (0, i)),
            full(tokens, width),
            full(tokens, width),
        ],
        out_shape=[
            like((tokens, hidden), low_type),
            like((tokens, hidden), low_type),
            like((tokens, width), wide_type),
            like((tokens, width), low_type),
        ],
        scratch_shapes=[VMEM((tokens, width), low_type)],
        compiler_params=params(),
        cost_estimate=cost(2e10, 3e7, 3e6),
        name="encoder_feed",
    )(mixed, norms, expand, expand_bias[None], shrink, shrink_bias[None])


def split_refs(refs, *counts):
    out, at = [], 0
    for count in counts:
        out.append(refs[at : at + count])
        at += count
    return out + [refs[at:]]


def hosting(plan):
    return (plan.ins, len(plan.outs())) if plan else (0, 0)


def encoder_feed_back_kernel(plan, *refs):
    grads = 6 if paired() else 3
    host_ins, host_outs = hosting(plan)
    main, guests, outs, guest_outs, scratch, guest_scratch = split_refs(
        refs, 9, host_ins, 3 + grads, host_outs, 4
    )
    g_ref, sum_ref, mixed_ref, h_ref, d_ref, c_ref, n_ref, e_ref, s_ref = main
    dmix_ref, vec_ref, eb_ref = outs[:3]
    wide_outs, tall_outs, out_outs = thirds(outs[3:])
    back_low, a_turned, between, hold = scratch
    step = pl.program_id(0)
    sums = plan.open(guests, guest_outs, guest_scratch) if plan else None

    def place(n):
        if sums:
            sums.slot(step, 4, 3, n)

    place(0)
    tokens = sum_ref.shape[0]
    block = 256

    @pl.when(step == 0)
    def _():
        vec_ref[...] = jnp.zeros(vec_ref.shape, wide_type)

        def rows_step(i, carry):
            rows = pl.ds(pl.multiple_of(i * 256, 256), 256)
            grad, gain, offset = norm_rows_back(
                sum_ref[rows, :], n_ref[1, 0:1], wide(g_ref[rows, :])
            )
            dmix_ref[rows, :] = grad
            back_low[rows, :] = low(grad)
            vec_ref[0:1] += gain
            vec_ref[1:2] += offset
            vec_ref[2:3] += jnp.sum(wide(low(grad)), 0, keepdims=True)
            first = norm_rows(mixed_ref[rows, :], n_ref[0, 0:1], n_ref[0, 1:2])
            a_turned[:, rows] = low(first).T
            return carry

        lax.fori_loop(0, tokens // 256, rows_step, 0)

    column = jnp.zeros(eb_ref.shape, wide_type)
    for i in range(tokens // block):
        rows = slice(i * block, (i + 1) * block)
        before = low(dot(back_low[rows, :], s_ref[...], NT) * wide(d_ref[rows, :]))
        between[rows, :] = before
        column += jnp.sum(wide(before), 0, keepdims=True)
        dmix_ref[rows, :] += dot(before, e_ref[...], NT)
        if i == 1:
            place(1)
    eb_ref[...] = column
    hold[...] = dot(a_turned[...], between[...])
    emit(wide_outs, step, hold)
    hold[...] = dot(h_ref[...], back_low[...], TN)
    emit_tall(tall_outs, step, hold)

    @pl.when(step == pl.num_programs(0) - 1)
    def _():

        def rows_step(i, carry):
            rows = pl.ds(pl.multiple_of(i * 256, 256), 256)
            grad, gain, offset = norm_rows_back(
                mixed_ref[rows, :], n_ref[0, 0:1], dmix_ref[rows, :]
            )
            dmix_ref[rows, :] = grad
            back_low[rows, :] = low(grad)
            vec_ref[3:4] += gain
            vec_ref[4:5] += offset
            vec_ref[5:6] += jnp.sum(wide(low(grad)), 0, keepdims=True)
            return carry

        lax.fori_loop(0, tokens // 256, rows_step, 0)
        hold[...] = dot(c_ref[...], back_low[...], TN)
        emit(out_outs, 0, hold)

    place(2)


def encoder_feed_back(
    grad, summed, mixed, hidden, slope, context, norms, expand, shrink, plan=None, guests=()
):
    tokens, width = mixed.shape
    total = expand.shape[1]
    cut = total // 4
    guest_outs = plan.outs() if plan else []
    outs = pl.pallas_call(
        functools.partial(encoder_feed_back_kernel, plan),
        grid=(4,),
        in_specs=[
            once(tokens, width),
            once(tokens, width),
            once(tokens, width),
            pl.BlockSpec((tokens, cut), lambda i: (0, i)),
            pl.BlockSpec((tokens, cut), lambda i: (0, i)),
            once(tokens, width),
            full(2, 2, width),
            pl.BlockSpec((width, cut), lambda i: (0, i)),
            pl.BlockSpec((cut, width), lambda i: (i, 0)),
            *(plan.in_specs() if plan else []),
        ],
        out_specs=[
            full(tokens, width),
            full(8, width),
            pl.BlockSpec((1, cut), lambda i: (0, i)),
            *grad_specs(4, width, width),
            *grad_specs(1, total, width),
            *grad_specs(1, width, width),
            *[spec for spec, _ in guest_outs],
        ],
        out_shape=[
            like((tokens, width), wide_type),
            like((8, width), wide_type),
            like((1, total), wide_type),
            *grad_shapes(4, width, width),
            *grad_shapes(1, total, width),
            *grad_shapes(1, width, width),
            *[shape for _, shape in guest_outs],
        ],
        scratch_shapes=[
            VMEM((tokens, width), low_type),
            VMEM((width, tokens), low_type),
            VMEM((tokens, cut), low_type),
            VMEM((width, width), wide_type),
            *(plan.scratch() if plan else []),
        ],
        compiler_params=host_params(plan),
        cost_estimate=cost(4e10, 5e7),
        name="encoder_feed_back",
    )(grad, summed, mixed, hidden, slope, context, norms, expand, shrink, *guests)
    main = len(outs) - len(guest_outs)
    return outs[:3], thirds(outs[3:main]), outs[main:]


def encoder_attend_back_kernel(plan, *refs):
    host_ins, host_outs = hosting(plan)
    main, guests, (dx_ref, vec_ref), outs, guest_outs, scratch, guest_scratch = split_refs(
        refs, 7, host_ins, 2, 2 if paired() else 1, host_outs, 9
    )
    dmix_ref, x_ref, qkv_ref, c_ref, stat_ref, w_ref, wo_ref = main
    dmix_low, x_turned, dc, weights, scores_back, dk, dv, dq_turned, hold = scratch
    group = pl.program_id(0)
    sums = plan.open(guests, guest_outs, guest_scratch) if plan else None

    def place(n):
        if sums:
            sums.slot(group, 3, 3, n)

    place(0)
    tokens = x_ref.shape[0]
    block = 512
    heads = GROUP // HEAD

    @pl.when(group == 0)
    def _():
        dx_ref[...] = dmix_ref[...]
        dmix_low[...] = low(dmix_ref[...])
        x_turned[...] = x_ref[...].T

    dc[...] = low(dot(dmix_low[...], wo_ref[...], NT))
    lanes_low = head_lanes(low_type)
    eighth = jnp.asarray(scale_scores, low_type)
    pick = (
        lax.broadcasted_iota(jnp.int32, (8, GROUP), 1) // HEAD
        == lax.broadcasted_iota(jnp.int32, (8, GROUP), 0)
    ).astype(wide_type)
    pick = low(pick)
    product = wide(dc[...]) * c_ref[...]
    product_high = low(product)
    product_rest = low(product - wide(product_high))
    inner = dot(pick, product_high, NT) + dot(pick, product_rest, NT)
    k_turned = qkv_ref[1].T
    dk[...] = jnp.zeros(dk.shape, wide_type)
    dv[...] = jnp.zeros(dv.shape, wide_type)
    for i in range(tokens // block):
        rows = slice(i * block, (i + 1) * block)
        q = qkv_ref[0, rows, :] * eighth
        q_heads = jnp.concatenate([q * lanes_low[h] for h in range(heads)], 0)
        dc_heads = jnp.concatenate([dc[rows, :] * lanes_low[h] for h in range(heads)], 0)
        for h in range(heads):
            part = slice(h * block, (h + 1) * block)
            scores = dot(qkv_ref[1], q_heads[part], NT)
            weight = jnp.exp(scores - stat_ref[0, h : h + 1, rows])
            weight_back = dot(qkv_ref[2], dc_heads[part], NT)
            weights[:, part] = low(weight)
            back = low(weight * (weight_back - inner[h : h + 1, rows]))
            scores_back[:, part] = back
            dq_turned[h * HEAD : (h + 1) * HEAD, rows] = dot(
                k_turned[h * HEAD : (h + 1) * HEAD], back
            )
        dv[...] += dot(weights[...], dc_heads)
        dk[...] += dot(scores_back[...], q_heads)
        if i == 0:
            place(1)
    dq = low(dq_turned[...].T * scale_scores)
    dk_low, dv_low = low(dk[...]), low(dv[...])
    vec_ref[...] = jnp.zeros(vec_ref.shape, wide_type)
    vec_ref[0:1] = jnp.sum(wide(dq), 0, keepdims=True)
    vec_ref[1:2] = jnp.sum(wide(dv_low), 0, keepdims=True)
    dx_ref[...] += (
        dot(dq, w_ref[0], NT) + dot(dk_low, w_ref[1], NT) + dot(dv_low, w_ref[2], NT)
    )
    for part, grad in enumerate((dq, dk_low, dv_low)):
        hold[...] = dot(x_turned[...], grad)
        emit(outs, part, hold)
    place(2)


def encoder_attend_back(
    dmix, x, qkv, context, stats, inward, outward, plan=None, guests=()
):
    tokens, width = x.shape
    groups = width // GROUP
    specs = grad_specs(3, width, GROUP, lambda g: (0, 0, g))
    guest_outs = plan.outs() if plan else []
    outs = pl.pallas_call(
        functools.partial(encoder_attend_back_kernel, plan),
        grid=(groups,),
        in_specs=[
            once(tokens, width),
            once(tokens, width),
            pl.BlockSpec((3, tokens, GROUP), lambda g: (0, 0, g)),
            pl.BlockSpec((tokens, GROUP), lambda g: (0, g)),
            pl.BlockSpec((1, 8, tokens), lambda g: (g, 0, 0)),
            pl.BlockSpec((3, width, GROUP), lambda g: (0, 0, g)),
            pl.BlockSpec((GROUP, width), lambda g: (g, 0)),
            *(plan.in_specs() if plan else []),
        ],
        out_specs=[
            full(tokens, width),
            pl.BlockSpec((8, GROUP), lambda g: (0, g)),
            *specs,
            *[spec for spec, _ in guest_outs],
        ],
        out_shape=[
            like((tokens, width), wide_type),
            like((8, width), wide_type),
            *grad_shapes(3, width, width),
            *[shape for _, shape in guest_outs],
        ],
        scratch_shapes=[
            VMEM((tokens, width), low_type),
            VMEM((width, tokens), low_type),
            VMEM((tokens, GROUP), low_type),
            VMEM((tokens, 4 * 512), low_type),
            VMEM((tokens, 4 * 512), low_type),
            VMEM((tokens, GROUP), wide_type),
            VMEM((tokens, GROUP), wide_type),
            VMEM((GROUP, tokens), wide_type),
            VMEM((width, GROUP), wide_type),
            *(plan.scratch() if plan else []),
        ],
        compiler_params=host_params(plan),
        cost_estimate=cost(5e10, 4e7, 1.3e7),
        name="encoder_attend_back",
    )(dmix, x, qkv, context, stats, inward, outward, *guests)
    main = len(outs) - len(guest_outs)
    return outs[:2], outs[2:main], outs[main:]


def mask_kernel(slots_ref, across_ref, down_ref):
    count, width = slots_ref.shape
    words = down_ref.shape[0] // 32
    block = 32
    row = lax.broadcasted_iota(jnp.int32, (32, width), 0)
    for start in range(0, words, block):

        def step(i, totals):
            piece = slots_ref[pl.ds(pl.multiple_of(i * 8, 8), 8), :]
            word = lax.shift_right_logical(piece, 5)
            bit = jnp.left_shift(jnp.int32(1), piece & 31)
            return tuple(
                total | jnp.where(word == start + w, bit, 0) for w, total in enumerate(totals)
            )

        zero = jnp.zeros((8, width), jnp.int32)
        totals = lax.fori_loop(0, count // 8, step, (zero,) * block)
        for w, total in enumerate(totals):
            joined = total[0:1]
            for k in range(1, 8):
                joined = joined | total[k : k + 1]
            bits = lax.shift_right_logical(jnp.broadcast_to(joined, (32, width)), row) & 1
            at = (start + w) * 32
            down_ref[at : at + 32, :] = (wide(bits) - 1.0) * 1e30
    across_ref[...] = down_ref[...].T


def slot_mask(slots, pool):
    queries = slots.shape[0]
    return pl.pallas_call(
        mask_kernel,
        out_shape=[like((queries, pool), wide_type), like((pool, queries), wide_type)],
        in_specs=[pl.BlockSpec(memory_space=VMEM)],
        out_specs=[pl.BlockSpec(memory_space=VMEM)] * 2,
        compiler_params=params(24),
        cost_estimate=cost(1e10, 1e6),
        name="slot_mask",
    )(slots.T)


def pick_kernel(table_ref, states_ref, out_ref):
    spot = lax.broadcasted_iota(jnp.int32, (table_ref.shape[0], states_ref.shape[0]), 1)
    chosen = low((spot == table_ref[...]).astype(wide_type))
    out_ref[...] = low(dot(chosen, states_ref[...]))


def pick_rows(table, states):
    tokens, width = states.shape
    return pl.pallas_call(
        pick_kernel,
        grid=(table.size // 256,),
        in_specs=[pl.BlockSpec((256, 1), lambda i: (i, 0)), full(tokens, width)],
        out_specs=pl.BlockSpec((256, width), lambda i: (i, 0)),
        out_shape=like((table.size, width), low_type),
        compiler_params=params(24),
        cost_estimate=cost(4e9, 5e6),
        name="pick_rows",
    )(table.reshape(-1, 1), states)


def spread_kernel(table_ref, rows_ref, out_ref, total):
    step = pl.program_id(0)
    spot = lax.broadcasted_iota(jnp.int32, (out_ref.shape[0], table_ref.shape[1]), 0)
    chosen = low((spot == table_ref[...]).astype(wide_type))
    part = dot(chosen, rows_ref[...])

    @pl.when(step == 0)
    def _():
        total[...] = part

    @pl.when(step != 0)
    def _():
        total[...] += part

    @pl.when(step == pl.num_programs(0) - 1)
    def _():
        out_ref[...] = low(total[...])


def spread_rows(table, rows, tokens):
    width = rows.shape[1]
    return pl.pallas_call(
        spread_kernel,
        grid=(table.size // 512,),
        in_specs=[
            pl.BlockSpec((1, 512), lambda i: (0, i)),
            pl.BlockSpec((512, width), lambda i: (i, 0)),
        ],
        out_specs=full(tokens, width),
        out_shape=like((tokens, width), low_type),
        scratch_shapes=[VMEM((tokens, width), wide_type)],
        compiler_params=params(24),
        cost_estimate=cost(4e9, 5e6),
        name="spread_rows",
    )(table.reshape(1, -1), rows)


def by_head(value, lanes):
    return jnp.concatenate([value * lane for lane in lanes], 0)


def own_lanes(stacked, lanes):
    rows = stacked.shape[0] // len(lanes)
    return sum(stacked[h * rows : (h + 1) * rows] * lane for h, lane in enumerate(lanes))


def softmax_rows(scores):
    top = jnp.max(scores, -1, keepdims=True)
    weights = jnp.exp(scores - top)
    return weights * (1.0 / jnp.sum(weights, -1, keepdims=True))


def self_mask(lengths_ref, size):
    row = lax.broadcasted_iota(jnp.int32, (size, size), 0)
    column = lax.broadcasted_iota(jnp.int32, (size, size), 1)
    row_part, column_part = jnp.zeros_like(row), jnp.zeros_like(row)
    end = jnp.int32(0)
    for n in range(lengths_ref.shape[0] - 1):
        end = end + lengths_ref[n]
        row_part += (row >= end).astype(jnp.int32)
        column_part += (column >= end).astype(jnp.int32)
    allowed = (row_part == column_part) & (column <= row)
    added = jnp.where(allowed, 0.0, -1e30)
    return jnp.concatenate([added] * (GROUP // HEAD), 0)


def groups_of(width):
    return [slice(g, g + GROUP) for g in range(0, width, GROUP)]


def self_kernel(
    lengths_ref, y_ref, w_ref, wo_ref, b_ref, n_ref, cw_ref, qkv_ref, c_ref, mixed_ref, cq_ref
):
    y = y_ref[...]
    lanes_low, lanes = head_lanes(low_type), head_lanes(wide_type)
    mask = self_mask(lengths_ref, y.shape[0])
    qkv_ref[0] = low(dot(y, w_ref[0]) + b_ref[0:1])
    qkv_ref[1] = low(dot(y, w_ref[1]))
    qkv_ref[2] = low(dot(y, w_ref[2]) + b_ref[1:2])
    for part in groups_of(y.shape[1]):
        q = qkv_ref[0, :, part] * jnp.asarray(scale_scores, low_type)
        scores = dot(by_head(q, lanes_low), qkv_ref[1, :, part], NT) + mask
        weights = low(softmax_rows(scores))
        c_ref[:, part] = low(own_lanes(dot(weights, qkv_ref[2, :, part]), lanes))
    mixed = wide(y) + (dot(c_ref[...], wo_ref[...]) + b_ref[2:3])
    mixed_ref[...] = mixed
    first = low(norm_rows(mixed, n_ref[0, 0:1], n_ref[0, 1:2]))
    cq_ref[...] = low(dot(first, cw_ref[0]) + b_ref[3:4])


def self_forward(lengths, y, inward, outward, biases, norms, cross_inward):
    rows, width = y.shape
    return pl.pallas_call(
        self_kernel,
        grid=(1,),
        in_specs=[
            pl.BlockSpec(memory_space=pltpu.SMEM),
            full(rows, width),
            full(3, width, width),
            full(width, width),
            full(6, width),
            full(3, 2, width),
            full(1, width, width),
        ],
        out_specs=[
            full(3, rows, width),
            full(rows, width),
            full(rows, width),
            full(rows, width),
        ],
        out_shape=[
            like((3, rows, width), low_type),
            like((rows, width), low_type),
            like((rows, width), wide_type),
            like((rows, width), low_type),
        ],
        compiler_params=params(40),
        cost_estimate=cost(2e10, 7e6),
        name="self_forward",
    )(lengths, y, inward, outward, biases, norms, cross_inward)


def cross_kernel(pooled_ref, q_ref, mask_ref, w_ref, bg_ref, kv_ref, c_ref, stat_ref, scores, weights):
    rows = q_ref.shape[0]
    heads = GROUP // HEAD
    lanes_low, lanes = head_lanes(low_type), head_lanes(wide_type)
    kv_ref[0] = low(dot(pooled_ref[...], w_ref[1]))
    kv_ref[1] = low(dot(pooled_ref[...], w_ref[2]) + bg_ref[4:5])
    q = q_ref[...] * jnp.asarray(scale_scores, low_type)
    scores[...] = dot(by_head(q, lanes_low), kv_ref[0], NT)
    stats, scales = [], []
    for h in range(heads):
        part = slice(h * rows, (h + 1) * rows)
        masked = scores[part, :] + mask_ref[...]
        top = jnp.max(masked, -1, keepdims=True)
        weight = jnp.exp(masked - top)
        total = jnp.sum(weight, -1, keepdims=True)
        weights[part, :] = low(weight)
        stats.append(top + jnp.log(total))
        scales.append(lanes[h] * (1.0 / total))
    mixed = dot(weights[...], kv_ref[1])
    c_ref[...] = sum(mixed[h * rows : (h + 1) * rows] * scales[h] for h in range(heads))
    column = jnp.concatenate(stats, 0)
    stat_ref[0] = jnp.broadcast_to(column, (heads * rows, 128)).T[0:8]


def cross_forward(pooled, q, mask, inward, biases):
    slots, width = pooled.shape
    rows = q.shape[0]
    groups = width // GROUP
    stacked = rows * (GROUP // HEAD)
    return pl.pallas_call(
        cross_kernel,
        grid=(groups,),
        in_specs=[
            full(slots, width),
            pl.BlockSpec((rows, GROUP), lambda g: (0, g)),
            full(rows, slots),
            pl.BlockSpec((3, width, GROUP), lambda g: (0, 0, g)),
            pl.BlockSpec((6, GROUP), lambda g: (0, g)),
        ],
        out_specs=[
            pl.BlockSpec((2, slots, GROUP), lambda g: (0, 0, g)),
            pl.BlockSpec((rows, GROUP), lambda g: (0, g)),
            pl.BlockSpec((1, 8, stacked), lambda g: (g, 0, 0)),
        ],
        out_shape=[
            like((2, slots, width), low_type),
            like((rows, width), wide_type),
            like((groups, 8, stacked), wide_type),
        ],
        scratch_shapes=[VMEM((stacked, slots), wide_type), VMEM((stacked, slots), low_type)],
        compiler_params=params(),
        cost_estimate=cost(2e10, 1.2e7, 3e6),
        name="cross_forward",
    )(pooled, q, mask, inward, biases)


def middle_kernel(
    mixed_ref, c_ref, co_ref, b_ref, n_ref, e_ref, eb_ref, s_ref, sb_ref, grad_ref, *rest
):
    out_ref, joined_back_ref, dc_ref, vec_ref, deb_ref = rest[:5]
    hidden, slope, between, hold = rest[-4:]
    feed_ref, out_outs = rest[5], rest[6:-4]
    parts = feed_ref.shape[0]
    width = mixed_ref.shape[1]
    blocks = [slice(i * width, (i + 1) * width) for i in range(e_ref.shape[1] // width)]
    first = norm_rows(mixed_ref[...], n_ref[0, 0:1], n_ref[0, 1:2])
    context = low(c_ref[...])
    joined = first + (dot(context, co_ref[...]) + b_ref[5:6])
    second = norm_rows(joined, n_ref[1, 0:1], n_ref[1, 1:2])
    second_low = low(second)
    total = jnp.zeros(joined.shape, wide_type)
    for part in blocks:
        value, rate = gelu_parts(dot(second_low, e_ref[:, part]) + eb_ref[:, part])
        hidden[:, part] = low(value)
        slope[:, part] = rate
        total += dot(hidden[:, part], s_ref[part, :])
    summed = second + (total + sb_ref[...])
    out_ref[...] = low(norm_rows(summed, n_ref[2, 0:1], n_ref[2, 1:2]))
    summed_back, gain, offset = norm_rows_back(summed, n_ref[2, 0:1], wide(grad_ref[...]))
    summed_low = low(summed_back)
    vec_ref[...] = jnp.zeros(vec_ref.shape, wide_type)
    vec_ref[0:1] = gain
    vec_ref[1:2] = offset
    vec_ref[2:3] = jnp.sum(wide(summed_low), 0, keepdims=True)
    second_back = summed_back
    for part in blocks:
        before = low(dot(summed_low, s_ref[part, :], NT) * slope[:, part])
        between[:, part] = before
        deb_ref[:, part] = jnp.sum(wide(before), 0, keepdims=True)
        second_back += dot(before, e_ref[:, part], NT)
    joined_back, gain, offset = norm_rows_back(joined, n_ref[1, 0:1], second_back)
    joined_low = low(joined_back)
    joined_back_ref[...] = joined_back
    vec_ref[3:4] = gain
    vec_ref[4:5] = offset
    vec_ref[5:6] = jnp.sum(wide(joined_low), 0, keepdims=True)
    dc_ref[...] = low(dot(joined_low, co_ref[...], NT))
    for i, part in enumerate(blocks):
        rows = width // parts
        grad = low(dot(second_low, between[:, part], TN))
        for n in range(parts):
            feed_ref[n, i * rows : (i + 1) * rows, :] = grad[n * rows : (n + 1) * rows]
        grad = low(dot(hidden[:, part], summed_low, TN))
        rows, first = 4 * rows, i * parts // 4
        for n in range(parts // 4):
            feed_ref[first + n, rows:, :] = grad[n * rows : (n + 1) * rows]
    hold[...] = dot(context, joined_low, TN)
    emit(out_outs, 0, hold)


def middle(mixed, context, outward, biases, norms, expand, expand_bias, shrink, shrink_bias, grad):
    rows, width = mixed.shape
    total = expand.shape[1]
    parts = lax.axis_size("dp")
    ins = (
        mixed,
        context,
        outward,
        biases,
        norms,
        expand,
        expand_bias[None],
        shrink,
        shrink_bias[None],
        grad,
    )
    outs = pl.pallas_call(
        middle_kernel,
        grid=(1,),
        in_specs=[full(*value.shape) for value in ins],
        out_specs=[
            full(rows, width),
            full(rows, width),
            full(rows, width),
            full(8, width),
            full(1, total),
            full(parts, 2 * total // parts, width),
            *grad_specs(1, width, width),
        ],
        out_shape=[
            like((rows, width), low_type),
            like((rows, width), wide_type),
            like((rows, width), low_type),
            like((8, width), wide_type),
            like((1, total), wide_type),
            like((parts, 2 * total // parts, width), low_type),
            *grad_shapes(1, width, width),
        ],
        scratch_shapes=[
            VMEM((rows, total), low_type),
            VMEM((rows, total), wide_type),
            VMEM((rows, total), low_type),
            VMEM((width, width), wide_type),
        ],
        compiler_params=params(),
        cost_estimate=cost(2e10, 2.2e7),
        name="middle",
    )(*ins)
    return outs[:5], outs[5], outs[6:]


def cross_back_kernel(
    kv_ref, q_ref, c_ref, dc_ref, stat_ref, mask_ref, w_ref, dkv_ref, dq_ref, vec_ref, dpool_ref,
    total, weights, scores_back
):
    group = pl.program_id(0)
    rows = q_ref.shape[0]
    heads = GROUP // HEAD
    lanes_low, lanes = head_lanes(low_type), head_lanes(wide_type)
    q_heads = by_head(q_ref[...] * jnp.asarray(scale_scores, low_type), lanes_low)
    dc_heads = by_head(dc_ref[...], lanes_low)
    product = wide(dc_heads) * jnp.concatenate([c_ref[...]] * heads, 0)
    column = jnp.sum(product, -1, keepdims=True)
    inner = jnp.broadcast_to(column, (heads * rows, 128)).T[0:1]
    stat = stat_ref[0, 0:1]
    for h in range(heads):
        part = slice(h * rows, (h + 1) * rows)
        weight = jnp.exp(dot(kv_ref[0], q_heads[part], NT) + mask_ref[...] - stat[:, part])
        weight_back = dot(kv_ref[1], dc_heads[part], NT)
        weights[:, part] = low(weight)
        scores_back[:, part] = low(weight * (weight_back - inner[:, part]))
    dk = low(dot(scores_back[...], q_heads))
    dv = low(dot(weights[...], dc_heads))
    dkv_ref[0] = dk
    dkv_ref[1] = dv
    dq = low(own_lanes(dot(scores_back[...], kv_ref[0], TN), lanes) * scale_scores)
    dq_ref[...] = dq
    vec_ref[...] = jnp.zeros(vec_ref.shape, wide_type)
    vec_ref[0:1] = jnp.sum(wide(dq), 0, keepdims=True)
    vec_ref[1:2] = jnp.sum(wide(dv), 0, keepdims=True)
    part = dot(dk, w_ref[1], NT) + dot(dv, w_ref[2], NT)

    @pl.when(group == 0)
    def _():
        total[...] = part

    @pl.when(group != 0)
    def _():
        total[...] += part

    @pl.when(group == pl.num_programs(0) - 1)
    def _():
        dpool_ref[...] = low(total[...])


def cross_back(kv, q, context, dc, stats, mask, inward):
    slots, width = kv.shape[1:]
    rows = q.shape[0]
    groups = width // GROUP
    stacked = rows * (GROUP // HEAD)
    column = pl.BlockSpec((rows, GROUP), lambda g: (0, g))
    return pl.pallas_call(
        cross_back_kernel,
        grid=(groups,),
        in_specs=[
            pl.BlockSpec((2, slots, GROUP), lambda g: (0, 0, g)),
            column,
            column,
            column,
            pl.BlockSpec((1, 8, stacked), lambda g: (g, 0, 0)),
            full(slots, rows),
            pl.BlockSpec((3, width, GROUP), lambda g: (0, 0, g)),
        ],
        out_specs=[
            pl.BlockSpec((2, slots, GROUP), lambda g: (0, 0, g)),
            column,
            pl.BlockSpec((8, GROUP), lambda g: (0, g)),
            full(slots, width),
        ],
        out_shape=[
            like((2, slots, width), low_type),
            like((rows, width), low_type),
            like((8, width), wide_type),
            like((slots, width), low_type),
        ],
        scratch_shapes=[
            VMEM((slots, width), wide_type),
            VMEM((slots, stacked), low_type),
            VMEM((slots, stacked), low_type),
        ],
        compiler_params=params(),
        cost_estimate=cost(3e10, 2.2e7, 3e6),
        name="cross_back",
    )(kv, q, context, dc, stats, mask, inward)


def cross_grads_kernel(pooled_ref, dkv_ref, mixed_ref, dq_ref, n_ref, *rest):
    outs, (turned, hold) = rest[:-2], rest[-2:]

    @pl.when(pl.program_id(0) == 0)
    def _():
        turned[...] = pooled_ref[...].T

    first = low(norm_rows(mixed_ref[...], n_ref[0, 0:1], n_ref[0, 1:2]))
    hold[...] = dot(first, dq_ref[...], TN)
    emit(outs, 0, hold)
    hold[...] = dot(turned[...], dkv_ref[0])
    emit(outs, 1, hold)
    hold[...] = dot(turned[...], dkv_ref[1])
    emit(outs, 2, hold)


def cross_grads(pooled, dkv, mixed, dq, norms):
    slots, width = pooled.shape
    rows = mixed.shape[0]
    return pl.pallas_call(
        cross_grads_kernel,
        grid=(width // GROUP,),
        in_specs=[
            full(slots, width),
            pl.BlockSpec((2, slots, GROUP), lambda g: (0, 0, g)),
            full(rows, width),
            pl.BlockSpec((rows, GROUP), lambda g: (0, g)),
            full(3, 2, width),
        ],
        out_specs=grad_specs(3, width, GROUP, lambda g: (0, 0, g)),
        out_shape=grad_shapes(3, width, width),
        scratch_shapes=[VMEM((width, slots), low_type), VMEM((width, GROUP), wide_type)],
        compiler_params=params(48),
        cost_estimate=cost(1e10, 1.5e7),
        name="cross_grads",
    )(pooled, dkv, mixed, dq, norms)


def self_back_kernel(
    lengths_ref, y_ref, mixed_ref, jb_ref, cdq_ref, qkv_ref, c_ref, w_ref, wo_ref, cw_ref, n_ref,
    dy_ref, vec_ref, *rest
):
    outs, (dqkv, hold) = rest[:-2], rest[-2:]
    width = y_ref.shape[1]
    y = y_ref[...]
    lanes_low, lanes = head_lanes(low_type), head_lanes(wide_type)
    mask = self_mask(lengths_ref, y.shape[0])
    first_back = jb_ref[...] + dot(cdq_ref[...], cw_ref[0], NT)
    mixed_back, gain, offset = norm_rows_back(mixed_ref[...], n_ref[0, 0:1], first_back)
    mixed_low = low(mixed_back)
    vec_ref[...] = jnp.zeros(vec_ref.shape, wide_type)
    vec_ref[0:1] = gain
    vec_ref[1:2] = offset
    vec_ref[2:3] = jnp.sum(wide(mixed_low), 0, keepdims=True)
    dc = low(dot(mixed_low, wo_ref[...], NT))
    for part in groups_of(width):
        q_heads = by_head(qkv_ref[0, :, part] * jnp.asarray(scale_scores, low_type), lanes_low)
        dc_heads = by_head(dc[:, part], lanes_low)
        weights = softmax_rows(dot(q_heads, qkv_ref[1, :, part], NT) + mask)
        weights_back = dot(dc_heads, qkv_ref[2, :, part], NT)
        inner = jnp.sum(weights * weights_back, -1, keepdims=True)
        scores_back = low(weights * (weights_back - inner))
        dq = own_lanes(dot(scores_back, qkv_ref[1, :, part]), lanes) * scale_scores
        dqkv[0, :, part] = low(dq)
        dqkv[1, :, part] = low(dot(scores_back, q_heads, TN))
        dqkv[2, :, part] = low(dot(low(weights), dc_heads, TN))
    vec_ref[3:4] = jnp.sum(wide(dqkv[0]), 0, keepdims=True)
    vec_ref[4:5] = jnp.sum(wide(dqkv[2]), 0, keepdims=True)
    dy_ref[...] = (
        mixed_back
        + dot(dqkv[0], w_ref[0], NT)
        + (dot(dqkv[1], w_ref[1], NT) + dot(dqkv[2], w_ref[2], NT))
    )
    for part in range(3):
        hold[...] = dot(y, dqkv[part], TN)
        emit(outs, part, hold)
    hold[...] = dot(c_ref[...], mixed_low, TN)
    emit(outs, 3, hold)


def self_back(lengths, y, mixed, joined_back, dq, qkv, context, inward, outward, cross_inward, norms):
    rows, width = y.shape
    ins = (y, mixed, joined_back, dq, qkv, context, inward, outward)
    outs = pl.pallas_call(
        self_back_kernel,
        grid=(1,),
        in_specs=[
            pl.BlockSpec(memory_space=pltpu.SMEM),
            *[full(*value.shape) for value in ins],
            full(1, width, width),
            full(3, 2, width),
        ],
        out_specs=[full(rows, width), full(8, width), *grad_specs(4, width, width)],
        out_shape=[
            like((rows, width), wide_type),
            like((8, width), wide_type),
            *grad_shapes(4, width, width),
        ],
        scratch_shapes=[VMEM((3, rows, width), low_type), VMEM((width, width), wide_type)],
        compiler_params=params(48),
        cost_estimate=cost(2e10, 1.5e7),
        name="self_back",
    )(lengths, *ins, cross_inward, norms)
    return outs[:2], outs[2:]


CUT = 192
HALF = CUT // 2
MESH = pl.DeviceIdType.MESH


def shifted(value, axis, by):
    length = lax.axis_size(axis)
    return lax.ppermute(value, axis, [(i, (i + by) % length) for i in range(length)])


def add_rows(to, other, rows):
    def step(i, carry):
        at = pl.ds(pl.multiple_of(i * 32, 32), 32)
        to[at, :] = low(wide(to[at, :]) + wide(other[at, :]))
        return carry

    lax.fori_loop(0, rows // 32, step, 0)


def partners():
    me, section = lax.axis_index("dp"), lax.axis_index("section")
    return (
        {"dp": me + 1 - 2 * (me % 2)},
        {"dp": me + 2 - 4 * ((me // 2) % 2)},
        {"dp": me + 4 - 8 * (me // 4)},
        {"section": section + 1 - 2 * (section % 2)},
        {"section": section + 2 - 4 * (section // 2)},
    )


def on_section(*sections):
    section = lax.axis_index("section")
    wanted = section == sections[0]
    for other in sections[1:]:
        wanted = wanted | (section == other)
    return pl.when(wanted)


def greet():
    barrier = pltpu.get_barrier_semaphore()
    for partner in partners():
        pl.semaphore_signal(barrier, 1, device_id=partner, device_id_type=MESH)

    @on_section(1, 2)
    def _():
        other = {"section": 3 - lax.axis_index("section")}
        pl.semaphore_signal(barrier, 1, device_id=other, device_id_type=MESH)
        pl.semaphore_wait(barrier, 6)

    @on_section(0, 3)
    def _():
        pl.semaphore_wait(barrier, 5)


def laid_out(pieces):
    out, at = [], 0
    for n, first, size in pieces:
        row = first
        while row < first + size:
            rows = min(CUT - at % CUT, first + size - row)
            out.append((n, row, rows, at // CUT, at % CUT))
            row, at = row + rows, at + rows
    return tuple(out), at // CUT


class Plan:
    def __init__(
        self, pieces, arrived, schedule, collective_id, onward=False, vector=0, moved=()
    ):
        self.arrays = 1 + max(piece[0] for piece in pieces)
        self.schedule, self.collective_id = schedule, collective_id
        self.sources, self.fresh = laid_out(pieces)
        self.from_kernels = tuple(arrived)
        arrived = sum(self.from_kernels)
        self.arrived, self.onward = arrived, onward
        self.vector = vector
        self.vector_order = (1, 2, 0, 3, 4)
        self.moved = tuple(moved)
        self.late = arrived + (self.fresh if onward else 0)
        self.ins = 2 * self.arrays + len(self.from_kernels) + len(self.moved) + (1 if vector else 0)

    def in_specs(self):
        anywhere = pl.BlockSpec(memory_space=pl.ANY)
        count = self.ins - (1 if self.vector else 0)
        return [anywhere] * count + ([pl.BlockSpec(memory_space=VMEM)] if self.vector else [])

    def outs(self):
        out = []
        if not self.onward:
            out.append((pl.BlockSpec(memory_space=pl.ANY), like((self.fresh * CUT, WIDTH), low_type)))
        if self.late:
            out.append((pl.BlockSpec(memory_space=pl.ANY), like((self.late * CUT, WIDTH), low_type)))
        for value in self.moved:
            out.append((pl.BlockSpec(memory_space=pl.ANY), value))
        if self.vector:
            out.append((pl.BlockSpec(memory_space=VMEM), like((self.vector, WIDTH), wide_type)))
        return out

    def scratch(self):
        dma = pltpu.SemaphoreType.DMA
        fresh, late, arrived = self.fresh, max(self.late, 1), max(self.arrived, 1)
        most = max(fresh, late)
        count = len(self.sources)
        return [
            VMEM((fresh, 4, CUT, WIDTH), low_type),
            VMEM((fresh, 4, CUT, WIDTH), low_type),
            VMEM((fresh, 2, 2, HALF, WIDTH), low_type),
            VMEM((fresh, 2, HALF, WIDTH), low_type),
            VMEM((arrived, CUT, WIDTH if self.late else 128), low_type),
            VMEM((late, CUT, WIDTH if self.late else 128), low_type),
            VMEM((late, HALF, WIDTH if self.late else 128), low_type),
            VMEM((late, CUT, WIDTH if self.late else 128), low_type),
            VMEM((5, self.vector or 8, WIDTH), wide_type),
            dma((count,)),
            dma((count,)),
            dma((count,)),
            dma((3, fresh, 3)),
            dma((3, fresh, 3)),
            dma((late, 5)),
            dma((late, 5)),
            dma((arrived,)),
            dma((2, most)),
            dma((5,)),
            dma((5,)),
            dma((max(len(self.moved), 1),)),
            dma((max(len(self.moved), 1),)),
        ]

    def open(self, ins, outs, scratch):
        return Sums(self, ins, outs, scratch)


class Sums:
    def __init__(self, plan, ins, outs, scratch):
        count = plan.arrays
        outs, ins = list(outs), list(ins)
        self.plan = plan
        self.keeps, self.sends = ins[:count], ins[count : 2 * count]
        ins = ins[2 * count :]
        self.arrived = [ins.pop(0) for _ in plan.from_kernels]
        self.moved = [ins.pop(0) for _ in plan.moved]
        self.vec_ref = ins.pop(0) if plan.vector else None
        self.shard_out = None if plan.onward else outs.pop(0)
        self.late_out = outs.pop(0) if plan.late else None
        self.moved_out = [outs.pop(0) for _ in plan.moved]
        self.vec_out = outs.pop(0) if plan.vector else None
        (
            self.own,
            self.from_core,
            self.from_one,
            self.from_two,
            self.waiting,
            self.from_outer,
            self.from_inner,
            self.whole,
            self.vec_in,
            self.load_sems,
            self.core_send,
            self.core_recv,
            self.send_sems,
            self.recv_sems,
            self.line_send,
            self.line_recv,
            self.arrive_sems,
            self.out_sems,
            self.vec_send,
            self.vec_recv,
            self.moved_send,
            self.moved_recv,
        ) = scratch
        self.core, self.over_x, self.over_y = partners()[:3]
        section = lax.axis_index("section")
        side = section // 2
        self.mine = pl.multiple_of(side * HALF, HALF)
        self.other = pl.multiple_of((1 - side) * HALF, HALF)
        self.outer = {"section": 3 * side}
        self.inner = {"section": 2 - side}
        self.inward = {"section": 1 + side}

    def remote(self, source, to, send, recv, partner):
        return pltpu.make_async_remote_copy(
            src_ref=source,
            dst_ref=to,
            send_sem=send,
            recv_sem=recv,
            device_id=partner,
            device_id_type=MESH,
        )

    def load(self, s):
        n, row, rows, chunk, at = self.plan.sources[s]
        return pltpu.make_async_copy(
            self.keeps[n].at[:, pl.ds(row, rows)],
            self.own.at[chunk, :, pl.ds(at, rows)],
            self.load_sems.at[s],
        )

    def cross(self, s):
        n, row, rows, chunk, at = self.plan.sources[s]
        return self.remote(
            self.sends[n].at[:, pl.ds(row, rows)],
            self.from_core.at[chunk, :, pl.ds(at, rows)],
            self.core_send.at[s],
            self.core_recv.at[s],
            self.core,
        )

    def arrive(self, k):
        at, source = k, 0
        while at >= self.plan.from_kernels[source]:
            at, source = at - self.plan.from_kernels[source], source + 1
        return pltpu.make_async_copy(
            self.arrived[source].at[pl.ds(at * CUT, CUT)],
            self.waiting.at[k],
            self.arrive_sems.at[k],
        )

    def summed(self, k):
        if k < self.plan.arrived:
            return self.waiting.at[k]
        return self.own.at[k - self.plan.arrived, 0]

    def pairs(self, stage, c):
        own, upper, lower = self.own, pl.ds(0, HALF), pl.ds(HALF, HALF)
        if stage == 1:
            return (
                (own.at[c, 1, upper], self.from_one.at[c, 0, 0], self.over_x),
                (own.at[c, 3, upper], self.from_one.at[c, 0, 1], self.over_x),
                (own.at[c, pl.ds(2, 2), lower], self.from_one.at[c, 1], self.over_y),
            )
        return (
            (own.at[c, 2, upper], self.from_two.at[c, 0], self.over_y),
            (own.at[c, 1, lower], self.from_two.at[c, 1], self.over_x),
        )

    def copies(self, stage, c):
        return [
            self.remote(
                source, to, self.send_sems.at[stage, c, k], self.recv_sems.at[stage, c, k], partner
            )
            for k, (source, to, partner) in enumerate(self.pairs(stage, c))
        ]

    def start(self, stage, c):
        for copy in self.copies(stage, c):
            copy.start()

    def line_copy(self, n, k):
        mine, other = pl.ds(self.mine, HALF), pl.ds(self.other, HALF)
        whole = self.whole.at[k]
        source, to, partner = (
            (self.summed(k), self.from_outer.at[k], self.inward),
            (self.summed(k).at[other], self.from_inner.at[k], self.inner),
            (whole.at[mine], whole.at[mine], self.inner),
            (whole.at[mine], whole.at[mine], self.outer),
            (whole.at[other], whole.at[other], self.outer),
        )[n]
        return self.remote(source, to, self.line_send.at[k, n], self.line_recv.at[k, n], partner)

    def line(self, stage, k):
        if stage == "go":

            @on_section(0, 3)
            def _():
                self.line_copy(0, k).start()

            return
        if stage == 6:

            @on_section(0, 3)
            def _():
                self.line_copy(3, k).wait_recv()
                self.line_copy(4, k).wait_recv()

            self.late_copy(k).start()
            return

        @on_section(1, 2)
        def _():
            self.line_copy(stage - 3, k).wait_recv()
            if stage == 3:
                add_rows(self.summed(k), self.from_outer.at[k], CUT)
                self.line_copy(1, k).start()
            elif stage == 4:
                rows = pl.ds(self.mine, HALF)
                self.whole[k, rows, :] = low(
                    wide(self.summed(k)[rows, :]) + wide(self.from_inner[k])
                )
                self.line_copy(2, k).start()
                self.line_copy(3, k).start()
            else:
                self.line_copy(4, k).start()

    def line_sent(self, k):
        @on_section(0, 3)
        def _():
            self.line_copy(0, k).wait_send()

        @on_section(1, 2)
        def _():
            for n in range(1, 5):
                self.line_copy(n, k).wait_send()

    def shard_copy(self, c):
        return pltpu.make_async_copy(
            self.own.at[c, 0], self.shard_out.at[pl.ds(c * CUT, CUT)], self.out_sems.at[0, c]
        )

    def late_copy(self, k):
        return pltpu.make_async_copy(
            self.whole.at[k], self.late_out.at[pl.ds(k * CUT, CUT)], self.out_sems.at[1, k]
        )

    def moved_copy(self, n):
        return self.remote(
            self.moved[n],
            self.moved_out[n],
            self.moved_send.at[n],
            self.moved_recv.at[n],
            partners()[4],
        )

    def vec_copy(self, stage):
        return self.remote(
            self.vec_out,
            self.vec_in.at[stage],
            self.vec_send.at[stage],
            self.vec_recv.at[stage],
            partners()[self.plan.vector_order[stage]],
        )

    def vec_step(self, stage):
        if stage:
            self.vec_copy(stage - 1).wait()
            self.vec_out[...] += self.vec_in[stage - 1]
        else:
            self.vec_out[...] = self.vec_ref[...]
        if stage < 5:
            self.vec_copy(stage).start()

    def begin(self):
        greet()
        for s in range(len(self.plan.sources)):
            self.cross(s).start()
            self.load(s).start()
        for k in range(self.plan.arrived):
            self.arrive(k).start()
        for n in range(len(self.moved)):
            self.moved_copy(n).start()

    def step(self, stage, c):
        if stage == "vec":
            self.vec_step(c)
            return
        if stage == "go":
            self.arrive(c).wait()
            self.line("go", c)
            return
        if stage > 2:
            self.line(stage, c)
            return
        if stage == 0:
            for s, source in enumerate(self.plan.sources):
                if source[3] == c:
                    self.load(s).wait()
                    self.cross(s).wait_recv()
            for at in range(4):
                add_rows(self.own.at[c, at], self.from_core.at[c, at], CUT)
            self.start(1, c)
            return
        for copy in self.copies(stage, c):
            copy.wait_recv()
        upper, lower = pl.ds(0, HALF), pl.ds(HALF, HALF)
        if stage == 1:
            for k in range(2):
                add_rows(self.own.at[c, 2 * k, upper], self.from_one.at[c, 0, k], HALF)
                add_rows(self.own.at[c, k, lower], self.from_one.at[c, 1, k], HALF)
            self.start(2, c)
        else:
            add_rows(self.own.at[c, 0, upper], self.from_two.at[c, 0], HALF)
            add_rows(self.own.at[c, 0, lower], self.from_two.at[c, 1], HALF)
            if self.plan.onward:
                self.line("go", self.plan.arrived + c)
            else:
                self.shard_copy(c).start()

    def finish(self):
        for n in range(len(self.moved)):
            self.moved_copy(n).wait()
        for s in range(len(self.plan.sources)):
            self.cross(s).wait_send()
        for c in range(self.plan.fresh):
            for stage in (1, 2):
                for copy in self.copies(stage, c):
                    copy.wait_send()
            if not self.plan.onward:
                self.shard_copy(c).wait()
        for k in range(self.plan.late):
            self.line_sent(k)
            self.late_copy(k).wait()

    def slot(self, grid_step, steps, slots, slot):
        for n in range(steps):
            wanted = self.plan.schedule.get(n * slots + slot, ())
            if not wanted:
                continue

            @pl.when(grid_step == n)
            def _(wanted=wanted):
                for stage, c in wanted:
                    if stage == "begin":
                        self.begin()
                    elif stage == "finish":
                        self.finish()
                    else:
                        self.step(stage, c)


def last_sums_kernel(plan, *refs):
    ins, rest = refs[: plan.ins], refs[plan.ins :]
    count = len(plan.outs())
    sums = plan.open(ins, rest[:count], rest[count:])
    sums.begin()
    for stage, c in plan.schedule:
        sums.step(stage, c)
    sums.finish()


def last_sums(plan, pairs, arrived, vector):
    outs = plan.outs()
    return pl.pallas_call(
        functools.partial(last_sums_kernel, plan),
        in_specs=plan.in_specs(),
        out_specs=[spec for spec, _ in outs],
        out_shape=[shape for _, shape in outs],
        scratch_shapes=plan.scratch(),
        compiler_params=params(60, collective_id=plan.collective_id, has_side_effects=True),
        cost_estimate=cost(1e8, 1e8),
        name="last_sums",
    )(*[p[0] for p in pairs], *[p[1] for p in pairs], *arrived, vector)


def feed_plan(moved):
    schedule = {
        0: [("begin", 0)],
        1: [(0, 0), (0, 1), (0, 2)],
        9: [(1, 0), (1, 1), (1, 2)],
        11: [(2, 0), (2, 1), (2, 2), ("finish", 0)],
    }
    return Plan(((0, 0, 288), (1, 0, 96), (2, 0, 192)), (), schedule, 1, moved=moved)


def attend_plan():
    schedule = {
        0: [("begin", 0), ("vec", 0)],
        1: [("vec", 1), (0, 0), (0, 1), (0, 2), (0, 3), (0, 4)],
        3: [("vec", 2)],
        4: [("vec", 3)],
        6: [("vec", 4), (1, 0), (1, 1), (1, 2)],
        7: [("vec", 5), (1, 3), (1, 4)],
        8: [(2, 0), (2, 1), (2, 2), (2, 3), (2, 4), ("finish", 0)],
    }
    return Plan(((0, 192, 192), (1, 0, 384), (2, 0, 384)), (), schedule, 2, vector=32)


def last_plan():
    order = [("vec", 0), *[("go", k) for k in range(5)], ("vec", 1), (0, 0), ("vec", 2), (0, 1)]
    order += [("vec", 3), (1, 0), (1, 1), (3, 0), (2, 0), (2, 1), (3, 1), (4, 0), (3, 2), (4, 1)]
    order += [(5, 0), (3, 3), (4, 2), (5, 1), (6, 0), (3, 4), ("vec", 4), (4, 3), (5, 2), (6, 1)]
    order += [(3, 5), (4, 4), (5, 3), (6, 2), (3, 6), (4, 5), (5, 4), (6, 3), (4, 6), (5, 5)]
    order += [(6, 4), ("vec", 5), (5, 6), (6, 5), (6, 6)]
    return Plan(((0, 0, 288), (1, 0, 96)), (5,), order, 3, onward=True, vector=8)


def unpack_kernel(feed_ref, first_ref, last_ref, vec_ref, bias_ref, *outs):
    (
        e_in, e_out, e_bias, e_norm, e_expand, e_expand_bias, e_shrink, e_shrink_bias,
        s_in, s_out, c_in, c_out, d_bias, d_norm, d_expand, d_expand_bias, d_shrink, d_shrink_bias,
    ) = outs
    rows = e_out.shape[0]

    def rows_of(ref, at, count=1):
        return wide(ref[at * rows : (at + count) * rows, :])

    for i in range(4):
        part = slice(i * WIDTH, (i + 1) * WIDTH)
        d_expand[:, part] = rows_of(feed_ref, i)
        e_expand[:, part] = rows_of(last_ref, 2 + i)
    d_shrink[...] = rows_of(feed_ref, 4, 4)
    for i in range(3):
        c_in[i] = rows_of(first_ref, i)
        e_in[i] = rows_of(last_ref, 10 + i)
    c_out[...] = rows_of(first_ref, 3)
    s_in[0] = rows_of(first_ref, 4)
    s_in[1] = rows_of(first_ref, 5)
    s_in[2] = rows_of(last_ref, 0)
    s_out[...] = rows_of(last_ref, 1)
    e_shrink[...] = rows_of(last_ref, 6, 4)
    e_out[...] = rows_of(last_ref, 13)
    me = lax.axis_index("dp")
    mine = pltpu.roll(vec_ref[...], WIDTH - me * rows, 1)
    e_bias[0:2] = pltpu.roll(bias_ref[...], WIDTH - me * rows, 1)[0:2, 0:rows]
    e_bias[2:3] = mine[2:3, 0:rows]
    e_norm[0] = mine[3:5, 0:rows]
    e_norm[1] = mine[5:7, 0:rows]
    e_shrink_bias[...] = mine[11:12, 0:rows]
    d_bias[...] = mine[12:18, 0:rows]
    for i in range(3):
        d_norm[i] = mine[18 + 2 * i : 20 + 2 * i, 0:rows]
    d_shrink_bias[...] = mine[28:29, 0:rows]
    for at, to in ((7, e_expand_bias), (24, d_expand_bias)):
        row = jnp.zeros((1, WIDTH), wide_type)
        for i in range(4):
            row = jnp.where(me // 2 == i, vec_ref[at + i : at + i + 1, :], row)
        to[...] = jnp.where(me % 2 == 0, row[:, : WIDTH // 2], row[:, WIDTH // 2 :])


def unpack(feed, first, last, vector, biases):
    rows, width = WIDTH // 8, WIDTH
    square, cube = (rows, width), (3, rows, width)
    wide_one, tall_one = (rows, 4 * width), (4 * rows, width)
    shapes = [
        cube, square, (3, rows), (2, 2, rows), wide_one, (1, 4 * rows), tall_one, (1, rows),
        cube, square, cube, square, (6, rows), (3, 2, rows), wide_one, (1, 4 * rows), tall_one,
        (1, rows),
    ]
    here = pl.BlockSpec(memory_space=VMEM)
    return pl.pallas_call(
        unpack_kernel,
        in_specs=[here] * 5,
        out_specs=[here] * len(shapes),
        out_shape=[like(shape, wide_type) for shape in shapes],
        compiler_params=params(40),
        cost_estimate=cost(1e7, 1.3e7),
        name="unpack",
    )(feed, first, last, vector, biases)


def sum_whole(grads):
    parts = lax.axis_size("dp")
    packed = []
    for grad in grads:
        count, rows, columns = grad.shape
        cut = grad.reshape(count, parts, rows // parts, columns // WIDTH, WIDTH)
        packed.append(cut.transpose(1, 0, 3, 2, 4).reshape(parts, -1, WIDTH))
    shard = lax.psum_scatter(jnp.concatenate(packed, 1), "dp", scatter_dimension=0, tiled=True)[0]
    total = wide(lax.psum(shard, "section"))
    outs, at = [], 0
    for grad in grads:
        count, rows, columns = grad.shape
        size = grad.size // parts // WIDTH
        cut = total[at : at + size].reshape(count, columns // WIDTH, rows // parts, WIDTH)
        outs.append(cut.transpose(0, 2, 1, 3).reshape(count * rows // parts, columns))
        at += size
    return outs


def beside(shard):
    rows = shard.shape[0] // 4
    return shard.reshape(4, rows, WIDTH).transpose(1, 0, 2).reshape(rows, 4 * WIDTH)


def sum_any(grads, d_feed, vectors):
    e_in, e_out, e_expand, e_shrink, s_all, c_in, c_out = sum_whole([grad[0] for grad in grads])
    d_feed = wide(lax.psum(d_feed, "section"))
    d_expand, d_shrink = d_feed[: d_feed.shape[0] // 2], d_feed[d_feed.shape[0] // 2 :]
    flat = lax.psum(jnp.concatenate([v.reshape(-1) for v in vectors]), ("dp", "section"))
    parts, mine = lax.axis_size("dp"), lax.axis_index("dp")
    outs, at = [], 0
    for v in vectors:
        whole = flat[at : at + v.size].reshape(v.shape)
        at += v.size
        size = v.shape[-1] // parts
        outs.append(lax.dynamic_slice_in_dim(whole, mine * size, size, v.ndim - 1))
    rows = WIDTH // parts
    return (
        e_in.reshape(3, rows, WIDTH),
        e_out,
        outs[0],
        outs[1],
        beside(e_expand),
        outs[2],
        e_shrink,
        outs[3],
        s_all[: 3 * rows].reshape(3, rows, WIDTH),
        s_all[3 * rows :],
        c_in.reshape(3, rows, WIDTH),
        c_out,
        outs[4],
        outs[5],
        beside(d_expand),
        outs[6],
        d_shrink,
        outs[7],
    )


def on_device(
    encoder_input,
    decoder_input,
    cotangent,
    pool_table,
    retrieved,
    decoder_lengths,
    encoder_inward,
    encoder_outward,
    encoder_biases,
    encoder_norms,
    encoder_expand,
    encoder_expand_bias,
    encoder_shrink,
    encoder_shrink_bias,
    self_inward,
    self_outward,
    cross_inward,
    cross_outward,
    decoder_biases,
    decoder_norms,
    decoder_expand,
    decoder_expand_bias,
    decoder_shrink,
    decoder_shrink_bias,
):
    x = encoder_input[0]
    half_way = lax.axis_size("section") // 2
    queries = decoder_input.shape[1]
    topk = retrieved.shape[2]
    rows_low = shifted(jnp.concatenate([decoder_input[0], cotangent[0]], 0), "section", -half_way)
    y, grad = rows_low[:queries], rows_low[queries:]
    lengths_row = jnp.pad(decoder_lengths[0], ((0, 0), (0, topk - decoder_lengths.shape[2])))
    integers = shifted(
        jnp.concatenate([retrieved[0], pool_table[0, 0].reshape(-1, topk), lengths_row], 0),
        "section",
        -half_way,
    )
    slots = integers[:queries]
    table = integers[queries:-1].reshape(-1)
    lengths = integers[-1, : decoder_lengths.shape[2]]
    owners = pool_table.shape[2]

    qkv, context, context_low, stats, mixed = encoder_attend(
        x, encoder_inward, encoder_outward, encoder_biases
    )
    hidden, slope, summed, states = encoder_feed(
        mixed,
        encoder_norms,
        encoder_expand,
        encoder_expand_bias,
        encoder_shrink,
        encoder_shrink_bias,
    )
    picked = pick_rows(table, states).reshape(owners, -1, WIDTH)
    pooled = lax.all_to_all(picked, "dp", split_axis=0, concat_axis=0, tiled=True)
    pooled = pooled.reshape(-1, WIDTH)

    mask_across, mask_down = slot_mask(slots, pooled.shape[0])
    self_qkv, self_context, self_mixed, cross_q = self_forward(
        lengths, y, self_inward, self_outward, decoder_biases, decoder_norms, cross_inward
    )
    kv, cross_context, cross_stats = cross_forward(
        pooled, cross_q, mask_across, cross_inward, decoder_biases
    )
    (out, joined_back, dc, mid_vec, mid_expand), d_feed, d_cross_out = middle(
        self_mixed,
        cross_context,
        cross_outward,
        decoder_biases,
        decoder_norms,
        decoder_expand,
        decoder_expand_bias,
        decoder_shrink,
        decoder_shrink_bias,
        grad,
    )
    d_feed = lax.psum_scatter(d_feed, "dp", scatter_dimension=0, tiled=True)[0]
    dkv, dq, cross_vec, dpool = cross_back(
        kv, cross_q, cross_context, dc, cross_stats, mask_down, cross_inward
    )
    returned = lax.all_to_all(
        dpool.reshape(owners, -1, WIDTH), "dp", split_axis=0, concat_axis=0, tiled=True
    )
    d_cross_in = cross_grads(pooled, dkv, self_mixed, dq, decoder_norms)
    (dy, self_vec), d_self = self_back(
        lengths,
        y,
        self_mixed,
        joined_back,
        dq,
        self_qkv,
        self_context,
        self_inward,
        self_outward,
        cross_inward,
        decoder_norms,
    )
    states_back = spread_rows(table, returned.reshape(-1, WIDTH), x.shape[0])

    hosts = paired()
    plan = feed_plan([like(out.shape, out.dtype), like(dy.shape, dy.dtype)]) if hosts else None
    pairs = (d_cross_in, d_cross_out, d_self)
    guests = [pair[k] for k in range(2) for pair in pairs] + [out, dy] if hosts else []
    (dmix, feed_vec, feed_expand), (e_expand, e_shrink, e_out), from_feed = encoder_feed_back(
        states_back,
        summed,
        mixed,
        hidden,
        slope,
        context_low,
        encoder_norms,
        encoder_expand,
        encoder_shrink,
        plan,
        guests,
    )
    if hosts:
        decoder_out, decoder_grad = from_feed[1:]
    else:
        decoder_out = shifted(out, "section", half_way)
        decoder_grad = shifted(dy, "section", half_way)
    rest = [
        jnp.concatenate([jnp.zeros((2, WIDTH), wide_type), feed_vec[5:6]], 0),
        jnp.stack([feed_vec[3:5], feed_vec[0:2]]),
        feed_expand[0],
        feed_vec[2],
        jnp.concatenate([self_vec[3:5], self_vec[2:3], cross_vec[0:2], mid_vec[5:6]], 0),
        jnp.stack([self_vec[0:2], mid_vec[3:5], mid_vec[0:2]]),
        mid_expand[0],
        mid_vec[2],
    ]
    plan = attend_plan() if hosts else None
    if hosts:
        guests = [pair[k] for k in range(2) for pair in (d_self, e_expand, e_shrink)]
        flat = jnp.concatenate([v.reshape(-1) for v in rest])
        flat = jnp.pad(flat, (0, 32 * WIDTH - flat.size)).reshape(32, WIDTH)
        guests.append(flat)
        early, dmix = lax.optimization_barrier(((d_feed, from_feed[0]), dmix))
        early = lax.psum(early, "section")
    (dx, attend_vec), e_in, from_attend = encoder_attend_back(
        dmix, x, qkv, context, stats, encoder_inward, encoder_outward, plan, guests
    )
    if hosts:
        last, vector = last_sums(last_plan(), (e_in, e_out), from_attend[:1], attend_vec)
        results = unpack(*early, last, from_attend[1], vector)
        results = [r[0] if n in (5, 7, 15, 17) else r for n, r in enumerate(results)]
    else:
        results = sum_any(
            [e_in, e_out, e_expand, e_shrink, d_self, d_cross_in, d_cross_out],
            d_feed,
            [rest[0] + jnp.pad(attend_vec[0:2], ((0, 1), (0, 0)))] + rest[1:],
        )
    return (decoder_out[None], dx[None], decoder_grad[None], *results)


def solution(mesh):
    in_specs = (
        P("section", "dp", None),
        P("section", "dp", None),
        P("section", "dp", None),
        P("section", "dp", None, None),
        P("section", "dp", None),
        P("section", "dp", None),
        P(),
        P(),
        P(),
        P(),
        P(),
        P(),
        P(),
        P(),
        P(),
        P(),
        P(),
        P(),
        P(),
        P(),
        P(),
        P(),
        P(),
        P(),
    )
    out_specs = (
        P("section", "dp", None),
        P("section", "dp", None),
        P("section", "dp", None),
        P(None, "dp", None),
        P("dp", None),
        P(None, "dp"),
        P(None, None, "dp"),
        P("dp", None),
        P("dp"),
        P("dp", None),
        P("dp"),
        P(None, "dp", None),
        P("dp", None),
        P(None, "dp", None),
        P("dp", None),
        P(None, "dp"),
        P(None, None, "dp"),
        P("dp", None),
        P("dp"),
        P("dp", None),
        P("dp"),
    )
    return jax.shard_map(
        on_device, mesh=mesh, in_specs=in_specs, out_specs=out_specs, check_vma=False
    )
```

```python
import functools

import jax
import jax.numpy as jnp
from jax import lax
from jax.experimental import pallas as pl
from jax.experimental.pallas import tpu as pltpu
from jax.sharding import PartitionSpec as P

HEAD = 64
WIDTH = 768


norm_eps = 1e-05
scale_scores = 0.125
low_type = jnp.bfloat16
wide_type = jnp.float32

NN = (((1,), (0,)), ((), ()))
NT = (((1,), (1,)), ((), ()))
TN = (((0,), (0,)), ((), ()))
GROUP = 256
VMEM = pltpu.VMEM


def dot(left, right, dims=NN):
    return lax.dot_general(left, right, dims, preferred_element_type=wide_type)


def low(value):
    return value.astype(low_type)


def wide(value):
    return value.astype(wide_type)


def head_lanes(dtype):
    lane = lax.broadcasted_iota(jnp.int32, (1, GROUP), 1) // HEAD
    return [(lane == h).astype(wide_type).astype(dtype) for h in range(GROUP // HEAD)]


def centred_of(values):
    centred = values - jnp.mean(values, -1, keepdims=True)
    spread = jnp.mean(centred * centred, -1, keepdims=True)
    return centred, lax.rsqrt(spread + norm_eps)


def norm_rows(values, gain, offset):
    centred, scale = centred_of(values)
    return centred * scale * (1.0 + gain) + offset


def norm_rows_back(values, gain, incoming):
    centred, scale = centred_of(values)
    unit = centred * scale
    inner = incoming * (1.0 + gain)
    mean_inner = jnp.mean(inner, -1, keepdims=True)
    mean_along = jnp.mean(inner * unit, -1, keepdims=True)
    return (
        scale * (inner - mean_inner - unit * mean_along),
        jnp.sum(incoming * unit, 0, keepdims=True),
        jnp.sum(incoming, 0, keepdims=True),
    )


def gelu_parts(u):
    size = jnp.abs(u) * 0.7071067811865476
    t = 1.0 / (1.0 + 0.3275911 * size)
    bell = jnp.exp(-0.5 * u * u)
    series = t * (
        0.254829592
        + t * (-0.284496736 + t * (1.421413741 + t * (-1.453152027 + t * 1.061405429)))
    )
    tail = 0.5 * series * bell
    share = jnp.where(u < 0.0, tail, 1.0 - tail)
    return u * share, share + u * (bell * 0.3989422804014327)


def params(limit=60, **rest):
    return pltpu.CompilerParams(vmem_limit_bytes=limit * 2**20, **rest)


def host_params(plan):
    if plan:
        return params(62, collective_id=plan.collective_id, has_side_effects=True)
    return params()


def cost(flops, size, exps=0):
    return pl.CostEstimate(flops=int(flops), bytes_accessed=int(size), transcendentals=int(exps))


def full(*shape):
    return pl.BlockSpec(shape, lambda *_: (0,) * len(shape))


def once(*shape):
    return pl.BlockSpec(shape, lambda *_: (0,) * len(shape), pipeline_mode=pl.Buffered(1))


def like(shape, dtype):
    return jax.ShapeDtypeStruct(shape, dtype)


def paired():
    return lax.axis_size("dp") == 8


def grad_shapes(parts, rows, columns):
    if paired():
        return [like((4, parts * rows // 8, columns), low_type)] * 2
    return [like((parts, rows, columns), low_type)]


def grad_specs(parts, rows, columns, index=None):
    if paired():
        block, count = (4, parts * rows // 8, columns), 2
    else:
        block, count = (parts, rows, columns), 1
    return [pl.BlockSpec(block, index or (lambda *_: (0, 0, 0)))] * count


def emit(outs, part, hold):
    if len(outs) == 1:
        outs[0][part] = low(hold[...])
        return
    keep, send = outs
    me = lax.axis_index("dp")
    rows = hold.shape[0] // 8
    to = pl.ds(pl.multiple_of(part * rows, rows), rows)
    for at in range(4):
        mine = pl.multiple_of((me ^ (2 * at)) * rows, rows)
        other = pl.multiple_of((me ^ (2 * at + 1)) * rows, rows)
        keep[at, to, :] = low(hold[pl.ds(mine, rows), :])
        send[at, to, :] = low(hold[pl.ds(other, rows), :])


def emit_tall(outs, block, hold):
    if len(outs) == 1:
        size = hold.shape[0]
        outs[0][0, pl.ds(pl.multiple_of(block * size, size), size), :] = low(hold[...])
        return
    keep, send = outs
    me = lax.axis_index("dp")
    rows = hold.shape[0] // 2
    at = block ^ lax.shift_right_logical(me, 1)
    core = me & 1
    keep[at, 0:rows, :] = low(hold[pl.ds(pl.multiple_of(core * rows, rows), rows), :])
    send[at, 0:rows, :] = low(hold[pl.ds(pl.multiple_of((1 - core) * rows, rows), rows), :])


def thirds(items):
    third = len(items) // 3
    return items[:third], items[third : 2 * third], items[2 * third :]


def encoder_attend_kernel(
    x_ref, w_ref, wo_ref, bg_ref, b_ref, qkv_ref, c_ref, cl_ref, stat_ref, mixed_ref, stats
):
    group = pl.program_id(0)
    tokens = x_ref.shape[0]
    block = 512
    x = x_ref[...]
    qkv_ref[0] = low(dot(x, w_ref[0]) + bg_ref[0:1])
    qkv_ref[1] = low(dot(x, w_ref[1]))
    qkv_ref[2] = low(dot(x, w_ref[2]) + bg_ref[1:2])
    lanes_low, lanes = head_lanes(low_type), head_lanes(wide_type)
    lane = lax.broadcasted_iota(jnp.int32, (1, 128), 1)

    @pl.when(group == 0)
    def _():
        mixed_ref[...] = wide(x) + b_ref[2:3]

    def rows_step(i, carry):
        rows = pl.ds(pl.multiple_of(i * block, block), block)
        q = qkv_ref[0, rows, :] * jnp.asarray(scale_scores, low_type)
        context = jnp.zeros((block, GROUP), wide_type)
        stat = jnp.zeros((block, 128), wide_type)
        for h in range(GROUP // HEAD):
            scores = dot(q * lanes_low[h], qkv_ref[1], NT)
            top = jnp.max(scores, -1, keepdims=True)
            weights = jnp.exp(scores - top)
            total = jnp.sum(weights, -1, keepdims=True)
            context += dot(low(weights), qkv_ref[2]) * (lanes[h] * (1.0 / total))
            stat = jnp.where(lane == h, top + jnp.log(total), stat)
        c_ref[rows, :] = context
        cl_ref[rows, :] = low(context)
        stats[rows, :] = stat
        mixed_ref[rows, :] += dot(low(context), wo_ref[...])
        return carry

    lax.fori_loop(0, tokens // block, rows_step, 0)
    stat_ref[0] = stats[...].T[0:8]


def encoder_attend(x, inward, outward, biases):
    tokens, width = x.shape
    groups = width // GROUP
    return pl.pallas_call(
        encoder_attend_kernel,
        grid=(groups,),
        in_specs=[
            full(tokens, width),
            pl.BlockSpec((3, width, GROUP), lambda g: (0, 0, g)),
            pl.BlockSpec((GROUP, width), lambda g: (g, 0)),
            pl.BlockSpec((3, GROUP), lambda g: (0, g)),
            full(3, width),
        ],
        out_specs=[
            pl.BlockSpec((3, tokens, GROUP), lambda g: (0, 0, g)),
            pl.BlockSpec((tokens, GROUP), lambda g: (0, g)),
            pl.BlockSpec((tokens, GROUP), lambda g: (0, g)),
            pl.BlockSpec((1, 8, tokens), lambda g: (g, 0, 0)),
            full(tokens, width),
        ],
        out_shape=[
            like((3, tokens, width), low_type),
            like((tokens, width), wide_type),
            like((tokens, width), low_type),
            like((groups, 8, tokens), wide_type),
            like((tokens, width), wide_type),
        ],
        scratch_shapes=[VMEM((tokens, 128), wide_type)],
        compiler_params=params(),
        cost_estimate=cost(3e10, 2e7, 1.3e7),
        name="encoder_attend",
    )(x, inward, outward, biases, biases)


def encoder_feed_kernel(
    mixed_ref, n_ref, e_ref, eb_ref, s_ref, sb_ref, h_ref, d_ref, sum_ref, out_ref, a_low
):
    step = pl.program_id(0)
    tokens = mixed_ref.shape[0]
    block = 256

    @pl.when(step == 0)
    def _():
        def rows_step(i, carry):
            rows = pl.ds(pl.multiple_of(i * 256, 256), 256)
            first = norm_rows(mixed_ref[rows, :], n_ref[0, 0:1], n_ref[0, 1:2])
            a_low[rows, :] = low(first)
            sum_ref[rows, :] = first + sb_ref[...]
            return carry

        lax.fori_loop(0, tokens // 256, rows_step, 0)

    for i in range(tokens // block):
        rows = slice(i * block, (i + 1) * block)
        hidden, slope = gelu_parts(dot(a_low[rows, :], e_ref[...]) + eb_ref[...])
        h_ref[rows, :] = low(hidden)
        d_ref[rows, :] = low(slope)
        sum_ref[rows, :] += dot(low(hidden), s_ref[...])

    @pl.when(step == pl.num_programs(0) - 1)
    def _():
        def rows_step(i, carry):
            rows = pl.ds(pl.multiple_of(i * 256, 256), 256)
            out_ref[rows, :] = low(norm_rows(sum_ref[rows, :], n_ref[1, 0:1], n_ref[1, 1:2]))
            return carry

        lax.fori_loop(0, tokens // 256, rows_step, 0)


def encoder_feed(mixed, norms, expand, expand_bias, shrink, shrink_bias):
    tokens, width = mixed.shape
    hidden = expand.shape[1]
    cut = hidden // 4
    return pl.pallas_call(
        encoder_feed_kernel,
        grid=(4,),
        in_specs=[
            full(tokens, width),
            full(2, 2, width),
            pl.BlockSpec((width, cut), lambda i: (0, i)),
            pl.BlockSpec((1, cut), lambda i: (0, i)),
            pl.BlockSpec((cut, width), lambda i: (i, 0)),
            full(1, width),
        ],
        out_specs=[
            pl.BlockSpec((tokens, cut), lambda i: (0, i)),
            pl.BlockSpec((tokens, cut), lambda i: (0, i)),
            full(tokens, width),
            full(tokens, width),
        ],
        out_shape=[
            like((tokens, hidden), low_type),
            like((tokens, hidden), low_type),
            like((tokens, width), wide_type),
            like((tokens, width), low_type),
        ],
        scratch_shapes=[VMEM((tokens, width), low_type)],
        compiler_params=params(),
        cost_estimate=cost(2e10, 3e7, 3e6),
        name="encoder_feed",
    )(mixed, norms, expand, expand_bias[None], shrink, shrink_bias[None])


def split_refs(refs, *counts):
    out, at = [], 0
    for count in counts:
        out.append(refs[at : at + count])
        at += count
    return out + [refs[at:]]


def hosting(plan):
    return (plan.ins, len(plan.outs())) if plan else (0, 0)


def encoder_feed_back_kernel(plan, *refs):
    grads = 6 if paired() else 3
    host_ins, host_outs = hosting(plan)
    main, guests, outs, guest_outs, scratch, guest_scratch = split_refs(
        refs, 9, host_ins, 3 + grads, host_outs, 4
    )
    g_ref, sum_ref, mixed_ref, h_ref, d_ref, c_ref, n_ref, e_ref, s_ref = main
    dmix_ref, vec_ref, eb_ref = outs[:3]
    wide_outs, tall_outs, out_outs = thirds(outs[3:])
    back_low, a_turned, between, hold = scratch
    step = pl.program_id(0)
    sums = plan.open(guests, guest_outs, guest_scratch) if plan else None

    def place(n):
        if sums:
            sums.slot(step, 4, 3, n)

    place(0)
    tokens = sum_ref.shape[0]
    block = 256

    @pl.when(step == 0)
    def _():
        vec_ref[...] = jnp.zeros(vec_ref.shape, wide_type)

        def rows_step(i, carry):
            rows = pl.ds(pl.multiple_of(i * 256, 256), 256)
            grad, gain, offset = norm_rows_back(
                sum_ref[rows, :], n_ref[1, 0:1], wide(g_ref[rows, :])
            )
            dmix_ref[rows, :] = grad
            back_low[rows, :] = low(grad)
            vec_ref[0:1] += gain
            vec_ref[1:2] += offset
            vec_ref[2:3] += jnp.sum(wide(low(grad)), 0, keepdims=True)
            first = norm_rows(mixed_ref[rows, :], n_ref[0, 0:1], n_ref[0, 1:2])
            a_turned[:, rows] = low(first).T
            return carry

        lax.fori_loop(0, tokens // 256, rows_step, 0)

    column = jnp.zeros(eb_ref.shape, wide_type)
    for i in range(tokens // block):
        rows = slice(i * block, (i + 1) * block)
        before = low(dot(back_low[rows, :], s_ref[...], NT) * wide(d_ref[rows, :]))
        between[rows, :] = before
        column += jnp.sum(wide(before), 0, keepdims=True)
        dmix_ref[rows, :] += dot(before, e_ref[...], NT)
        if i == 1:
            place(1)
    eb_ref[...] = column
    hold[...] = dot(a_turned[...], between[...])
    emit(wide_outs, step, hold)
    hold[...] = dot(h_ref[...], back_low[...], TN)
    emit_tall(tall_outs, step, hold)

    @pl.when(step == pl.num_programs(0) - 1)
    def _():

        def rows_step(i, carry):
            rows = pl.ds(pl.multiple_of(i * 256, 256), 256)
            grad, gain, offset = norm_rows_back(
                mixed_ref[rows, :], n_ref[0, 0:1], dmix_ref[rows, :]
            )
            dmix_ref[rows, :] = grad
            back_low[rows, :] = low(grad)
            vec_ref[3:4] += gain
            vec_ref[4:5] += offset
            vec_ref[5:6] += jnp.sum(wide(low(grad)), 0, keepdims=True)
            return carry

        lax.fori_loop(0, tokens // 256, rows_step, 0)
        hold[...] = dot(c_ref[...], back_low[...], TN)
        emit(out_outs, 0, hold)

    place(2)


def encoder_feed_back(
    grad, summed, mixed, hidden, slope, context, norms, expand, shrink, plan=None, guests=()
):
    tokens, width = mixed.shape
    total = expand.shape[1]
    cut = total // 4
    guest_outs = plan.outs() if plan else []
    outs = pl.pallas_call(
        functools.partial(encoder_feed_back_kernel, plan),
        grid=(4,),
        in_specs=[
            once(tokens, width),
            once(tokens, width),
            once(tokens, width),
            pl.BlockSpec((tokens, cut), lambda i: (0, i)),
            pl.BlockSpec((tokens, cut), lambda i: (0, i)),
            once(tokens, width),
            full(2, 2, width),
            pl.BlockSpec((width, cut), lambda i: (0, i)),
            pl.BlockSpec((cut, width), lambda i: (i, 0)),
            *(plan.in_specs() if plan else []),
        ],
        out_specs=[
            full(tokens, width),
            full(8, width),
            pl.BlockSpec((1, cut), lambda i: (0, i)),
            *grad_specs(4, width, width),
            *grad_specs(1, total, width),
            *grad_specs(1, width, width),
            *[spec for spec, _ in guest_outs],
        ],
        out_shape=[
            like((tokens, width), wide_type),
            like((8, width), wide_type),
            like((1, total), wide_type),
            *grad_shapes(4, width, width),
            *grad_shapes(1, total, width),
            *grad_shapes(1, width, width),
            *[shape for _, shape in guest_outs],
        ],
        scratch_shapes=[
            VMEM((tokens, width), low_type),
            VMEM((width, tokens), low_type),
            VMEM((tokens, cut), low_type),
            VMEM((width, width), wide_type),
            *(plan.scratch() if plan else []),
        ],
        compiler_params=host_params(plan),
        cost_estimate=cost(4e10, 5e7),
        name="encoder_feed_back",
    )(grad, summed, mixed, hidden, slope, context, norms, expand, shrink, *guests)
    main = len(outs) - len(guest_outs)
    return outs[:3], thirds(outs[3:main]), outs[main:]


def encoder_attend_back_kernel(plan, *refs):
    host_ins, host_outs = hosting(plan)
    main, guests, (dx_ref, vec_ref), outs, guest_outs, scratch, guest_scratch = split_refs(
        refs, 7, host_ins, 2, 2 if paired() else 1, host_outs, 9
    )
    dmix_ref, x_ref, qkv_ref, c_ref, stat_ref, w_ref, wo_ref = main
    dmix_low, x_turned, dc, weights, scores_back, dk, dv, dq_turned, hold = scratch
    group = pl.program_id(0)
    sums = plan.open(guests, guest_outs, guest_scratch) if plan else None

    def place(n):
        if sums:
            sums.slot(group, 3, 3, n)

    place(0)
    tokens = x_ref.shape[0]
    block = 512
    heads = GROUP // HEAD

    @pl.when(group == 0)
    def _():
        dx_ref[...] = dmix_ref[...]
        dmix_low[...] = low(dmix_ref[...])
        x_turned[...] = x_ref[...].T

    dc[...] = low(dot(dmix_low[...], wo_ref[...], NT))
    lanes_low = head_lanes(low_type)
    eighth = jnp.asarray(scale_scores, low_type)
    pick = (
        lax.broadcasted_iota(jnp.int32, (8, GROUP), 1) // HEAD
        == lax.broadcasted_iota(jnp.int32, (8, GROUP), 0)
    ).astype(wide_type)
    pick = low(pick)
    product = wide(dc[...]) * c_ref[...]
    product_high = low(product)
    product_rest = low(product - wide(product_high))
    inner = dot(pick, product_high, NT) + dot(pick, product_rest, NT)
    k_turned = qkv_ref[1].T
    dk[...] = jnp.zeros(dk.shape, wide_type)
    dv[...] = jnp.zeros(dv.shape, wide_type)
    for i in range(tokens // block):
        rows = slice(i * block, (i + 1) * block)
        q = qkv_ref[0, rows, :] * eighth
        q_heads = jnp.concatenate([q * lanes_low[h] for h in range(heads)], 0)
        dc_heads = jnp.concatenate([dc[rows, :] * lanes_low[h] for h in range(heads)], 0)
        for h in range(heads):
            part = slice(h * block, (h + 1) * block)
            scores = dot(qkv_ref[1], q_heads[part], NT)
            weight = jnp.exp(scores - stat_ref[0, h : h + 1, rows])
            weight_back = dot(qkv_ref[2], dc_heads[part], NT)
            weights[:, part] = low(weight)
            back = low(weight * (weight_back - inner[h : h + 1, rows]))
            scores_back[:, part] = back
            dq_turned[h * HEAD : (h + 1) * HEAD, rows] = dot(
                k_turned[h * HEAD : (h + 1) * HEAD], back
            )
        dv[...] += dot(weights[...], dc_heads)
        dk[...] += dot(scores_back[...], q_heads)
        if i == 0:
            place(1)
    dq = low(dq_turned[...].T * scale_scores)
    dk_low, dv_low = low(dk[...]), low(dv[...])
    vec_ref[...] = jnp.zeros(vec_ref.shape, wide_type)
    vec_ref[0:1] = jnp.sum(wide(dq), 0, keepdims=True)
    vec_ref[1:2] = jnp.sum(wide(dv_low), 0, keepdims=True)
    dx_ref[...] += (
        dot(dq, w_ref[0], NT) + dot(dk_low, w_ref[1], NT) + dot(dv_low, w_ref[2], NT)
    )
    for part, grad in enumerate((dq, dk_low, dv_low)):
        hold[...] = dot(x_turned[...], grad)
        emit(outs, part, hold)
    place(2)


def encoder_attend_back(
    dmix, x, qkv, context, stats, inward, outward, plan=None, guests=()
):
    tokens, width = x.shape
    groups = width // GROUP
    specs = grad_specs(3, width, GROUP, lambda g: (0, 0, g))
    guest_outs = plan.outs() if plan else []
    outs = pl.pallas_call(
        functools.partial(encoder_attend_back_kernel, plan),
        grid=(groups,),
        in_specs=[
            once(tokens, width),
            once(tokens, width),
            pl.BlockSpec((3, tokens, GROUP), lambda g: (0, 0, g)),
            pl.BlockSpec((tokens, GROUP), lambda g: (0, g)),
            pl.BlockSpec((1, 8, tokens), lambda g: (g, 0, 0)),
            pl.BlockSpec((3, width, GROUP), lambda g: (0, 0, g)),
            pl.BlockSpec((GROUP, width), lambda g: (g, 0)),
            *(plan.in_specs() if plan else []),
        ],
        out_specs=[
            full(tokens, width),
            pl.BlockSpec((8, GROUP), lambda g: (0, g)),
            *specs,
            *[spec for spec, _ in guest_outs],
        ],
        out_shape=[
            like((tokens, width), wide_type),
            like((8, width), wide_type),
            *grad_shapes(3, width, width),
            *[shape for _, shape in guest_outs],
        ],
        scratch_shapes=[
            VMEM((tokens, width), low_type),
            VMEM((width, tokens), low_type),
            VMEM((tokens, GROUP), low_type),
            VMEM((tokens, 4 * 512), low_type),
            VMEM((tokens, 4 * 512), low_type),
            VMEM((tokens, GROUP), wide_type),
            VMEM((tokens, GROUP), wide_type),
            VMEM((GROUP, tokens), wide_type),
            VMEM((width, GROUP), wide_type),
            *(plan.scratch() if plan else []),
        ],
        compiler_params=host_params(plan),
        cost_estimate=cost(5e10, 4e7, 1.3e7),
        name="encoder_attend_back",
    )(dmix, x, qkv, context, stats, inward, outward, *guests)
    main = len(outs) - len(guest_outs)
    return outs[:2], outs[2:main], outs[main:]


def mask_kernel(slots_ref, across_ref, down_ref):
    count, width = slots_ref.shape
    words = down_ref.shape[0] // 32
    block = 32
    row = lax.broadcasted_iota(jnp.int32, (32, width), 0)
    for start in range(0, words, block):

        def step(i, totals):
            piece = slots_ref[pl.ds(pl.multiple_of(i * 8, 8), 8), :]
            word = lax.shift_right_logical(piece, 5)
            bit = jnp.left_shift(jnp.int32(1), piece & 31)
            return tuple(
                total | jnp.where(word == start + w, bit, 0) for w, total in enumerate(totals)
            )

        zero = jnp.zeros((8, width), jnp.int32)
        totals = lax.fori_loop(0, count // 8, step, (zero,) * block)
        for w, total in enumerate(totals):
            joined = total[0:1]
            for k in range(1, 8):
                joined = joined | total[k : k + 1]
            bits = lax.shift_right_logical(jnp.broadcast_to(joined, (32, width)), row) & 1
            at = (start + w) * 32
            down_ref[at : at + 32, :] = (wide(bits) - 1.0) * 1e30
    across_ref[...] = down_ref[...].T


def slot_mask(slots, pool):
    queries = slots.shape[0]
    return pl.pallas_call(
        mask_kernel,
        out_shape=[like((queries, pool), wide_type), like((pool, queries), wide_type)],
        in_specs=[pl.BlockSpec(memory_space=VMEM)],
        out_specs=[pl.BlockSpec(memory_space=VMEM)] * 2,
        compiler_params=params(24),
        cost_estimate=cost(1e10, 1e6),
        name="slot_mask",
    )(slots.T)


def pick_kernel(table_ref, states_ref, out_ref):
    spot = lax.broadcasted_iota(jnp.int32, (table_ref.shape[0], states_ref.shape[0]), 1)
    chosen = low((spot == table_ref[...]).astype(wide_type))
    out_ref[...] = low(dot(chosen, states_ref[...]))


def pick_rows(table, states):
    tokens, width = states.shape
    return pl.pallas_call(
        pick_kernel,
        grid=(table.size // 256,),
        in_specs=[pl.BlockSpec((256, 1), lambda i: (i, 0)), full(tokens, width)],
        out_specs=pl.BlockSpec((256, width), lambda i: (i, 0)),
        out_shape=like((table.size, width), low_type),
        compiler_params=params(24),
        cost_estimate=cost(4e9, 5e6),
        name="pick_rows",
    )(table.reshape(-1, 1), states)


def spread_kernel(table_ref, rows_ref, out_ref, total):
    step = pl.program_id(0)
    spot = lax.broadcasted_iota(jnp.int32, (out_ref.shape[0], table_ref.shape[1]), 0)
    chosen = low((spot == table_ref[...]).astype(wide_type))
    part = dot(chosen, rows_ref[...])

    @pl.when(step == 0)
    def _():
        total[...] = part

    @pl.when(step != 0)
    def _():
        total[...] += part

    @pl.when(step == pl.num_programs(0) - 1)
    def _():
        out_ref[...] = low(total[...])


def spread_rows(table, rows, tokens):
    width = rows.shape[1]
    return pl.pallas_call(
        spread_kernel,
        grid=(table.size // 512,),
        in_specs=[
            pl.BlockSpec((1, 512), lambda i: (0, i)),
            pl.BlockSpec((512, width), lambda i: (i, 0)),
        ],
        out_specs=full(tokens, width),
        out_shape=like((tokens, width), low_type),
        scratch_shapes=[VMEM((tokens, width), wide_type)],
        compiler_params=params(24),
        cost_estimate=cost(4e9, 5e6),
        name="spread_rows",
    )(table.reshape(1, -1), rows)


def by_head(value, lanes):
    return jnp.concatenate([value * lane for lane in lanes], 0)


def own_lanes(stacked, lanes):
    rows = stacked.shape[0] // len(lanes)
    return sum(stacked[h * rows : (h + 1) * rows] * lane for h, lane in enumerate(lanes))


def softmax_rows(scores):
    top = jnp.max(scores, -1, keepdims=True)
    weights = jnp.exp(scores - top)
    return weights * (1.0 / jnp.sum(weights, -1, keepdims=True))


def self_mask(lengths_ref, size):
    row = lax.broadcasted_iota(jnp.int32, (size, size), 0)
    column = lax.broadcasted_iota(jnp.int32, (size, size), 1)
    row_part, column_part = jnp.zeros_like(row), jnp.zeros_like(row)
    end = jnp.int32(0)
    for n in range(lengths_ref.shape[0] - 1):
        end = end + lengths_ref[n]
        row_part += (row >= end).astype(jnp.int32)
        column_part += (column >= end).astype(jnp.int32)
    allowed = (row_part == column_part) & (column <= row)
    added = jnp.where(allowed, 0.0, -1e30)
    return jnp.concatenate([added] * (GROUP // HEAD), 0)


def groups_of(width):
    return [slice(g, g + GROUP) for g in range(0, width, GROUP)]


def self_kernel(
    lengths_ref, y_ref, w_ref, wo_ref, b_ref, n_ref, cw_ref, qkv_ref, c_ref, mixed_ref, cq_ref
):
    y = y_ref[...]
    lanes_low, lanes = head_lanes(low_type), head_lanes(wide_type)
    mask = self_mask(lengths_ref, y.shape[0])
    qkv_ref[0] = low(dot(y, w_ref[0]) + b_ref[0:1])
    qkv_ref[1] = low(dot(y, w_ref[1]))
    qkv_ref[2] = low(dot(y, w_ref[2]) + b_ref[1:2])
    for part in groups_of(y.shape[1]):
        q = qkv_ref[0, :, part] * jnp.asarray(scale_scores, low_type)
        scores = dot(by_head(q, lanes_low), qkv_ref[1, :, part], NT) + mask
        weights = low(softmax_rows(scores))
        c_ref[:, part] = low(own_lanes(dot(weights, qkv_ref[2, :, part]), lanes))
    mixed = wide(y) + (dot(c_ref[...], wo_ref[...]) + b_ref[2:3])
    mixed_ref[...] = mixed
    first = low(norm_rows(mixed, n_ref[0, 0:1], n_ref[0, 1:2]))
    cq_ref[...] = low(dot(first, cw_ref[0]) + b_ref[3:4])


def self_forward(lengths, y, inward, outward, biases, norms, cross_inward):
    rows, width = y.shape
    return pl.pallas_call(
        self_kernel,
        grid=(1,),
        in_specs=[
            pl.BlockSpec(memory_space=pltpu.SMEM),
            full(rows, width),
            full(3, width, width),
            full(width, width),
            full(6, width),
            full(3, 2, width),
            full(1, width, width),
        ],
        out_specs=[
            full(3, rows, width),
            full(rows, width),
            full(rows, width),
            full(rows, width),
        ],
        out_shape=[
            like((3, rows, width), low_type),
            like((rows, width), low_type),
            like((rows, width), wide_type),
            like((rows, width), low_type),
        ],
        compiler_params=params(40),
        cost_estimate=cost(2e10, 7e6),
        name="self_forward",
    )(lengths, y, inward, outward, biases, norms, cross_inward)


def cross_kernel(pooled_ref, q_ref, mask_ref, w_ref, bg_ref, kv_ref, c_ref, stat_ref, scores, weights):
    rows = q_ref.shape[0]
    heads = GROUP // HEAD
    lanes_low, lanes = head_lanes(low_type), head_lanes(wide_type)
    kv_ref[0] = low(dot(pooled_ref[...], w_ref[1]))
    kv_ref[1] = low(dot(pooled_ref[...], w_ref[2]) + bg_ref[4:5])
    q = q_ref[...] * jnp.asarray(scale_scores, low_type)
    scores[...] = dot(by_head(q, lanes_low), kv_ref[0], NT)
    stats, scales = [], []
    for h in range(heads):
        part = slice(h * rows, (h + 1) * rows)
        masked = scores[part, :] + mask_ref[...]
        top = jnp.max(masked, -1, keepdims=True)
        weight = jnp.exp(masked - top)
        total = jnp.sum(weight, -1, keepdims=True)
        weights[part, :] = low(weight)
        stats.append(top + jnp.log(total))
        scales.append(lanes[h] * (1.0 / total))
    mixed = dot(weights[...], kv_ref[1])
    c_ref[...] = sum(mixed[h * rows : (h + 1) * rows] * scales[h] for h in range(heads))
    column = jnp.concatenate(stats, 0)
    stat_ref[0] = jnp.broadcast_to(column, (heads * rows, 128)).T[0:8]


def cross_forward(pooled, q, mask, inward, biases):
    slots, width = pooled.shape
    rows = q.shape[0]
    groups = width // GROUP
    stacked = rows * (GROUP // HEAD)
    return pl.pallas_call(
        cross_kernel,
        grid=(groups,),
        in_specs=[
            full(slots, width),
            pl.BlockSpec((rows, GROUP), lambda g: (0, g)),
            full(rows, slots),
            pl.BlockSpec((3, width, GROUP), lambda g: (0, 0, g)),
            pl.BlockSpec((6, GROUP), lambda g: (0, g)),
        ],
        out_specs=[
            pl.BlockSpec((2, slots, GROUP), lambda g: (0, 0, g)),
            pl.BlockSpec((rows, GROUP), lambda g: (0, g)),
            pl.BlockSpec((1, 8, stacked), lambda g: (g, 0, 0)),
        ],
        out_shape=[
            like((2, slots, width), low_type),
            like((rows, width), wide_type),
            like((groups, 8, stacked), wide_type),
        ],
        scratch_shapes=[VMEM((stacked, slots), wide_type), VMEM((stacked, slots), low_type)],
        compiler_params=params(),
        cost_estimate=cost(2e10, 1.2e7, 3e6),
        name="cross_forward",
    )(pooled, q, mask, inward, biases)


def middle_kernel(
    mixed_ref, c_ref, co_ref, b_ref, n_ref, e_ref, eb_ref, s_ref, sb_ref, grad_ref, *rest
):
    out_ref, joined_back_ref, dc_ref, vec_ref, deb_ref = rest[:5]
    hidden, slope, between, hold = rest[-4:]
    feed_ref, out_outs = rest[5], rest[6:-4]
    parts = feed_ref.shape[0]
    width = mixed_ref.shape[1]
    blocks = [slice(i * width, (i + 1) * width) for i in range(e_ref.shape[1] // width)]
    first = norm_rows(mixed_ref[...], n_ref[0, 0:1], n_ref[0, 1:2])
    context = low(c_ref[...])
    joined = first + (dot(context, co_ref[...]) + b_ref[5:6])
    second = norm_rows(joined, n_ref[1, 0:1], n_ref[1, 1:2])
    second_low = low(second)
    total = jnp.zeros(joined.shape, wide_type)
    for part in blocks:
        value, rate = gelu_parts(dot(second_low, e_ref[:, part]) + eb_ref[:, part])
        hidden[:, part] = low(value)
        slope[:, part] = rate
        total += dot(hidden[:, part], s_ref[part, :])
    summed = second + (total + sb_ref[...])
    out_ref[...] = low(norm_rows(summed, n_ref[2, 0:1], n_ref[2, 1:2]))
    summed_back, gain, offset = norm_rows_back(summed, n_ref[2, 0:1], wide(grad_ref[...]))
    summed_low = low(summed_back)
    vec_ref[...] = jnp.zeros(vec_ref.shape, wide_type)
    vec_ref[0:1] = gain
    vec_ref[1:2] = offset
    vec_ref[2:3] = jnp.sum(wide(summed_low), 0, keepdims=True)
    second_back = summed_back
    for part in blocks:
        before = low(dot(summed_low, s_ref[part, :], NT) * slope[:, part])
        between[:, part] = before
        deb_ref[:, part] = jnp.sum(wide(before), 0, keepdims=True)
        second_back += dot(before, e_ref[:, part], NT)
    joined_back, gain, offset = norm_rows_back(joined, n_ref[1, 0:1], second_back)
    joined_low = low(joined_back)
    joined_back_ref[...] = joined_back
    vec_ref[3:4] = gain
    vec_ref[4:5] = offset
    vec_ref[5:6] = jnp.sum(wide(joined_low), 0, keepdims=True)
    dc_ref[...] = low(dot(joined_low, co_ref[...], NT))
    for i, part in enumerate(blocks):
        rows = width // parts
        grad = low(dot(second_low, between[:, part], TN))
        for n in range(parts):
            feed_ref[n, i * rows : (i + 1) * rows, :] = grad[n * rows : (n + 1) * rows]
        grad = low(dot(hidden[:, part], summed_low, TN))
        rows, first = 4 * rows, i * parts // 4
        for n in range(parts // 4):
            feed_ref[first + n, rows:, :] = grad[n * rows : (n + 1) * rows]
    hold[...] = dot(context, joined_low, TN)
    emit(out_outs, 0, hold)


def middle(mixed, context, outward, biases, norms, expand, expand_bias, shrink, shrink_bias, grad):
    rows, width = mixed.shape
    total = expand.shape[1]
    parts = lax.axis_size("dp")
    ins = (
        mixed,
        context,
        outward,
        biases,
        norms,
        expand,
        expand_bias[None],
        shrink,
        shrink_bias[None],
        grad,
    )
    outs = pl.pallas_call(
        middle_kernel,
        grid=(1,),
        in_specs=[full(*value.shape) for value in ins],
        out_specs=[
            full(rows, width),
            full(rows, width),
            full(rows, width),
            full(8, width),
            full(1, total),
            full(parts, 2 * total // parts, width),
            *grad_specs(1, width, width),
        ],
        out_shape=[
            like((rows, width), low_type),
            like((rows, width), wide_type),
            like((rows, width), low_type),
            like((8, width), wide_type),
            like((1, total), wide_type),
            like((parts, 2 * total // parts, width), low_type),
            *grad_shapes(1, width, width),
        ],
        scratch_shapes=[
            VMEM((rows, total), low_type),
            VMEM((rows, total), wide_type),
            VMEM((rows, total), low_type),
            VMEM((width, width), wide_type),
        ],
        compiler_params=params(),
        cost_estimate=cost(2e10, 2.2e7),
        name="middle",
    )(*ins)
    return outs[:5], outs[5], outs[6:]


def cross_back_kernel(
    kv_ref, q_ref, c_ref, dc_ref, stat_ref, mask_ref, w_ref, dkv_ref, dq_ref, vec_ref, dpool_ref,
    total, weights, scores_back
):
    group = pl.program_id(0)
    rows = q_ref.shape[0]
    heads = GROUP // HEAD
    lanes_low, lanes = head_lanes(low_type), head_lanes(wide_type)
    q_heads = by_head(q_ref[...] * jnp.asarray(scale_scores, low_type), lanes_low)
    dc_heads = by_head(dc_ref[...], lanes_low)
    product = wide(dc_heads) * jnp.concatenate([c_ref[...]] * heads, 0)
    column = jnp.sum(product, -1, keepdims=True)
    inner = jnp.broadcast_to(column, (heads * rows, 128)).T[0:1]
    stat = stat_ref[0, 0:1]
    mask = jnp.concatenate([mask_ref[...]] * 2, 1)
    for h in range(0, heads, 2):
        part = slice(h * rows, (h + 2) * rows)
        weight = jnp.exp(dot(kv_ref[0], q_heads[part], NT) + mask - stat[:, part])
        weight_back = dot(kv_ref[1], dc_heads[part], NT)
        weights[:, part] = low(weight)
        scores_back[:, part] = low(weight * (weight_back - inner[:, part]))
    dk = low(dot(scores_back[...], q_heads))
    dv = low(dot(weights[...], dc_heads))
    dkv_ref[0] = dk
    dkv_ref[1] = dv
    dq = low(own_lanes(dot(scores_back[...], kv_ref[0], TN), lanes) * scale_scores)
    dq_ref[...] = dq
    vec_ref[...] = jnp.zeros(vec_ref.shape, wide_type)
    vec_ref[0:1] = jnp.sum(wide(dq), 0, keepdims=True)
    vec_ref[1:2] = jnp.sum(wide(dv), 0, keepdims=True)
    part = dot(dk, w_ref[1], NT) + dot(dv, w_ref[2], NT)

    @pl.when(group == 0)
    def _():
        total[...] = part

    @pl.when(group != 0)
    def _():
        total[...] += part

    @pl.when(group == pl.num_programs(0) - 1)
    def _():
        dpool_ref[...] = low(total[...])


def cross_back(kv, q, context, dc, stats, mask, inward):
    slots, width = kv.shape[1:]
    rows = q.shape[0]
    groups = width // GROUP
    stacked = rows * (GROUP // HEAD)
    column = pl.BlockSpec((rows, GROUP), lambda g: (0, g))
    return pl.pallas_call(
        cross_back_kernel,
        grid=(groups,),
        in_specs=[
            pl.BlockSpec((2, slots, GROUP), lambda g: (0, 0, g)),
            column,
            column,
            column,
            pl.BlockSpec((1, 8, stacked), lambda g: (g, 0, 0)),
            full(slots, rows),
            pl.BlockSpec((3, width, GROUP), lambda g: (0, 0, g)),
        ],
        out_specs=[
            pl.BlockSpec((2, slots, GROUP), lambda g: (0, 0, g)),
            column,
            pl.BlockSpec((8, GROUP), lambda g: (0, g)),
            full(slots, width),
        ],
        out_shape=[
            like((2, slots, width), low_type),
            like((rows, width), low_type),
            like((8, width), wide_type),
            like((slots, width), low_type),
        ],
        scratch_shapes=[
            VMEM((slots, width), wide_type),
            VMEM((slots, stacked), low_type),
            VMEM((slots, stacked), low_type),
        ],
        compiler_params=params(),
        cost_estimate=cost(3e10, 2.2e7, 3e6),
        name="cross_back",
    )(kv, q, context, dc, stats, mask, inward)


def cross_grads_kernel(pooled_ref, dkv_ref, mixed_ref, dq_ref, n_ref, *rest):
    outs, (turned, hold) = rest[:-2], rest[-2:]

    @pl.when(pl.program_id(0) == 0)
    def _():
        turned[...] = pooled_ref[...].T

    first = low(norm_rows(mixed_ref[...], n_ref[0, 0:1], n_ref[0, 1:2]))
    hold[...] = dot(first, dq_ref[...], TN)
    emit(outs, 0, hold)
    hold[...] = dot(turned[...], dkv_ref[0])
    emit(outs, 1, hold)
    hold[...] = dot(turned[...], dkv_ref[1])
    emit(outs, 2, hold)


def cross_grads(pooled, dkv, mixed, dq, norms):
    slots, width = pooled.shape
    rows = mixed.shape[0]
    return pl.pallas_call(
        cross_grads_kernel,
        grid=(width // GROUP,),
        in_specs=[
            full(slots, width),
            pl.BlockSpec((2, slots, GROUP), lambda g: (0, 0, g)),
            full(rows, width),
            pl.BlockSpec((rows, GROUP), lambda g: (0, g)),
            full(3, 2, width),
        ],
        out_specs=grad_specs(3, width, GROUP, lambda g: (0, 0, g)),
        out_shape=grad_shapes(3, width, width),
        scratch_shapes=[VMEM((width, slots), low_type), VMEM((width, GROUP), wide_type)],
        compiler_params=params(48),
        cost_estimate=cost(1e10, 1.5e7),
        name="cross_grads",
    )(pooled, dkv, mixed, dq, norms)


def self_back_kernel(
    lengths_ref, y_ref, mixed_ref, jb_ref, cdq_ref, qkv_ref, c_ref, w_ref, wo_ref, cw_ref, n_ref,
    dy_ref, vec_ref, *rest
):
    outs, (dqkv, hold) = rest[:-2], rest[-2:]
    width = y_ref.shape[1]
    y = y_ref[...]
    lanes_low, lanes = head_lanes(low_type), head_lanes(wide_type)
    mask = self_mask(lengths_ref, y.shape[0])
    first_back = jb_ref[...] + dot(cdq_ref[...], cw_ref[0], NT)
    mixed_back, gain, offset = norm_rows_back(mixed_ref[...], n_ref[0, 0:1], first_back)
    mixed_low = low(mixed_back)
    vec_ref[...] = jnp.zeros(vec_ref.shape, wide_type)
    vec_ref[0:1] = gain
    vec_ref[1:2] = offset
    vec_ref[2:3] = jnp.sum(wide(mixed_low), 0, keepdims=True)
    dc = low(dot(mixed_low, wo_ref[...], NT))
    for part in groups_of(width):
        q_heads = by_head(qkv_ref[0, :, part] * jnp.asarray(scale_scores, low_type), lanes_low)
        dc_heads = by_head(dc[:, part], lanes_low)
        weights = softmax_rows(dot(q_heads, qkv_ref[1, :, part], NT) + mask)
        weights_back = dot(dc_heads, qkv_ref[2, :, part], NT)
        inner = jnp.sum(weights * weights_back, -1, keepdims=True)
        scores_back = low(weights * (weights_back - inner))
        dq = own_lanes(dot(scores_back, qkv_ref[1, :, part]), lanes) * scale_scores
        dqkv[0, :, part] = low(dq)
        dqkv[1, :, part] = low(dot(scores_back, q_heads, TN))
        dqkv[2, :, part] = low(dot(low(weights), dc_heads, TN))
    vec_ref[3:4] = jnp.sum(wide(dqkv[0]), 0, keepdims=True)
    vec_ref[4:5] = jnp.sum(wide(dqkv[2]), 0, keepdims=True)
    dy_ref[...] = (
        mixed_back
        + dot(dqkv[0], w_ref[0], NT)
        + (dot(dqkv[1], w_ref[1], NT) + dot(dqkv[2], w_ref[2], NT))
    )
    for part in range(3):
        hold[...] = dot(y, dqkv[part], TN)
        emit(outs, part, hold)
    hold[...] = dot(c_ref[...], mixed_low, TN)
    emit(outs, 3, hold)


def self_back(lengths, y, mixed, joined_back, dq, qkv, context, inward, outward, cross_inward, norms):
    rows, width = y.shape
    ins = (y, mixed, joined_back, dq, qkv, context, inward, outward)
    outs = pl.pallas_call(
        self_back_kernel,
        grid=(1,),
        in_specs=[
            pl.BlockSpec(memory_space=pltpu.SMEM),
            *[full(*value.shape) for value in ins],
            full(1, width, width),
            full(3, 2, width),
        ],
        out_specs=[full(rows, width), full(8, width), *grad_specs(4, width, width)],
        out_shape=[
            like((rows, width), wide_type),
            like((8, width), wide_type),
            *grad_shapes(4, width, width),
        ],
        scratch_shapes=[VMEM((3, rows, width), low_type), VMEM((width, width), wide_type)],
        compiler_params=params(48),
        cost_estimate=cost(2e10, 1.5e7),
        name="self_back",
    )(lengths, *ins, cross_inward, norms)
    return outs[:2], outs[2:]


CUT = 192
HALF = CUT // 2
MESH = pl.DeviceIdType.MESH


def shifted(value, axis, by):
    length = lax.axis_size(axis)
    return lax.ppermute(value, axis, [(i, (i + by) % length) for i in range(length)])


def add_rows(to, other, rows):
    def step(i, carry):
        at = pl.ds(pl.multiple_of(i * 32, 32), 32)
        to[at, :] = low(wide(to[at, :]) + wide(other[at, :]))
        return carry

    lax.fori_loop(0, rows // 32, step, 0)


def partners():
    me, section = lax.axis_index("dp"), lax.axis_index("section")
    return (
        {"dp": me + 1 - 2 * (me % 2)},
        {"dp": me + 2 - 4 * ((me // 2) % 2)},
        {"dp": me + 4 - 8 * (me // 4)},
        {"section": section + 1 - 2 * (section % 2)},
        {"section": section + 2 - 4 * (section // 2)},
    )


def on_section(*sections):
    section = lax.axis_index("section")
    wanted = section == sections[0]
    for other in sections[1:]:
        wanted = wanted | (section == other)
    return pl.when(wanted)


def greet():
    barrier = pltpu.get_barrier_semaphore()
    for partner in partners():
        pl.semaphore_signal(barrier, 1, device_id=partner, device_id_type=MESH)

    @on_section(1, 2)
    def _():
        other = {"section": 3 - lax.axis_index("section")}
        pl.semaphore_signal(barrier, 1, device_id=other, device_id_type=MESH)
        pl.semaphore_wait(barrier, 6)

    @on_section(0, 3)
    def _():
        pl.semaphore_wait(barrier, 5)


def laid_out(pieces):
    out, at = [], 0
    for n, first, size in pieces:
        row = first
        while row < first + size:
            rows = min(CUT - at % CUT, first + size - row)
            out.append((n, row, rows, at // CUT, at % CUT))
            row, at = row + rows, at + rows
    return tuple(out), at // CUT


class Plan:
    def __init__(
        self, pieces, arrived, schedule, collective_id, onward=False, vector=0, moved=()
    ):
        self.arrays = 1 + max(piece[0] for piece in pieces)
        self.schedule, self.collective_id = schedule, collective_id
        self.sources, self.fresh = laid_out(pieces)
        self.from_kernels = tuple(arrived)
        arrived = sum(self.from_kernels)
        self.arrived, self.onward = arrived, onward
        self.vector = vector
        self.vector_order = (1, 2, 0, 3, 4)
        self.moved = tuple(moved)
        self.late = arrived + (self.fresh if onward else 0)
        self.ins = 2 * self.arrays + len(self.from_kernels) + len(self.moved) + (1 if vector else 0)

    def in_specs(self):
        anywhere = pl.BlockSpec(memory_space=pl.ANY)
        count = self.ins - (1 if self.vector else 0)
        return [anywhere] * count + ([pl.BlockSpec(memory_space=VMEM)] if self.vector else [])

    def outs(self):
        out = []
        if not self.onward:
            out.append((pl.BlockSpec(memory_space=pl.ANY), like((self.fresh * CUT, WIDTH), low_type)))
        if self.late:
            out.append((pl.BlockSpec(memory_space=pl.ANY), like((self.late * CUT, WIDTH), low_type)))
        for value in self.moved:
            out.append((pl.BlockSpec(memory_space=pl.ANY), value))
        if self.vector:
            out.append((pl.BlockSpec(memory_space=VMEM), like((self.vector, WIDTH), wide_type)))
        return out

    def scratch(self):
        dma = pltpu.SemaphoreType.DMA
        fresh, late, arrived = self.fresh, max(self.late, 1), max(self.arrived, 1)
        most = max(fresh, late)
        count = len(self.sources)
        return [
            VMEM((fresh, 4, CUT, WIDTH), low_type),
            VMEM((fresh, 4, CUT, WIDTH), low_type),
            VMEM((fresh, 2, 2, HALF, WIDTH), low_type),
            VMEM((fresh, 2, HALF, WIDTH), low_type),
            VMEM((arrived, CUT, WIDTH if self.late else 128), low_type),
            VMEM((late, CUT, WIDTH if self.late else 128), low_type),
            VMEM((late, HALF, WIDTH if self.late else 128), low_type),
            VMEM((late, CUT, WIDTH if self.late else 128), low_type),
            VMEM((5, self.vector or 8, WIDTH), wide_type),
            dma((count,)),
            dma((count,)),
            dma((count,)),
            dma((3, fresh, 3)),
            dma((3, fresh, 3)),
            dma((late, 5)),
            dma((late, 5)),
            dma((arrived,)),
            dma((2, most)),
            dma((5,)),
            dma((5,)),
            dma((max(len(self.moved), 1),)),
            dma((max(len(self.moved), 1),)),
        ]

    def open(self, ins, outs, scratch):
        return Sums(self, ins, outs, scratch)


class Sums:
    def __init__(self, plan, ins, outs, scratch):
        count = plan.arrays
        outs, ins = list(outs), list(ins)
        self.plan = plan
        self.keeps, self.sends = ins[:count], ins[count : 2 * count]
        ins = ins[2 * count :]
        self.arrived = [ins.pop(0) for _ in plan.from_kernels]
        self.moved = [ins.pop(0) for _ in plan.moved]
        self.vec_ref = ins.pop(0) if plan.vector else None
        self.shard_out = None if plan.onward else outs.pop(0)
        self.late_out = outs.pop(0) if plan.late else None
        self.moved_out = [outs.pop(0) for _ in plan.moved]
        self.vec_out = outs.pop(0) if plan.vector else None
        (
            self.own,
            self.from_core,
            self.from_one,
            self.from_two,
            self.waiting,
            self.from_outer,
            self.from_inner,
            self.whole,
            self.vec_in,
            self.load_sems,
            self.core_send,
            self.core_recv,
            self.send_sems,
            self.recv_sems,
            self.line_send,
            self.line_recv,
            self.arrive_sems,
            self.out_sems,
            self.vec_send,
            self.vec_recv,
            self.moved_send,
            self.moved_recv,
        ) = scratch
        self.core, self.over_x, self.over_y = partners()[:3]
        section = lax.axis_index("section")
        side = section // 2
        self.mine = pl.multiple_of(side * HALF, HALF)
        self.other = pl.multiple_of((1 - side) * HALF, HALF)
        self.outer = {"section": 3 * side}
        self.inner = {"section": 2 - side}
        self.inward = {"section": 1 + side}

    def remote(self, source, to, send, recv, partner):
        return pltpu.make_async_remote_copy(
            src_ref=source,
            dst_ref=to,
            send_sem=send,
            recv_sem=recv,
            device_id=partner,
            device_id_type=MESH,
        )

    def load(self, s):
        n, row, rows, chunk, at = self.plan.sources[s]
        return pltpu.make_async_copy(
            self.keeps[n].at[:, pl.ds(row, rows)],
            self.own.at[chunk, :, pl.ds(at, rows)],
            self.load_sems.at[s],
        )

    def cross(self, s):
        n, row, rows, chunk, at = self.plan.sources[s]
        return self.remote(
            self.sends[n].at[:, pl.ds(row, rows)],
            self.from_core.at[chunk, :, pl.ds(at, rows)],
            self.core_send.at[s],
            self.core_recv.at[s],
            self.core,
        )

    def arrive(self, k):
        at, source = k, 0
        while at >= self.plan.from_kernels[source]:
            at, source = at - self.plan.from_kernels[source], source + 1
        return pltpu.make_async_copy(
            self.arrived[source].at[pl.ds(at * CUT, CUT)],
            self.waiting.at[k],
            self.arrive_sems.at[k],
        )

    def summed(self, k):
        if k < self.plan.arrived:
            return self.waiting.at[k]
        return self.own.at[k - self.plan.arrived, 0]

    def pairs(self, stage, c):
        own, upper, lower = self.own, pl.ds(0, HALF), pl.ds(HALF, HALF)
        if stage == 1:
            return (
                (own.at[c, 1, upper], self.from_one.at[c, 0, 0], self.over_x),
                (own.at[c, 3, upper], self.from_one.at[c, 0, 1], self.over_x),
                (own.at[c, pl.ds(2, 2), lower], self.from_one.at[c, 1], self.over_y),
            )
        return (
            (own.at[c, 2, upper], self.from_two.at[c, 0], self.over_y),
            (own.at[c, 1, lower], self.from_two.at[c, 1], self.over_x),
        )

    def copies(self, stage, c):
        return [
            self.remote(
                source, to, self.send_sems.at[stage, c, k], self.recv_sems.at[stage, c, k], partner
            )
            for k, (source, to, partner) in enumerate(self.pairs(stage, c))
        ]

    def start(self, stage, c):
        for copy in self.copies(stage, c):
            copy.start()

    def line_copy(self, n, k):
        mine, other = pl.ds(self.mine, HALF), pl.ds(self.other, HALF)
        whole = self.whole.at[k]
        source, to, partner = (
            (self.summed(k), self.from_outer.at[k], self.inward),
            (self.summed(k).at[other], self.from_inner.at[k], self.inner),
            (whole.at[mine], whole.at[mine], self.inner),
            (whole.at[mine], whole.at[mine], self.outer),
            (whole.at[other], whole.at[other], self.outer),
        )[n]
        return self.remote(source, to, self.line_send.at[k, n], self.line_recv.at[k, n], partner)

    def line(self, stage, k):
        if stage == "go":

            @on_section(0, 3)
            def _():
                self.line_copy(0, k).start()

            return
        if stage == 6:

            @on_section(0, 3)
            def _():
                self.line_copy(3, k).wait_recv()
                self.line_copy(4, k).wait_recv()

            self.late_copy(k).start()
            return

        @on_section(1, 2)
        def _():
            self.line_copy(stage - 3, k).wait_recv()
            if stage == 3:
                add_rows(self.summed(k), self.from_outer.at[k], CUT)
                self.line_copy(1, k).start()
            elif stage == 4:
                rows = pl.ds(self.mine, HALF)
                self.whole[k, rows, :] = low(
                    wide(self.summed(k)[rows, :]) + wide(self.from_inner[k])
                )
                self.line_copy(2, k).start()
                self.line_copy(3, k).start()
            else:
                self.line_copy(4, k).start()

    def line_sent(self, k):
        @on_section(0, 3)
        def _():
            self.line_copy(0, k).wait_send()

        @on_section(1, 2)
        def _():
            for n in range(1, 5):
                self.line_copy(n, k).wait_send()

    def shard_copy(self, c):
        return pltpu.make_async_copy(
            self.own.at[c, 0], self.shard_out.at[pl.ds(c * CUT, CUT)], self.out_sems.at[0, c]
        )

    def late_copy(self, k):
        return pltpu.make_async_copy(
            self.whole.at[k], self.late_out.at[pl.ds(k * CUT, CUT)], self.out_sems.at[1, k]
        )

    def moved_copy(self, n):
        return self.remote(
            self.moved[n],
            self.moved_out[n],
            self.moved_send.at[n],
            self.moved_recv.at[n],
            partners()[4],
        )

    def vec_copy(self, stage):
        return self.remote(
            self.vec_out,
            self.vec_in.at[stage],
            self.vec_send.at[stage],
            self.vec_recv.at[stage],
            partners()[self.plan.vector_order[stage]],
        )

    def vec_step(self, stage):
        if stage:
            self.vec_copy(stage - 1).wait()
            self.vec_out[...] += self.vec_in[stage - 1]
        else:
            self.vec_out[...] = self.vec_ref[...]
        if stage < 5:
            self.vec_copy(stage).start()

    def begin(self):
        greet()
        for s in range(len(self.plan.sources)):
            self.cross(s).start()
            self.load(s).start()
        for k in range(self.plan.arrived):
            self.arrive(k).start()
        for n in range(len(self.moved)):
            self.moved_copy(n).start()

    def step(self, stage, c):
        if stage == "vec":
            self.vec_step(c)
            return
        if stage == "go":
            self.arrive(c).wait()
            self.line("go", c)
            return
        if stage > 2:
            self.line(stage, c)
            return
        if stage == 0:
            for s, source in enumerate(self.plan.sources):
                if source[3] == c:
                    self.load(s).wait()
                    self.cross(s).wait_recv()
            for at in range(4):
                add_rows(self.own.at[c, at], self.from_core.at[c, at], CUT)
            self.start(1, c)
            return
        for copy in self.copies(stage, c):
            copy.wait_recv()
        upper, lower = pl.ds(0, HALF), pl.ds(HALF, HALF)
        if stage == 1:
            for k in range(2):
                add_rows(self.own.at[c, 2 * k, upper], self.from_one.at[c, 0, k], HALF)
                add_rows(self.own.at[c, k, lower], self.from_one.at[c, 1, k], HALF)
            self.start(2, c)
        else:
            add_rows(self.own.at[c, 0, upper], self.from_two.at[c, 0], HALF)
            add_rows(self.own.at[c, 0, lower], self.from_two.at[c, 1], HALF)
            if self.plan.onward:
                self.line("go", self.plan.arrived + c)
            else:
                self.shard_copy(c).start()

    def finish(self):
        for n in range(len(self.moved)):
            self.moved_copy(n).wait()
        for s in range(len(self.plan.sources)):
            self.cross(s).wait_send()
        for c in range(self.plan.fresh):
            for stage in (1, 2):
                for copy in self.copies(stage, c):
                    copy.wait_send()
            if not self.plan.onward:
                self.shard_copy(c).wait()
        for k in range(self.plan.late):
            self.line_sent(k)
            self.late_copy(k).wait()

    def slot(self, grid_step, steps, slots, slot):
        for n in range(steps):
            wanted = self.plan.schedule.get(n * slots + slot, ())
            if not wanted:
                continue

            @pl.when(grid_step == n)
            def _(wanted=wanted):
                for stage, c in wanted:
                    if stage == "begin":
                        self.begin()
                    elif stage == "finish":
                        self.finish()
                    else:
                        self.step(stage, c)


def last_sums_kernel(plan, *refs):
    ins, rest = refs[: plan.ins], refs[plan.ins :]
    count = len(plan.outs())
    sums = plan.open(ins, rest[:count], rest[count:])
    sums.begin()
    for stage, c in plan.schedule:
        sums.step(stage, c)
    sums.finish()


def last_sums(plan, pairs, arrived, vector):
    outs = plan.outs()
    return pl.pallas_call(
        functools.partial(last_sums_kernel, plan),
        in_specs=plan.in_specs(),
        out_specs=[spec for spec, _ in outs],
        out_shape=[shape for _, shape in outs],
        scratch_shapes=plan.scratch(),
        compiler_params=params(60, collective_id=plan.collective_id, has_side_effects=True),
        cost_estimate=cost(1e8, 1e8),
        name="last_sums",
    )(*[p[0] for p in pairs], *[p[1] for p in pairs], *arrived, vector)


def feed_plan(moved):
    schedule = {
        0: [("begin", 0)],
        1: [(0, 0), (0, 1), (0, 2)],
        9: [(1, 0), (1, 1), (1, 2)],
        11: [(2, 0), (2, 1), (2, 2), ("finish", 0)],
    }
    return Plan(((0, 0, 288), (1, 0, 96), (2, 0, 192)), (), schedule, 1, moved=moved)


def attend_plan():
    schedule = {
        0: [("begin", 0), ("vec", 0)],
        1: [("vec", 1), (0, 0), (0, 1), (0, 2), (0, 3), (0, 4)],
        3: [("vec", 2)],
        4: [("vec", 3)],
        6: [("vec", 4), (1, 0), (1, 1), (1, 2)],
        7: [("vec", 5), (1, 3), (1, 4)],
        8: [(2, 0), (2, 1), (2, 2), (2, 3), (2, 4), ("finish", 0)],
    }
    return Plan(((0, 192, 192), (1, 0, 384), (2, 0, 384)), (), schedule, 2, vector=32)


def last_plan():
    order = [("vec", 0), *[("go", k) for k in range(5)], ("vec", 1), (0, 0), ("vec", 2), (0, 1)]
    order += [("vec", 3), (1, 0), (1, 1), (3, 0), (2, 0), (2, 1), (3, 1), (4, 0), (3, 2), (4, 1)]
    order += [(5, 0), (3, 3), (4, 2), (5, 1), (6, 0), (3, 4), ("vec", 4), (4, 3), (5, 2), (6, 1)]
    order += [(3, 5), (4, 4), (5, 3), (6, 2), (3, 6), (4, 5), (5, 4), (6, 3), (4, 6), (5, 5)]
    order += [(6, 4), ("vec", 5), (5, 6), (6, 5), (6, 6)]
    return Plan(((0, 0, 288), (1, 0, 96)), (5,), order, 3, onward=True, vector=8)


def unpack_kernel(feed_ref, first_ref, last_ref, vec_ref, bias_ref, *outs):
    (
        e_in, e_out, e_bias, e_norm, e_expand, e_expand_bias, e_shrink, e_shrink_bias,
        s_in, s_out, c_in, c_out, d_bias, d_norm, d_expand, d_expand_bias, d_shrink, d_shrink_bias,
    ) = outs
    rows = e_out.shape[0]

    def rows_of(ref, at, count=1):
        return wide(ref[at * rows : (at + count) * rows, :])

    for i in range(4):
        part = slice(i * WIDTH, (i + 1) * WIDTH)
        d_expand[:, part] = rows_of(feed_ref, i)
        e_expand[:, part] = rows_of(last_ref, 2 + i)
    d_shrink[...] = rows_of(feed_ref, 4, 4)
    for i in range(3):
        c_in[i] = rows_of(first_ref, i)
        e_in[i] = rows_of(last_ref, 10 + i)
    c_out[...] = rows_of(first_ref, 3)
    s_in[0] = rows_of(first_ref, 4)
    s_in[1] = rows_of(first_ref, 5)
    s_in[2] = rows_of(last_ref, 0)
    s_out[...] = rows_of(last_ref, 1)
    e_shrink[...] = rows_of(last_ref, 6, 4)
    e_out[...] = rows_of(last_ref, 13)
    me = lax.axis_index("dp")
    mine = pltpu.roll(vec_ref[...], WIDTH - me * rows, 1)
    e_bias[0:2] = pltpu.roll(bias_ref[...], WIDTH - me * rows, 1)[0:2, 0:rows]
    e_bias[2:3] = mine[2:3, 0:rows]
    e_norm[0] = mine[3:5, 0:rows]
    e_norm[1] = mine[5:7, 0:rows]
    e_shrink_bias[...] = mine[11:12, 0:rows]
    d_bias[...] = mine[12:18, 0:rows]
    for i in range(3):
        d_norm[i] = mine[18 + 2 * i : 20 + 2 * i, 0:rows]
    d_shrink_bias[...] = mine[28:29, 0:rows]
    for at, to in ((7, e_expand_bias), (24, d_expand_bias)):
        row = jnp.zeros((1, WIDTH), wide_type)
        for i in range(4):
            row = jnp.where(me // 2 == i, vec_ref[at + i : at + i + 1, :], row)
        to[...] = jnp.where(me % 2 == 0, row[:, : WIDTH // 2], row[:, WIDTH // 2 :])


def unpack(feed, first, last, vector, biases):
    rows, width = WIDTH // 8, WIDTH
    square, cube = (rows, width), (3, rows, width)
    wide_one, tall_one = (rows, 4 * width), (4 * rows, width)
    shapes = [
        cube, square, (3, rows), (2, 2, rows), wide_one, (1, 4 * rows), tall_one, (1, rows),
        cube, square, cube, square, (6, rows), (3, 2, rows), wide_one, (1, 4 * rows), tall_one,
        (1, rows),
    ]
    here = pl.BlockSpec(memory_space=VMEM)
    return pl.pallas_call(
        unpack_kernel,
        in_specs=[here] * 5,
        out_specs=[here] * len(shapes),
        out_shape=[like(shape, wide_type) for shape in shapes],
        compiler_params=params(),
        cost_estimate=cost(1e7, 1.3e7),
        name="unpack",
    )(feed, first, last, vector, biases)


def sum_whole(grads):
    parts = lax.axis_size("dp")
    packed = []
    for grad in grads:
        count, rows, columns = grad.shape
        cut = grad.reshape(count, parts, rows // parts, columns // WIDTH, WIDTH)
        packed.append(cut.transpose(1, 0, 3, 2, 4).reshape(parts, -1, WIDTH))
    shard = lax.psum_scatter(jnp.concatenate(packed, 1), "dp", scatter_dimension=0, tiled=True)[0]
    total = wide(lax.psum(shard, "section"))
    outs, at = [], 0
    for grad in grads:
        count, rows, columns = grad.shape
        size = grad.size // parts // WIDTH
        cut = total[at : at + size].reshape(count, columns // WIDTH, rows // parts, WIDTH)
        outs.append(cut.transpose(0, 2, 1, 3).reshape(count * rows // parts, columns))
        at += size
    return outs


def beside(shard):
    rows = shard.shape[0] // 4
    return shard.reshape(4, rows, WIDTH).transpose(1, 0, 2).reshape(rows, 4 * WIDTH)


def sum_any(grads, d_feed, vectors):
    e_in, e_out, e_expand, e_shrink, s_all, c_in, c_out = sum_whole([grad[0] for grad in grads])
    d_feed = wide(lax.psum(d_feed, "section"))
    d_expand, d_shrink = d_feed[: d_feed.shape[0] // 2], d_feed[d_feed.shape[0] // 2 :]
    flat = lax.psum(jnp.concatenate([v.reshape(-1) for v in vectors]), ("dp", "section"))
    parts, mine = lax.axis_size("dp"), lax.axis_index("dp")
    outs, at = [], 0
    for v in vectors:
        whole = flat[at : at + v.size].reshape(v.shape)
        at += v.size
        size = v.shape[-1] // parts
        outs.append(lax.dynamic_slice_in_dim(whole, mine * size, size, v.ndim - 1))
    rows = WIDTH // parts
    return (
        e_in.reshape(3, rows, WIDTH),
        e_out,
        outs[0],
        outs[1],
        beside(e_expand),
        outs[2],
        e_shrink,
        outs[3],
        s_all[: 3 * rows].reshape(3, rows, WIDTH),
        s_all[3 * rows :],
        c_in.reshape(3, rows, WIDTH),
        c_out,
        outs[4],
        outs[5],
        beside(d_expand),
        outs[6],
        d_shrink,
        outs[7],
    )


def on_device(
    encoder_input,
    decoder_input,
    cotangent,
    pool_table,
    retrieved,
    decoder_lengths,
    encoder_inward,
    encoder_outward,
    encoder_biases,
    encoder_norms,
    encoder_expand,
    encoder_expand_bias,
    encoder_shrink,
    encoder_shrink_bias,
    self_inward,
    self_outward,
    cross_inward,
    cross_outward,
    decoder_biases,
    decoder_norms,
    decoder_expand,
    decoder_expand_bias,
    decoder_shrink,
    decoder_shrink_bias,
):
    x = encoder_input[0]
    half_way = lax.axis_size("section") // 2
    y, grad, slots, table, lengths = [
        shifted(value, "section", -half_way)
        for value in (
            decoder_input[0],
            cotangent[0],
            retrieved[0],
            pool_table[0, 0],
            decoder_lengths[0],
        )
    ]
    table, lengths = table.reshape(-1), lengths[0]
    owners = pool_table.shape[2]

    qkv, context, context_low, stats, mixed = encoder_attend(
        x, encoder_inward, encoder_outward, encoder_biases
    )
    hidden, slope, summed, states = encoder_feed(
        mixed,
        encoder_norms,
        encoder_expand,
        encoder_expand_bias,
        encoder_shrink,
        encoder_shrink_bias,
    )
    picked = pick_rows(table, states).reshape(owners, -1, WIDTH)
    pooled = lax.all_to_all(picked, "dp", split_axis=0, concat_axis=0, tiled=True)
    pooled = pooled.reshape(-1, WIDTH)

    mask_across, mask_down = slot_mask(slots, pooled.shape[0])
    self_qkv, self_context, self_mixed, cross_q = self_forward(
        lengths, y, self_inward, self_outward, decoder_biases, decoder_norms, cross_inward
    )
    kv, cross_context, cross_stats = cross_forward(
        pooled, cross_q, mask_across, cross_inward, decoder_biases
    )
    (out, joined_back, dc, mid_vec, mid_expand), d_feed, d_cross_out = middle(
        self_mixed,
        cross_context,
        cross_outward,
        decoder_biases,
        decoder_norms,
        decoder_expand,
        decoder_expand_bias,
        decoder_shrink,
        decoder_shrink_bias,
        grad,
    )
    d_feed = lax.psum_scatter(d_feed, "dp", scatter_dimension=0, tiled=True)[0]
    dkv, dq, cross_vec, dpool = cross_back(
        kv, cross_q, cross_context, dc, cross_stats, mask_down, cross_inward
    )
    returned = lax.all_to_all(
        dpool.reshape(owners, -1, WIDTH), "dp", split_axis=0, concat_axis=0, tiled=True
    )
    d_cross_in = cross_grads(pooled, dkv, self_mixed, dq, decoder_norms)
    (dy, self_vec), d_self = self_back(
        lengths,
        y,
        self_mixed,
        joined_back,
        dq,
        self_qkv,
        self_context,
        self_inward,
        self_outward,
        cross_inward,
        decoder_norms,
    )
    states_back = spread_rows(table, returned.reshape(-1, WIDTH), x.shape[0])

    hosts = paired()
    plan = feed_plan([like(out.shape, out.dtype), like(dy.shape, dy.dtype)]) if hosts else None
    pairs = (d_cross_in, d_cross_out, d_self)
    guests = [pair[k] for k in range(2) for pair in pairs] + [out, dy] if hosts else []
    (dmix, feed_vec, feed_expand), (e_expand, e_shrink, e_out), from_feed = encoder_feed_back(
        states_back,
        summed,
        mixed,
        hidden,
        slope,
        context_low,
        encoder_norms,
        encoder_expand,
        encoder_shrink,
        plan,
        guests,
    )
    if hosts:
        decoder_out, decoder_grad = from_feed[1:]
    else:
        decoder_out = shifted(out, "section", half_way)
        decoder_grad = shifted(dy, "section", half_way)
    rest = [
        jnp.concatenate([jnp.zeros((2, WIDTH), wide_type), feed_vec[5:6]], 0),
        jnp.stack([feed_vec[3:5], feed_vec[0:2]]),
        feed_expand[0],
        feed_vec[2],
        jnp.concatenate([self_vec[3:5], self_vec[2:3], cross_vec[0:2], mid_vec[5:6]], 0),
        jnp.stack([self_vec[0:2], mid_vec[3:5], mid_vec[0:2]]),
        mid_expand[0],
        mid_vec[2],
    ]
    plan = attend_plan() if hosts else None
    if hosts:
        guests = [pair[k] for k in range(2) for pair in (d_self, e_expand, e_shrink)]
        flat = jnp.concatenate([v.reshape(-1) for v in rest])
        flat = jnp.pad(flat, (0, 32 * WIDTH - flat.size)).reshape(32, WIDTH)
        guests.append(flat)
        early, dmix = lax.optimization_barrier(((d_feed, from_feed[0]), dmix))
        early = lax.psum(early, "section")
    (dx, attend_vec), e_in, from_attend = encoder_attend_back(
        dmix, x, qkv, context, stats, encoder_inward, encoder_outward, plan, guests
    )
    if hosts:
        last, vector = last_sums(last_plan(), (e_in, e_out), from_attend[:1], attend_vec)
        results = unpack(*early, last, from_attend[1], vector)
        results = [r[0] if n in (5, 7, 15, 17) else r for n, r in enumerate(results)]
    else:
        results = sum_any(
            [e_in, e_out, e_expand, e_shrink, d_self, d_cross_in, d_cross_out],
            d_feed,
            [rest[0] + jnp.pad(attend_vec[0:2], ((0, 1), (0, 0)))] + rest[1:],
        )
    return (decoder_out[None], dx[None], decoder_grad[None], *results)


def solution(mesh):
    in_specs = (
        P("section", "dp", None),
        P("section", "dp", None),
        P("section", "dp", None),
        P("section", "dp", None, None),
        P("section", "dp", None),
        P("section", "dp", None),
        P(),
        P(),
        P(),
        P(),
        P(),
        P(),
        P(),
        P(),
        P(),
        P(),
        P(),
        P(),
        P(),
        P(),
        P(),
        P(),
        P(),
        P(),
    )
    out_specs = (
        P("section", "dp", None),
        P("section", "dp", None),
        P("section", "dp", None),
        P(None, "dp", None),
        P("dp", None),
        P(None, "dp"),
        P(None, None, "dp"),
        P("dp", None),
        P("dp"),
        P("dp", None),
        P("dp"),
        P(None, "dp", None),
        P("dp", None),
        P(None, "dp", None),
        P("dp", None),
        P(None, "dp"),
        P(None, None, "dp"),
        P("dp", None),
        P("dp"),
        P("dp", None),
        P("dp"),
    )
    return jax.shard_map(
        on_device, mesh=mesh, in_specs=in_specs, out_specs=out_specs, check_vma=False
    )
```

```python
import functools

import jax
import jax.numpy as jnp
from jax import lax
from jax.experimental import pallas as pl
from jax.experimental.pallas import tpu as pltpu
from jax.sharding import PartitionSpec as P

HEAD = 64
WIDTH = 768


norm_eps = 1e-05
scale_scores = 0.125
low_type = jnp.bfloat16
wide_type = jnp.float32

NN = (((1,), (0,)), ((), ()))
NT = (((1,), (1,)), ((), ()))
TN = (((0,), (0,)), ((), ()))
GROUP = 256
VMEM = pltpu.VMEM


def dot(left, right, dims=NN):
    return lax.dot_general(left, right, dims, preferred_element_type=wide_type)


def low(value):
    return value.astype(low_type)


def wide(value):
    return value.astype(wide_type)


def head_lanes(dtype):
    lane = lax.broadcasted_iota(jnp.int32, (1, GROUP), 1) // HEAD
    return [(lane == h).astype(wide_type).astype(dtype) for h in range(GROUP // HEAD)]


def centred_of(values):
    centred = values - jnp.mean(values, -1, keepdims=True)
    spread = jnp.mean(centred * centred, -1, keepdims=True)
    return centred, lax.rsqrt(spread + norm_eps)


def norm_rows(values, gain, offset):
    centred, scale = centred_of(values)
    return centred * scale * (1.0 + gain) + offset


def norm_rows_back(values, gain, incoming):
    centred, scale = centred_of(values)
    unit = centred * scale
    inner = incoming * (1.0 + gain)
    mean_inner = jnp.mean(inner, -1, keepdims=True)
    mean_along = jnp.mean(inner * unit, -1, keepdims=True)
    return (
        scale * (inner - mean_inner - unit * mean_along),
        jnp.sum(incoming * unit, 0, keepdims=True),
        jnp.sum(incoming, 0, keepdims=True),
    )


def gelu_parts(u):
    size = jnp.abs(u) * 0.7071067811865476
    t = 1.0 / (1.0 + 0.3275911 * size)
    bell = jnp.exp(-0.5 * u * u)
    series = t * (
        0.254829592
        + t * (-0.284496736 + t * (1.421413741 + t * (-1.453152027 + t * 1.061405429)))
    )
    tail = 0.5 * series * bell
    share = jnp.where(u < 0.0, tail, 1.0 - tail)
    return u * share, share + u * (bell * 0.3989422804014327)


def params(limit=60, **rest):
    return pltpu.CompilerParams(vmem_limit_bytes=limit * 2**20, **rest)


def host_params(plan):
    if plan:
        return params(62, collective_id=plan.collective_id, has_side_effects=True)
    return params()


def cost(flops, size, exps=0):
    return pl.CostEstimate(flops=int(flops), bytes_accessed=int(size), transcendentals=int(exps))


def full(*shape):
    return pl.BlockSpec(shape, lambda *_: (0,) * len(shape))


def once(*shape):
    return pl.BlockSpec(shape, lambda *_: (0,) * len(shape), pipeline_mode=pl.Buffered(1))


def like(shape, dtype):
    return jax.ShapeDtypeStruct(shape, dtype)


def paired():
    return lax.axis_size("dp") == 8


def grad_shapes(parts, rows, columns):
    if paired():
        return [like((4, parts * rows // 8, columns), low_type)] * 2
    return [like((parts, rows, columns), low_type)]


def grad_specs(parts, rows, columns, index=None):
    if paired():
        block, count = (4, parts * rows // 8, columns), 2
    else:
        block, count = (parts, rows, columns), 1
    return [pl.BlockSpec(block, index or (lambda *_: (0, 0, 0)))] * count


def emit(outs, part, hold):
    if len(outs) == 1:
        outs[0][part] = low(hold[...])
        return
    keep, send = outs
    me = lax.axis_index("dp")
    rows = hold.shape[0] // 8
    to = pl.ds(pl.multiple_of(part * rows, rows), rows)
    for at in range(4):
        mine = pl.multiple_of((me ^ (2 * at)) * rows, rows)
        other = pl.multiple_of((me ^ (2 * at + 1)) * rows, rows)
        keep[at, to, :] = low(hold[pl.ds(mine, rows), :])
        send[at, to, :] = low(hold[pl.ds(other, rows), :])


def emit_tall(outs, block, hold):
    if len(outs) == 1:
        size = hold.shape[0]
        outs[0][0, pl.ds(pl.multiple_of(block * size, size), size), :] = low(hold[...])
        return
    keep, send = outs
    me = lax.axis_index("dp")
    rows = hold.shape[0] // 2
    at = block ^ lax.shift_right_logical(me, 1)
    core = me & 1
    keep[at, 0:rows, :] = low(hold[pl.ds(pl.multiple_of(core * rows, rows), rows), :])
    send[at, 0:rows, :] = low(hold[pl.ds(pl.multiple_of((1 - core) * rows, rows), rows), :])


def thirds(items):
    third = len(items) // 3
    return items[:third], items[third : 2 * third], items[2 * third :]


def encoder_attend_kernel(
    x_ref, w_ref, wo_ref, bg_ref, b_ref, qkv_ref, c_ref, cl_ref, stat_ref, mixed_ref, stats
):
    group = pl.program_id(0)
    tokens = x_ref.shape[0]
    block = 512
    x = x_ref[...]
    qkv_ref[0] = low(dot(x, w_ref[0]) + bg_ref[0:1])
    qkv_ref[1] = low(dot(x, w_ref[1]))
    qkv_ref[2] = low(dot(x, w_ref[2]) + bg_ref[1:2])
    lanes_low, lanes = head_lanes(low_type), head_lanes(wide_type)
    lane = lax.broadcasted_iota(jnp.int32, (1, 128), 1)

    @pl.when(group == 0)
    def _():
        mixed_ref[...] = wide(x) + b_ref[2:3]

    def rows_step(i, carry):
        rows = pl.ds(pl.multiple_of(i * block, block), block)
        q = qkv_ref[0, rows, :] * jnp.asarray(scale_scores, low_type)
        context = jnp.zeros((block, GROUP), wide_type)
        stat = jnp.zeros((block, 128), wide_type)
        for h in range(GROUP // HEAD):
            scores = dot(q * lanes_low[h], qkv_ref[1], NT)
            top = jnp.max(scores, -1, keepdims=True)
            weights = jnp.exp(scores - top)
            total = jnp.sum(weights, -1, keepdims=True)
            context += dot(low(weights), qkv_ref[2]) * (lanes[h] * (1.0 / total))
            stat = jnp.where(lane == h, top + jnp.log(total), stat)
        c_ref[rows, :] = context
        cl_ref[rows, :] = low(context)
        stats[rows, :] = stat
        mixed_ref[rows, :] += dot(low(context), wo_ref[...])
        return carry

    lax.fori_loop(0, tokens // block, rows_step, 0)
    stat_ref[0] = stats[...].T[0:8]


def encoder_attend(x, inward, outward, biases):
    tokens, width = x.shape
    groups = width // GROUP
    return pl.pallas_call(
        encoder_attend_kernel,
        grid=(groups,),
        in_specs=[
            full(tokens, width),
            pl.BlockSpec((3, width, GROUP), lambda g: (0, 0, g)),
            pl.BlockSpec((GROUP, width), lambda g: (g, 0)),
            pl.BlockSpec((3, GROUP), lambda g: (0, g)),
            full(3, width),
        ],
        out_specs=[
            pl.BlockSpec((3, tokens, GROUP), lambda g: (0, 0, g)),
            pl.BlockSpec((tokens, GROUP), lambda g: (0, g)),
            pl.BlockSpec((tokens, GROUP), lambda g: (0, g)),
            pl.BlockSpec((1, 8, tokens), lambda g: (g, 0, 0)),
            full(tokens, width),
        ],
        out_shape=[
            like((3, tokens, width), low_type),
            like((tokens, width), wide_type),
            like((tokens, width), low_type),
            like((groups, 8, tokens), wide_type),
            like((tokens, width), wide_type),
        ],
        scratch_shapes=[VMEM((tokens, 128), wide_type)],
        compiler_params=params(),
        cost_estimate=cost(3e10, 2e7, 1.3e7),
        name="encoder_attend",
    )(x, inward, outward, biases, biases)


def encoder_feed_kernel(
    mixed_ref, n_ref, e_ref, eb_ref, s_ref, sb_ref, h_ref, d_ref, sum_ref, out_ref, a_low
):
    step = pl.program_id(0)
    tokens = mixed_ref.shape[0]
    block = 256

    @pl.when(step == 0)
    def _():
        def rows_step(i, carry):
            rows = pl.ds(pl.multiple_of(i * 256, 256), 256)
            first = norm_rows(mixed_ref[rows, :], n_ref[0, 0:1], n_ref[0, 1:2])
            a_low[rows, :] = low(first)
            sum_ref[rows, :] = first + sb_ref[...]
            return carry

        lax.fori_loop(0, tokens // 256, rows_step, 0)

    for i in range(tokens // block):
        rows = slice(i * block, (i + 1) * block)
        hidden, slope = gelu_parts(dot(a_low[rows, :], e_ref[...]) + eb_ref[...])
        h_ref[rows, :] = low(hidden)
        d_ref[rows, :] = low(slope)
        sum_ref[rows, :] += dot(low(hidden), s_ref[...])

    @pl.when(step == pl.num_programs(0) - 1)
    def _():
        def rows_step(i, carry):
            rows = pl.ds(pl.multiple_of(i * 256, 256), 256)
            out_ref[rows, :] = low(norm_rows(sum_ref[rows, :], n_ref[1, 0:1], n_ref[1, 1:2]))
            return carry

        lax.fori_loop(0, tokens // 256, rows_step, 0)


def encoder_feed(mixed, norms, expand, expand_bias, shrink, shrink_bias):
    tokens, width = mixed.shape
    hidden = expand.shape[1]
    cut = hidden // 4
    return pl.pallas_call(
        encoder_feed_kernel,
        grid=(4,),
        in_specs=[
            full(tokens, width),
            full(2, 2, width),
            pl.BlockSpec((width, cut), lambda i: (0, i)),
            pl.BlockSpec((1, cut), lambda i: (0, i)),
            pl.BlockSpec((cut, width), lambda i: (i, 0)),
            full(1, width),
        ],
        out_specs=[
            pl.BlockSpec((tokens, cut), lambda i: (0, i)),
            pl.BlockSpec((tokens, cut), lambda i: (0, i)),
            full(tokens, width),
            full(tokens, width),
        ],
        out_shape=[
            like((tokens, hidden), low_type),
            like((tokens, hidden), low_type),
            like((tokens, width), wide_type),
            like((tokens, width), low_type),
        ],
        scratch_shapes=[VMEM((tokens, width), low_type)],
        compiler_params=params(),
        cost_estimate=cost(2e10, 3e7, 3e6),
        name="encoder_feed",
    )(mixed, norms, expand, expand_bias[None], shrink, shrink_bias[None])


def split_refs(refs, *counts):
    out, at = [], 0
    for count in counts:
        out.append(refs[at : at + count])
        at += count
    return out + [refs[at:]]


def hosting(plan):
    return (plan.ins, len(plan.outs())) if plan else (0, 0)


def encoder_feed_back_kernel(plan, *refs):
    grads = 6 if paired() else 3
    host_ins, host_outs = hosting(plan)
    main, guests, outs, guest_outs, scratch, guest_scratch = split_refs(
        refs, 9, host_ins, 3 + grads, host_outs, 4
    )
    g_ref, sum_ref, mixed_ref, h_ref, d_ref, c_ref, n_ref, e_ref, s_ref = main
    dmix_ref, vec_ref, eb_ref = outs[:3]
    wide_outs, tall_outs, out_outs = thirds(outs[3:])
    back_low, a_turned, between, hold = scratch
    step = pl.program_id(0)
    sums = plan.open(guests, guest_outs, guest_scratch) if plan else None

    def place(n):
        if sums:
            sums.slot(step, 4, 3, n)

    place(0)
    tokens = sum_ref.shape[0]
    block = 256

    @pl.when(step == 0)
    def _():
        vec_ref[...] = jnp.zeros(vec_ref.shape, wide_type)

        def rows_step(i, carry):
            rows = pl.ds(pl.multiple_of(i * 256, 256), 256)
            grad, gain, offset = norm_rows_back(
                sum_ref[rows, :], n_ref[1, 0:1], wide(g_ref[rows, :])
            )
            dmix_ref[rows, :] = grad
            back_low[rows, :] = low(grad)
            vec_ref[0:1] += gain
            vec_ref[1:2] += offset
            vec_ref[2:3] += jnp.sum(wide(low(grad)), 0, keepdims=True)
            first = norm_rows(mixed_ref[rows, :], n_ref[0, 0:1], n_ref[0, 1:2])
            a_turned[:, rows] = low(first).T
            return carry

        lax.fori_loop(0, tokens // 256, rows_step, 0)

    column = jnp.zeros(eb_ref.shape, wide_type)
    for i in range(tokens // block):
        rows = slice(i * block, (i + 1) * block)
        before = low(dot(back_low[rows, :], s_ref[...], NT) * wide(d_ref[rows, :]))
        between[rows, :] = before
        column += jnp.sum(wide(before), 0, keepdims=True)
        dmix_ref[rows, :] += dot(before, e_ref[...], NT)
        if i == 1:
            place(1)
    eb_ref[...] = column
    hold[...] = dot(a_turned[...], between[...])
    emit(wide_outs, step, hold)
    hold[...] = dot(h_ref[...], back_low[...], TN)
    emit_tall(tall_outs, step, hold)

    @pl.when(step == pl.num_programs(0) - 1)
    def _():

        def rows_step(i, carry):
            rows = pl.ds(pl.multiple_of(i * 256, 256), 256)
            grad, gain, offset = norm_rows_back(
                mixed_ref[rows, :], n_ref[0, 0:1], dmix_ref[rows, :]
            )
            dmix_ref[rows, :] = grad
            back_low[rows, :] = low(grad)
            vec_ref[3:4] += gain
            vec_ref[4:5] += offset
            vec_ref[5:6] += jnp.sum(wide(low(grad)), 0, keepdims=True)
            return carry

        lax.fori_loop(0, tokens // 256, rows_step, 0)
        hold[...] = dot(c_ref[...], back_low[...], TN)
        emit(out_outs, 0, hold)

    place(2)


def encoder_feed_back(
    grad, summed, mixed, hidden, slope, context, norms, expand, shrink, plan=None, guests=()
):
    tokens, width = mixed.shape
    total = expand.shape[1]
    cut = total // 4
    guest_outs = plan.outs() if plan else []
    outs = pl.pallas_call(
        functools.partial(encoder_feed_back_kernel, plan),
        grid=(4,),
        in_specs=[
            once(tokens, width),
            once(tokens, width),
            once(tokens, width),
            pl.BlockSpec((tokens, cut), lambda i: (0, i)),
            pl.BlockSpec((tokens, cut), lambda i: (0, i)),
            once(tokens, width),
            full(2, 2, width),
            pl.BlockSpec((width, cut), lambda i: (0, i)),
            pl.BlockSpec((cut, width), lambda i: (i, 0)),
            *(plan.in_specs() if plan else []),
        ],
        out_specs=[
            full(tokens, width),
            full(8, width),
            pl.BlockSpec((1, cut), lambda i: (0, i)),
            *grad_specs(4, width, width),
            *grad_specs(1, total, width),
            *grad_specs(1, width, width),
            *[spec for spec, _ in guest_outs],
        ],
        out_shape=[
            like((tokens, width), wide_type),
            like((8, width), wide_type),
            like((1, total), wide_type),
            *grad_shapes(4, width, width),
            *grad_shapes(1, total, width),
            *grad_shapes(1, width, width),
            *[shape for _, shape in guest_outs],
        ],
        scratch_shapes=[
            VMEM((tokens, width), low_type),
            VMEM((width, tokens), low_type),
            VMEM((tokens, cut), low_type),
            VMEM((width, width), wide_type),
            *(plan.scratch() if plan else []),
        ],
        compiler_params=host_params(plan),
        cost_estimate=cost(4e10, 5e7),
        name="encoder_feed_back",
    )(grad, summed, mixed, hidden, slope, context, norms, expand, shrink, *guests)
    main = len(outs) - len(guest_outs)
    return outs[:3], thirds(outs[3:main]), outs[main:]


def encoder_attend_back_kernel(plan, *refs):
    host_ins, host_outs = hosting(plan)
    main, guests, (dx_ref, vec_ref), outs, guest_outs, scratch, guest_scratch = split_refs(
        refs, 7, host_ins, 2, 2 if paired() else 1, host_outs, 9
    )
    dmix_ref, x_ref, qkv_ref, c_ref, stat_ref, w_ref, wo_ref = main
    dmix_low, x_turned, dc, weights, scores_back, dk, dv, dq_turned, hold = scratch
    group = pl.program_id(0)
    sums = plan.open(guests, guest_outs, guest_scratch) if plan else None

    def place(n):
        if sums:
            sums.slot(group, 3, 3, n)

    place(0)
    tokens = x_ref.shape[0]
    block = 512
    heads = GROUP // HEAD

    @pl.when(group == 0)
    def _():
        dx_ref[...] = dmix_ref[...]
        dmix_low[...] = low(dmix_ref[...])
        x_turned[...] = x_ref[...].T

    dc[...] = low(dot(dmix_low[...], wo_ref[...], NT))
    lanes_low = head_lanes(low_type)
    eighth = jnp.asarray(scale_scores, low_type)
    pick = (
        lax.broadcasted_iota(jnp.int32, (8, GROUP), 1) // HEAD
        == lax.broadcasted_iota(jnp.int32, (8, GROUP), 0)
    ).astype(wide_type)
    pick = low(pick)
    product = wide(dc[...]) * c_ref[...]
    product_high = low(product)
    product_rest = low(product - wide(product_high))
    inner = dot(pick, product_high, NT) + dot(pick, product_rest, NT)
    k_turned = qkv_ref[1].T
    dk[...] = jnp.zeros(dk.shape, wide_type)
    dv[...] = jnp.zeros(dv.shape, wide_type)
    for i in range(tokens // block):
        rows = slice(i * block, (i + 1) * block)
        q = qkv_ref[0, rows, :] * eighth
        q_heads = jnp.concatenate([q * lanes_low[h] for h in range(heads)], 0)
        dc_heads = jnp.concatenate([dc[rows, :] * lanes_low[h] for h in range(heads)], 0)
        for h in range(heads):
            part = slice(h * block, (h + 1) * block)
            scores = dot(qkv_ref[1], q_heads[part], NT)
            weight = jnp.exp(scores - stat_ref[0, h : h + 1, rows])
            weight_back = dot(qkv_ref[2], dc_heads[part], NT)
            weights[:, part] = low(weight)
            back = low(weight * (weight_back - inner[h : h + 1, rows]))
            scores_back[:, part] = back
            dq_turned[h * HEAD : (h + 1) * HEAD, rows] = dot(
                k_turned[h * HEAD : (h + 1) * HEAD], back
            )
        dv[...] += dot(weights[...], dc_heads)
        dk[...] += dot(scores_back[...], q_heads)
        if i == 0:
            place(1)
    dq = low(dq_turned[...].T * scale_scores)
    dk_low, dv_low = low(dk[...]), low(dv[...])
    vec_ref[...] = jnp.zeros(vec_ref.shape, wide_type)
    vec_ref[0:1] = jnp.sum(wide(dq), 0, keepdims=True)
    vec_ref[1:2] = jnp.sum(wide(dv_low), 0, keepdims=True)
    dx_ref[...] += (
        dot(dq, w_ref[0], NT) + dot(dk_low, w_ref[1], NT) + dot(dv_low, w_ref[2], NT)
    )
    for part, grad in enumerate((dq, dk_low, dv_low)):
        hold[...] = dot(x_turned[...], grad)
        emit(outs, part, hold)
    place(2)


def encoder_attend_back(
    dmix, x, qkv, context, stats, inward, outward, plan=None, guests=()
):
    tokens, width = x.shape
    groups = width // GROUP
    specs = grad_specs(3, width, GROUP, lambda g: (0, 0, g))
    guest_outs = plan.outs() if plan else []
    outs = pl.pallas_call(
        functools.partial(encoder_attend_back_kernel, plan),
        grid=(groups,),
        in_specs=[
            once(tokens, width),
            once(tokens, width),
            pl.BlockSpec((3, tokens, GROUP), lambda g: (0, 0, g)),
            pl.BlockSpec((tokens, GROUP), lambda g: (0, g)),
            pl.BlockSpec((1, 8, tokens), lambda g: (g, 0, 0)),
            pl.BlockSpec((3, width, GROUP), lambda g: (0, 0, g)),
            pl.BlockSpec((GROUP, width), lambda g: (g, 0)),
            *(plan.in_specs() if plan else []),
        ],
        out_specs=[
            full(tokens, width),
            pl.BlockSpec((8, GROUP), lambda g: (0, g)),
            *specs,
            *[spec for spec, _ in guest_outs],
        ],
        out_shape=[
            like((tokens, width), wide_type),
            like((8, width), wide_type),
            *grad_shapes(3, width, width),
            *[shape for _, shape in guest_outs],
        ],
        scratch_shapes=[
            VMEM((tokens, width), low_type),
            VMEM((width, tokens), low_type),
            VMEM((tokens, GROUP), low_type),
            VMEM((tokens, 4 * 512), low_type),
            VMEM((tokens, 4 * 512), low_type),
            VMEM((tokens, GROUP), wide_type),
            VMEM((tokens, GROUP), wide_type),
            VMEM((GROUP, tokens), wide_type),
            VMEM((width, GROUP), wide_type),
            *(plan.scratch() if plan else []),
        ],
        compiler_params=host_params(plan),
        cost_estimate=cost(5e10, 4e7, 1.3e7),
        name="encoder_attend_back",
    )(dmix, x, qkv, context, stats, inward, outward, *guests)
    main = len(outs) - len(guest_outs)
    return outs[:2], outs[2:main], outs[main:]


def mask_kernel(slots_ref, across_ref, down_ref):
    count, width = slots_ref.shape
    words = down_ref.shape[0] // 32
    block = 32
    row = lax.broadcasted_iota(jnp.int32, (32, width), 0)
    for start in range(0, words, block):

        def step(i, totals):
            piece = slots_ref[pl.ds(pl.multiple_of(i * 8, 8), 8), :]
            word = lax.shift_right_logical(piece, 5)
            bit = jnp.left_shift(jnp.int32(1), piece & 31)
            return tuple(
                total | jnp.where(word == start + w, bit, 0) for w, total in enumerate(totals)
            )

        zero = jnp.zeros((8, width), jnp.int32)
        totals = lax.fori_loop(0, count // 8, step, (zero,) * block)
        for w, total in enumerate(totals):
            joined = total[0:1]
            for k in range(1, 8):
                joined = joined | total[k : k + 1]
            bits = lax.shift_right_logical(jnp.broadcast_to(joined, (32, width)), row) & 1
            at = (start + w) * 32
            down_ref[at : at + 32, :] = (wide(bits) - 1.0) * 1e30
    across_ref[...] = down_ref[...].T


def slot_mask(slots, pool):
    queries = slots.shape[0]
    return pl.pallas_call(
        mask_kernel,
        out_shape=[like((queries, pool), wide_type), like((pool, queries), wide_type)],
        in_specs=[pl.BlockSpec(memory_space=VMEM)],
        out_specs=[pl.BlockSpec(memory_space=VMEM)] * 2,
        compiler_params=params(24),
        cost_estimate=cost(1e10, 1e6),
        name="slot_mask",
    )(slots.T)


def pick_kernel(table_ref, states_ref, out_ref):
    spot = lax.broadcasted_iota(jnp.int32, (table_ref.shape[0], states_ref.shape[0]), 1)
    chosen = low((spot == table_ref[...]).astype(wide_type))
    out_ref[...] = low(dot(chosen, states_ref[...]))


def pick_rows(table, states):
    tokens, width = states.shape
    return pl.pallas_call(
        pick_kernel,
        grid=(table.size // 256,),
        in_specs=[pl.BlockSpec((256, 1), lambda i: (i, 0)), full(tokens, width)],
        out_specs=pl.BlockSpec((256, width), lambda i: (i, 0)),
        out_shape=like((table.size, width), low_type),
        compiler_params=params(24),
        cost_estimate=cost(4e9, 5e6),
        name="pick_rows",
    )(table.reshape(-1, 1), states)


def spread_kernel(table_ref, rows_ref, out_ref, total):
    step = pl.program_id(0)
    spot = lax.broadcasted_iota(jnp.int32, (out_ref.shape[0], table_ref.shape[1]), 0)
    chosen = low((spot == table_ref[...]).astype(wide_type))
    part = dot(chosen, rows_ref[...])

    @pl.when(step == 0)
    def _():
        total[...] = part

    @pl.when(step != 0)
    def _():
        total[...] += part

    @pl.when(step == pl.num_programs(0) - 1)
    def _():
        out_ref[...] = low(total[...])


def spread_rows(table, rows, tokens):
    width = rows.shape[1]
    return pl.pallas_call(
        spread_kernel,
        grid=(table.size // 512,),
        in_specs=[
            pl.BlockSpec((1, 512), lambda i: (0, i)),
            pl.BlockSpec((512, width), lambda i: (i, 0)),
        ],
        out_specs=full(tokens, width),
        out_shape=like((tokens, width), low_type),
        scratch_shapes=[VMEM((tokens, width), wide_type)],
        compiler_params=params(24),
        cost_estimate=cost(4e9, 5e6),
        name="spread_rows",
    )(table.reshape(1, -1), rows)


def by_head(value, lanes):
    return jnp.concatenate([value * lane for lane in lanes], 0)


def own_lanes(stacked, lanes):
    rows = stacked.shape[0] // len(lanes)
    return sum(stacked[h * rows : (h + 1) * rows] * lane for h, lane in enumerate(lanes))


def softmax_rows(scores):
    top = jnp.max(scores, -1, keepdims=True)
    weights = jnp.exp(scores - top)
    return weights * (1.0 / jnp.sum(weights, -1, keepdims=True))


def self_mask(lengths_ref, size):
    row = lax.broadcasted_iota(jnp.int32, (size, size), 0)
    column = lax.broadcasted_iota(jnp.int32, (size, size), 1)
    row_part, column_part = jnp.zeros_like(row), jnp.zeros_like(row)
    end = jnp.int32(0)
    for n in range(lengths_ref.shape[0] - 1):
        end = end + lengths_ref[n]
        row_part += (row >= end).astype(jnp.int32)
        column_part += (column >= end).astype(jnp.int32)
    allowed = (row_part == column_part) & (column <= row)
    added = jnp.where(allowed, 0.0, -1e30)
    return jnp.concatenate([added] * (GROUP // HEAD), 0)


def groups_of(width):
    return [slice(g, g + GROUP) for g in range(0, width, GROUP)]


def self_kernel(
    lengths_ref, y_ref, w_ref, wo_ref, b_ref, n_ref, cw_ref, qkv_ref, c_ref, mixed_ref, cq_ref
):
    y = y_ref[...]
    lanes_low, lanes = head_lanes(low_type), head_lanes(wide_type)
    mask = self_mask(lengths_ref, y.shape[0])
    qkv_ref[0] = low(dot(y, w_ref[0]) + b_ref[0:1])
    qkv_ref[1] = low(dot(y, w_ref[1]))
    qkv_ref[2] = low(dot(y, w_ref[2]) + b_ref[1:2])
    for part in groups_of(y.shape[1]):
        q = qkv_ref[0, :, part] * jnp.asarray(scale_scores, low_type)
        scores = dot(by_head(q, lanes_low), qkv_ref[1, :, part], NT) + mask
        weights = low(softmax_rows(scores))
        c_ref[:, part] = low(own_lanes(dot(weights, qkv_ref[2, :, part]), lanes))
    mixed = wide(y) + (dot(c_ref[...], wo_ref[...]) + b_ref[2:3])
    mixed_ref[...] = mixed
    first = low(norm_rows(mixed, n_ref[0, 0:1], n_ref[0, 1:2]))
    cq_ref[...] = low(dot(first, cw_ref[0]) + b_ref[3:4])


def self_forward(lengths, y, inward, outward, biases, norms, cross_inward):
    rows, width = y.shape
    return pl.pallas_call(
        self_kernel,
        grid=(1,),
        in_specs=[
            pl.BlockSpec(memory_space=pltpu.SMEM),
            full(rows, width),
            full(3, width, width),
            full(width, width),
            full(6, width),
            full(3, 2, width),
            full(1, width, width),
        ],
        out_specs=[
            full(3, rows, width),
            full(rows, width),
            full(rows, width),
            full(rows, width),
        ],
        out_shape=[
            like((3, rows, width), low_type),
            like((rows, width), low_type),
            like((rows, width), wide_type),
            like((rows, width), low_type),
        ],
        compiler_params=params(40),
        cost_estimate=cost(2e10, 7e6),
        name="self_forward",
    )(lengths, y, inward, outward, biases, norms, cross_inward)


def cross_kernel(pooled_ref, q_ref, mask_ref, w_ref, bg_ref, kv_ref, c_ref, stat_ref, scores, weights):
    rows = q_ref.shape[0]
    heads = GROUP // HEAD
    lanes_low, lanes = head_lanes(low_type), head_lanes(wide_type)
    kv_ref[0] = low(dot(pooled_ref[...], w_ref[1]))
    kv_ref[1] = low(dot(pooled_ref[...], w_ref[2]) + bg_ref[4:5])
    q = q_ref[...] * jnp.asarray(scale_scores, low_type)
    scores[...] = dot(by_head(q, lanes_low), kv_ref[0], NT)
    stats, scales = [], []
    for h in range(heads):
        part = slice(h * rows, (h + 1) * rows)
        masked = scores[part, :] + mask_ref[...]
        top = jnp.max(masked, -1, keepdims=True)
        weight = jnp.exp(masked - top)
        total = jnp.sum(weight, -1, keepdims=True)
        weights[part, :] = low(weight)
        stats.append(top + jnp.log(total))
        scales.append(lanes[h] * (1.0 / total))
    mixed = dot(weights[...], kv_ref[1])
    c_ref[...] = sum(mixed[h * rows : (h + 1) * rows] * scales[h] for h in range(heads))
    column = jnp.concatenate(stats, 0)
    stat_ref[0] = jnp.broadcast_to(column, (heads * rows, 128)).T[0:8]


def cross_forward(pooled, q, mask, inward, biases):
    slots, width = pooled.shape
    rows = q.shape[0]
    groups = width // GROUP
    stacked = rows * (GROUP // HEAD)
    return pl.pallas_call(
        cross_kernel,
        grid=(groups,),
        in_specs=[
            full(slots, width),
            pl.BlockSpec((rows, GROUP), lambda g: (0, g)),
            full(rows, slots),
            pl.BlockSpec((3, width, GROUP), lambda g: (0, 0, g)),
            pl.BlockSpec((6, GROUP), lambda g: (0, g)),
        ],
        out_specs=[
            pl.BlockSpec((2, slots, GROUP), lambda g: (0, 0, g)),
            pl.BlockSpec((rows, GROUP), lambda g: (0, g)),
            pl.BlockSpec((1, 8, stacked), lambda g: (g, 0, 0)),
        ],
        out_shape=[
            like((2, slots, width), low_type),
            like((rows, width), wide_type),
            like((groups, 8, stacked), wide_type),
        ],
        scratch_shapes=[VMEM((stacked, slots), wide_type), VMEM((stacked, slots), low_type)],
        compiler_params=params(),
        cost_estimate=cost(2e10, 1.2e7, 3e6),
        name="cross_forward",
    )(pooled, q, mask, inward, biases)


def middle_kernel(
    mixed_ref, c_ref, co_ref, b_ref, n_ref, e_ref, eb_ref, s_ref, sb_ref, grad_ref, *rest
):
    out_ref, joined_back_ref, dc_ref, vec_ref, deb_ref = rest[:5]
    hidden, slope, between, hold = rest[-4:]
    feed_ref, out_outs = rest[5], rest[6:-4]
    parts = feed_ref.shape[0]
    width = mixed_ref.shape[1]
    blocks = [slice(i * width, (i + 1) * width) for i in range(e_ref.shape[1] // width)]
    first = norm_rows(mixed_ref[...], n_ref[0, 0:1], n_ref[0, 1:2])
    context = low(c_ref[...])
    joined = first + (dot(context, co_ref[...]) + b_ref[5:6])
    second = norm_rows(joined, n_ref[1, 0:1], n_ref[1, 1:2])
    second_low = low(second)
    total = jnp.zeros(joined.shape, wide_type)
    for part in blocks:
        value, rate = gelu_parts(dot(second_low, e_ref[:, part]) + eb_ref[:, part])
        hidden[:, part] = low(value)
        slope[:, part] = rate
        total += dot(hidden[:, part], s_ref[part, :])
    summed = second + (total + sb_ref[...])
    out_ref[...] = low(norm_rows(summed, n_ref[2, 0:1], n_ref[2, 1:2]))
    summed_back, gain, offset = norm_rows_back(summed, n_ref[2, 0:1], wide(grad_ref[...]))
    summed_low = low(summed_back)
    vec_ref[...] = jnp.zeros(vec_ref.shape, wide_type)
    vec_ref[0:1] = gain
    vec_ref[1:2] = offset
    vec_ref[2:3] = jnp.sum(wide(summed_low), 0, keepdims=True)
    second_back = summed_back
    for part in blocks:
        before = low(dot(summed_low, s_ref[part, :], NT) * slope[:, part])
        between[:, part] = before
        deb_ref[:, part] = jnp.sum(wide(before), 0, keepdims=True)
        second_back += dot(before, e_ref[:, part], NT)
    joined_back, gain, offset = norm_rows_back(joined, n_ref[1, 0:1], second_back)
    joined_low = low(joined_back)
    joined_back_ref[...] = joined_back
    vec_ref[3:4] = gain
    vec_ref[4:5] = offset
    vec_ref[5:6] = jnp.sum(wide(joined_low), 0, keepdims=True)
    dc_ref[...] = low(dot(joined_low, co_ref[...], NT))
    for i, part in enumerate(blocks):
        rows = width // parts
        grad = low(dot(second_low, between[:, part], TN))
        for n in range(parts):
            feed_ref[n, i * rows : (i + 1) * rows, :] = grad[n * rows : (n + 1) * rows]
        grad = low(dot(hidden[:, part], summed_low, TN))
        rows, first = 4 * rows, i * parts // 4
        for n in range(parts // 4):
            feed_ref[first + n, rows:, :] = grad[n * rows : (n + 1) * rows]
    hold[...] = dot(context, joined_low, TN)
    emit(out_outs, 0, hold)


def middle(mixed, context, outward, biases, norms, expand, expand_bias, shrink, shrink_bias, grad):
    rows, width = mixed.shape
    total = expand.shape[1]
    parts = lax.axis_size("dp")
    ins = (
        mixed,
        context,
        outward,
        biases,
        norms,
        expand,
        expand_bias[None],
        shrink,
        shrink_bias[None],
        grad,
    )
    outs = pl.pallas_call(
        middle_kernel,
        grid=(1,),
        in_specs=[full(*value.shape) for value in ins],
        out_specs=[
            full(rows, width),
            full(rows, width),
            full(rows, width),
            full(8, width),
            full(1, total),
            full(parts, 2 * total // parts, width),
            *grad_specs(1, width, width),
        ],
        out_shape=[
            like((rows, width), low_type),
            like((rows, width), wide_type),
            like((rows, width), low_type),
            like((8, width), wide_type),
            like((1, total), wide_type),
            like((parts, 2 * total // parts, width), low_type),
            *grad_shapes(1, width, width),
        ],
        scratch_shapes=[
            VMEM((rows, total), low_type),
            VMEM((rows, total), wide_type),
            VMEM((rows, total), low_type),
            VMEM((width, width), wide_type),
        ],
        compiler_params=params(),
        cost_estimate=cost(2e10, 2.2e7),
        name="middle",
    )(*ins)
    return outs[:5], outs[5], outs[6:]


def cross_back_kernel(
    kv_ref, q_ref, c_ref, dc_ref, stat_ref, mask_ref, w_ref, dkv_ref, dq_ref, vec_ref, dpool_ref,
    total, weights, scores_back
):
    group = pl.program_id(0)
    rows = q_ref.shape[0]
    heads = GROUP // HEAD
    lanes_low, lanes = head_lanes(low_type), head_lanes(wide_type)
    q_heads = by_head(q_ref[...] * jnp.asarray(scale_scores, low_type), lanes_low)
    dc_heads = by_head(dc_ref[...], lanes_low)
    product = wide(dc_heads) * jnp.concatenate([c_ref[...]] * heads, 0)
    column = jnp.sum(product, -1, keepdims=True)
    inner = jnp.broadcast_to(column, (heads * rows, 128)).T[0:1]
    stat = stat_ref[0, 0:1]
    mask = jnp.concatenate([mask_ref[...]] * 2, 1)
    for h in range(0, heads, 2):
        part = slice(h * rows, (h + 2) * rows)
        weight = jnp.exp(dot(kv_ref[0], q_heads[part], NT) + mask - stat[:, part])
        weight_back = dot(kv_ref[1], dc_heads[part], NT)
        weights[:, part] = low(weight)
        scores_back[:, part] = low(weight * (weight_back - inner[:, part]))
    dk = low(dot(scores_back[...], q_heads))
    dv = low(dot(weights[...], dc_heads))
    dkv_ref[0] = dk
    dkv_ref[1] = dv
    dq = low(own_lanes(dot(scores_back[...], kv_ref[0], TN), lanes) * scale_scores)
    dq_ref[...] = dq
    vec_ref[...] = jnp.zeros(vec_ref.shape, wide_type)
    vec_ref[0:1] = jnp.sum(wide(dq), 0, keepdims=True)
    vec_ref[1:2] = jnp.sum(wide(dv), 0, keepdims=True)
    part = dot(dk, w_ref[1], NT) + dot(dv, w_ref[2], NT)

    @pl.when(group == 0)
    def _():
        total[...] = part

    @pl.when(group != 0)
    def _():
        total[...] += part

    @pl.when(group == pl.num_programs(0) - 1)
    def _():
        dpool_ref[...] = low(total[...])


def cross_back(kv, q, context, dc, stats, mask, inward):
    slots, width = kv.shape[1:]
    rows = q.shape[0]
    groups = width // GROUP
    stacked = rows * (GROUP // HEAD)
    column = pl.BlockSpec((rows, GROUP), lambda g: (0, g))
    return pl.pallas_call(
        cross_back_kernel,
        grid=(groups,),
        in_specs=[
            pl.BlockSpec((2, slots, GROUP), lambda g: (0, 0, g)),
            column,
            column,
            column,
            pl.BlockSpec((1, 8, stacked), lambda g: (g, 0, 0)),
            full(slots, rows),
            pl.BlockSpec((3, width, GROUP), lambda g: (0, 0, g)),
        ],
        out_specs=[
            pl.BlockSpec((2, slots, GROUP), lambda g: (0, 0, g)),
            column,
            pl.BlockSpec((8, GROUP), lambda g: (0, g)),
            full(slots, width),
        ],
        out_shape=[
            like((2, slots, width), low_type),
            like((rows, width), low_type),
            like((8, width), wide_type),
            like((slots, width), low_type),
        ],
        scratch_shapes=[
            VMEM((slots, width), wide_type),
            VMEM((slots, stacked), low_type),
            VMEM((slots, stacked), low_type),
        ],
        compiler_params=params(),
        cost_estimate=cost(3e10, 2.2e7, 3e6),
        name="cross_back",
    )(kv, q, context, dc, stats, mask, inward)


def cross_grads_kernel(pooled_ref, dkv_ref, mixed_ref, dq_ref, n_ref, *rest):
    outs, (turned, hold) = rest[:-2], rest[-2:]

    @pl.when(pl.program_id(0) == 0)
    def _():
        turned[...] = pooled_ref[...].T

    first = low(norm_rows(mixed_ref[...], n_ref[0, 0:1], n_ref[0, 1:2]))
    hold[...] = dot(first, dq_ref[...], TN)
    emit(outs, 0, hold)
    hold[...] = dot(turned[...], dkv_ref[0])
    emit(outs, 1, hold)
    hold[...] = dot(turned[...], dkv_ref[1])
    emit(outs, 2, hold)


def cross_grads(pooled, dkv, mixed, dq, norms):
    slots, width = pooled.shape
    rows = mixed.shape[0]
    return pl.pallas_call(
        cross_grads_kernel,
        grid=(width // GROUP,),
        in_specs=[
            full(slots, width),
            pl.BlockSpec((2, slots, GROUP), lambda g: (0, 0, g)),
            full(rows, width),
            pl.BlockSpec((rows, GROUP), lambda g: (0, g)),
            full(3, 2, width),
        ],
        out_specs=grad_specs(3, width, GROUP, lambda g: (0, 0, g)),
        out_shape=grad_shapes(3, width, width),
        scratch_shapes=[VMEM((width, slots), low_type), VMEM((width, GROUP), wide_type)],
        compiler_params=params(48),
        cost_estimate=cost(1e10, 1.5e7),
        name="cross_grads",
    )(pooled, dkv, mixed, dq, norms)


def self_back_kernel(
    lengths_ref, y_ref, mixed_ref, jb_ref, cdq_ref, qkv_ref, c_ref, w_ref, wo_ref, cw_ref, n_ref,
    dy_ref, vec_ref, *rest
):
    outs, (dqkv, hold) = rest[:-2], rest[-2:]
    width = y_ref.shape[1]
    y = y_ref[...]
    lanes_low, lanes = head_lanes(low_type), head_lanes(wide_type)
    mask = self_mask(lengths_ref, y.shape[0])
    first_back = jb_ref[...] + dot(cdq_ref[...], cw_ref[0], NT)
    mixed_back, gain, offset = norm_rows_back(mixed_ref[...], n_ref[0, 0:1], first_back)
    mixed_low = low(mixed_back)
    vec_ref[...] = jnp.zeros(vec_ref.shape, wide_type)
    vec_ref[0:1] = gain
    vec_ref[1:2] = offset
    vec_ref[2:3] = jnp.sum(wide(mixed_low), 0, keepdims=True)
    dc = low(dot(mixed_low, wo_ref[...], NT))
    for part in groups_of(width):
        q_heads = by_head(qkv_ref[0, :, part] * jnp.asarray(scale_scores, low_type), lanes_low)
        dc_heads = by_head(dc[:, part], lanes_low)
        weights = softmax_rows(dot(q_heads, qkv_ref[1, :, part], NT) + mask)
        weights_back = dot(dc_heads, qkv_ref[2, :, part], NT)
        inner = jnp.sum(weights * weights_back, -1, keepdims=True)
        scores_back = low(weights * (weights_back - inner))
        dq = own_lanes(dot(scores_back, qkv_ref[1, :, part]), lanes) * scale_scores
        dqkv[0, :, part] = low(dq)
        dqkv[1, :, part] = low(dot(scores_back, q_heads, TN))
        dqkv[2, :, part] = low(dot(low(weights), dc_heads, TN))
    vec_ref[3:4] = jnp.sum(wide(dqkv[0]), 0, keepdims=True)
    vec_ref[4:5] = jnp.sum(wide(dqkv[2]), 0, keepdims=True)
    dy_ref[...] = (
        mixed_back
        + dot(dqkv[0], w_ref[0], NT)
        + (dot(dqkv[1], w_ref[1], NT) + dot(dqkv[2], w_ref[2], NT))
    )
    for part in range(3):
        hold[...] = dot(y, dqkv[part], TN)
        emit(outs, part, hold)
    hold[...] = dot(c_ref[...], mixed_low, TN)
    emit(outs, 3, hold)


def self_back(lengths, y, mixed, joined_back, dq, qkv, context, inward, outward, cross_inward, norms):
    rows, width = y.shape
    ins = (y, mixed, joined_back, dq, qkv, context, inward, outward)
    outs = pl.pallas_call(
        self_back_kernel,
        grid=(1,),
        in_specs=[
            pl.BlockSpec(memory_space=pltpu.SMEM),
            *[full(*value.shape) for value in ins],
            full(1, width, width),
            full(3, 2, width),
        ],
        out_specs=[full(rows, width), full(8, width), *grad_specs(4, width, width)],
        out_shape=[
            like((rows, width), wide_type),
            like((8, width), wide_type),
            *grad_shapes(4, width, width),
        ],
        scratch_shapes=[VMEM((3, rows, width), low_type), VMEM((width, width), wide_type)],
        compiler_params=params(48),
        cost_estimate=cost(2e10, 1.5e7),
        name="self_back",
    )(lengths, *ins, cross_inward, norms)
    return outs[:2], outs[2:]


CUT = 192
HALF = CUT // 2
MESH = pl.DeviceIdType.MESH


def shifted(value, axis, by):
    length = lax.axis_size(axis)
    return lax.ppermute(value, axis, [(i, (i + by) % length) for i in range(length)])


def add_rows(to, other, rows):
    def step(i, carry):
        at = pl.ds(pl.multiple_of(i * 32, 32), 32)
        to[at, :] = low(wide(to[at, :]) + wide(other[at, :]))
        return carry

    lax.fori_loop(0, rows // 32, step, 0)


def partners():
    me, section = lax.axis_index("dp"), lax.axis_index("section")
    return (
        {"dp": me + 1 - 2 * (me % 2)},
        {"dp": me + 2 - 4 * ((me // 2) % 2)},
        {"dp": me + 4 - 8 * (me // 4)},
        {"section": section + 1 - 2 * (section % 2)},
        {"section": section + 2 - 4 * (section // 2)},
    )


def on_section(*sections):
    section = lax.axis_index("section")
    wanted = section == sections[0]
    for other in sections[1:]:
        wanted = wanted | (section == other)
    return pl.when(wanted)


def greet():
    barrier = pltpu.get_barrier_semaphore()
    for partner in partners():
        pl.semaphore_signal(barrier, 1, device_id=partner, device_id_type=MESH)

    @on_section(1, 2)
    def _():
        other = {"section": 3 - lax.axis_index("section")}
        pl.semaphore_signal(barrier, 1, device_id=other, device_id_type=MESH)
        pl.semaphore_wait(barrier, 6)

    @on_section(0, 3)
    def _():
        pl.semaphore_wait(barrier, 5)


def laid_out(pieces):
    out, at = [], 0
    for n, first, size in pieces:
        row = first
        while row < first + size:
            rows = min(CUT - at % CUT, first + size - row)
            out.append((n, row, rows, at // CUT, at % CUT))
            row, at = row + rows, at + rows
    return tuple(out), at // CUT


class Plan:
    def __init__(
        self, pieces, arrived, schedule, collective_id, onward=False, vector=0, moved=()
    ):
        self.arrays = 1 + max(piece[0] for piece in pieces)
        self.schedule, self.collective_id = schedule, collective_id
        self.sources, self.fresh = laid_out(pieces)
        self.from_kernels = tuple(arrived)
        arrived = sum(self.from_kernels)
        self.arrived, self.onward = arrived, onward
        self.vector = vector
        self.vector_order = (1, 2, 0, 3, 4)
        self.moved = tuple(moved)
        self.late = arrived + (self.fresh if onward else 0)
        self.ins = 2 * self.arrays + len(self.from_kernels) + len(self.moved) + (1 if vector else 0)

    def in_specs(self):
        anywhere = pl.BlockSpec(memory_space=pl.ANY)
        count = self.ins - (1 if self.vector else 0)
        return [anywhere] * count + ([pl.BlockSpec(memory_space=VMEM)] if self.vector else [])

    def outs(self):
        out = []
        if not self.onward:
            out.append((pl.BlockSpec(memory_space=pl.ANY), like((self.fresh * CUT, WIDTH), low_type)))
        if self.late:
            out.append((pl.BlockSpec(memory_space=pl.ANY), like((self.late * CUT, WIDTH), low_type)))
        for value in self.moved:
            out.append((pl.BlockSpec(memory_space=pl.ANY), value))
        if self.vector:
            out.append((pl.BlockSpec(memory_space=VMEM), like((self.vector, WIDTH), wide_type)))
        return out

    def scratch(self):
        dma = pltpu.SemaphoreType.DMA
        fresh, late, arrived = self.fresh, max(self.late, 1), max(self.arrived, 1)
        most = max(fresh, late)
        count = len(self.sources)
        return [
            VMEM((fresh, 4, CUT, WIDTH), low_type),
            VMEM((fresh, 4, CUT, WIDTH), low_type),
            VMEM((fresh, 2, 2, HALF, WIDTH), low_type),
            VMEM((fresh, 2, HALF, WIDTH), low_type),
            VMEM((arrived, CUT, WIDTH if self.late else 128), low_type),
            VMEM((late, CUT, WIDTH if self.late else 128), low_type),
            VMEM((late, HALF, WIDTH if self.late else 128), low_type),
            VMEM((late, CUT, WIDTH if self.late else 128), low_type),
            VMEM((5, self.vector or 8, WIDTH), wide_type),
            dma((count,)),
            dma((count,)),
            dma((count,)),
            dma((3, fresh, 3)),
            dma((3, fresh, 3)),
            dma((late, 5)),
            dma((late, 5)),
            dma((arrived,)),
            dma((2, most)),
            dma((5,)),
            dma((5,)),
            dma((max(len(self.moved), 1),)),
            dma((max(len(self.moved), 1),)),
        ]

    def open(self, ins, outs, scratch):
        return Sums(self, ins, outs, scratch)


class Sums:
    def __init__(self, plan, ins, outs, scratch):
        count = plan.arrays
        outs, ins = list(outs), list(ins)
        self.plan = plan
        self.keeps, self.sends = ins[:count], ins[count : 2 * count]
        ins = ins[2 * count :]
        self.arrived = [ins.pop(0) for _ in plan.from_kernels]
        self.moved = [ins.pop(0) for _ in plan.moved]
        self.vec_ref = ins.pop(0) if plan.vector else None
        self.shard_out = None if plan.onward else outs.pop(0)
        self.late_out = outs.pop(0) if plan.late else None
        self.moved_out = [outs.pop(0) for _ in plan.moved]
        self.vec_out = outs.pop(0) if plan.vector else None
        (
            self.own,
            self.from_core,
            self.from_one,
            self.from_two,
            self.waiting,
            self.from_outer,
            self.from_inner,
            self.whole,
            self.vec_in,
            self.load_sems,
            self.core_send,
            self.core_recv,
            self.send_sems,
            self.recv_sems,
            self.line_send,
            self.line_recv,
            self.arrive_sems,
            self.out_sems,
            self.vec_send,
            self.vec_recv,
            self.moved_send,
            self.moved_recv,
        ) = scratch
        self.core, self.over_x, self.over_y = partners()[:3]
        section = lax.axis_index("section")
        side = section // 2
        self.mine = pl.multiple_of(side * HALF, HALF)
        self.other = pl.multiple_of((1 - side) * HALF, HALF)
        self.outer = {"section": 3 * side}
        self.inner = {"section": 2 - side}
        self.inward = {"section": 1 + side}

    def remote(self, source, to, send, recv, partner):
        return pltpu.make_async_remote_copy(
            src_ref=source,
            dst_ref=to,
            send_sem=send,
            recv_sem=recv,
            device_id=partner,
            device_id_type=MESH,
        )

    def load(self, s):
        n, row, rows, chunk, at = self.plan.sources[s]
        return pltpu.make_async_copy(
            self.keeps[n].at[:, pl.ds(row, rows)],
            self.own.at[chunk, :, pl.ds(at, rows)],
            self.load_sems.at[s],
        )

    def cross(self, s):
        n, row, rows, chunk, at = self.plan.sources[s]
        return self.remote(
            self.sends[n].at[:, pl.ds(row, rows)],
            self.from_core.at[chunk, :, pl.ds(at, rows)],
            self.core_send.at[s],
            self.core_recv.at[s],
            self.core,
        )

    def arrive(self, k):
        at, source = k, 0
        while at >= self.plan.from_kernels[source]:
            at, source = at - self.plan.from_kernels[source], source + 1
        return pltpu.make_async_copy(
            self.arrived[source].at[pl.ds(at * CUT, CUT)],
            self.waiting.at[k],
            self.arrive_sems.at[k],
        )

    def summed(self, k):
        if k < self.plan.arrived:
            return self.waiting.at[k]
        return self.own.at[k - self.plan.arrived, 0]

    def pairs(self, stage, c):
        own, upper, lower = self.own, pl.ds(0, HALF), pl.ds(HALF, HALF)
        if stage == 1:
            return (
                (own.at[c, 1, upper], self.from_one.at[c, 0, 0], self.over_x),
                (own.at[c, 3, upper], self.from_one.at[c, 0, 1], self.over_x),
                (own.at[c, pl.ds(2, 2), lower], self.from_one.at[c, 1], self.over_y),
            )
        return (
            (own.at[c, 2, upper], self.from_two.at[c, 0], self.over_y),
            (own.at[c, 1, lower], self.from_two.at[c, 1], self.over_x),
        )

    def copies(self, stage, c):
        return [
            self.remote(
                source, to, self.send_sems.at[stage, c, k], self.recv_sems.at[stage, c, k], partner
            )
            for k, (source, to, partner) in enumerate(self.pairs(stage, c))
        ]

    def start(self, stage, c):
        for copy in self.copies(stage, c):
            copy.start()

    def line_copy(self, n, k):
        mine, other = pl.ds(self.mine, HALF), pl.ds(self.other, HALF)
        whole = self.whole.at[k]
        source, to, partner = (
            (self.summed(k), self.from_outer.at[k], self.inward),
            (self.summed(k).at[other], self.from_inner.at[k], self.inner),
            (whole.at[mine], whole.at[mine], self.inner),
            (whole.at[mine], whole.at[mine], self.outer),
            (whole.at[other], whole.at[other], self.outer),
        )[n]
        return self.remote(source, to, self.line_send.at[k, n], self.line_recv.at[k, n], partner)

    def line(self, stage, k):
        if stage == "go":

            @on_section(0, 3)
            def _():
                self.line_copy(0, k).start()

            return
        if stage == 6:

            @on_section(0, 3)
            def _():
                self.line_copy(3, k).wait_recv()
                self.line_copy(4, k).wait_recv()

            self.late_copy(k).start()
            return

        @on_section(1, 2)
        def _():
            self.line_copy(stage - 3, k).wait_recv()
            if stage == 3:
                add_rows(self.summed(k), self.from_outer.at[k], CUT)
                self.line_copy(1, k).start()
            elif stage == 4:
                rows = pl.ds(self.mine, HALF)
                self.whole[k, rows, :] = low(
                    wide(self.summed(k)[rows, :]) + wide(self.from_inner[k])
                )
                self.line_copy(2, k).start()
                self.line_copy(3, k).start()
            else:
                self.line_copy(4, k).start()

    def line_sent(self, k):
        @on_section(0, 3)
        def _():
            self.line_copy(0, k).wait_send()

        @on_section(1, 2)
        def _():
            for n in range(1, 5):
                self.line_copy(n, k).wait_send()

    def shard_copy(self, c):
        return pltpu.make_async_copy(
            self.own.at[c, 0], self.shard_out.at[pl.ds(c * CUT, CUT)], self.out_sems.at[0, c]
        )

    def late_copy(self, k):
        return pltpu.make_async_copy(
            self.whole.at[k], self.late_out.at[pl.ds(k * CUT, CUT)], self.out_sems.at[1, k]
        )

    def moved_copy(self, n):
        return self.remote(
            self.moved[n],
            self.moved_out[n],
            self.moved_send.at[n],
            self.moved_recv.at[n],
            partners()[4],
        )

    def vec_copy(self, stage):
        return self.remote(
            self.vec_out,
            self.vec_in.at[stage],
            self.vec_send.at[stage],
            self.vec_recv.at[stage],
            partners()[self.plan.vector_order[stage]],
        )

    def vec_step(self, stage):
        if stage:
            self.vec_copy(stage - 1).wait()
            self.vec_out[...] += self.vec_in[stage - 1]
        else:
            self.vec_out[...] = self.vec_ref[...]
        if stage < 5:
            self.vec_copy(stage).start()

    def begin(self):
        greet()
        for s in range(len(self.plan.sources)):
            self.cross(s).start()
            self.load(s).start()
        for k in range(self.plan.arrived):
            self.arrive(k).start()
        for n in range(len(self.moved)):
            self.moved_copy(n).start()

    def step(self, stage, c):
        if stage == "vec":
            self.vec_step(c)
            return
        if stage == "go":
            self.arrive(c).wait()
            self.line("go", c)
            return
        if stage > 2:
            self.line(stage, c)
            return
        if stage == 0:
            for s, source in enumerate(self.plan.sources):
                if source[3] == c:
                    self.load(s).wait()
                    self.cross(s).wait_recv()
            for at in range(4):
                add_rows(self.own.at[c, at], self.from_core.at[c, at], CUT)
            self.start(1, c)
            return
        for copy in self.copies(stage, c):
            copy.wait_recv()
        upper, lower = pl.ds(0, HALF), pl.ds(HALF, HALF)
        if stage == 1:
            for k in range(2):
                add_rows(self.own.at[c, 2 * k, upper], self.from_one.at[c, 0, k], HALF)
                add_rows(self.own.at[c, k, lower], self.from_one.at[c, 1, k], HALF)
            self.start(2, c)
        else:
            add_rows(self.own.at[c, 0, upper], self.from_two.at[c, 0], HALF)
            add_rows(self.own.at[c, 0, lower], self.from_two.at[c, 1], HALF)
            if self.plan.onward:
                self.line("go", self.plan.arrived + c)
            else:
                self.shard_copy(c).start()

    def finish(self):
        for n in range(len(self.moved)):
            self.moved_copy(n).wait()
        for s in range(len(self.plan.sources)):
            self.cross(s).wait_send()
        for c in range(self.plan.fresh):
            for stage in (1, 2):
                for copy in self.copies(stage, c):
                    copy.wait_send()
            if not self.plan.onward:
                self.shard_copy(c).wait()
        for k in range(self.plan.late):
            self.line_sent(k)
            self.late_copy(k).wait()

    def slot(self, grid_step, steps, slots, slot):
        for n in range(steps):
            wanted = self.plan.schedule.get(n * slots + slot, ())
            if not wanted:
                continue

            @pl.when(grid_step == n)
            def _(wanted=wanted):
                for stage, c in wanted:
                    if stage == "begin":
                        self.begin()
                    elif stage == "finish":
                        self.finish()
                    else:
                        self.step(stage, c)


def last_sums_kernel(plan, *refs):
    ins, rest = refs[: plan.ins], refs[plan.ins :]
    count = len(plan.outs())
    sums = plan.open(ins, rest[:count], rest[count:])
    sums.begin()
    for stage, c in plan.schedule:
        sums.step(stage, c)
    sums.finish()


def last_sums(plan, pairs, arrived, vector):
    outs = plan.outs()
    return pl.pallas_call(
        functools.partial(last_sums_kernel, plan),
        in_specs=plan.in_specs(),
        out_specs=[spec for spec, _ in outs],
        out_shape=[shape for _, shape in outs],
        scratch_shapes=plan.scratch(),
        compiler_params=params(60, collective_id=plan.collective_id, has_side_effects=True),
        cost_estimate=cost(1e8, 1e8),
        name="last_sums",
    )(*[p[0] for p in pairs], *[p[1] for p in pairs], *arrived, vector)


def feed_plan(moved):
    schedule = {
        0: [("begin", 0)],
        1: [(0, 0), (0, 1), (0, 2)],
        9: [(1, 0), (1, 1), (1, 2)],
        11: [(2, 0), (2, 1), (2, 2), ("finish", 0)],
    }
    return Plan(((0, 0, 288), (1, 0, 96), (2, 0, 192)), (), schedule, 1, moved=moved)


def attend_plan():
    schedule = {
        0: [("begin", 0), ("vec", 0)],
        1: [("vec", 1), (0, 0), (0, 1), (0, 2), (0, 3), (0, 4)],
        3: [("vec", 2)],
        4: [("vec", 3)],
        6: [("vec", 4), (1, 0), (1, 1), (1, 2)],
        7: [("vec", 5), (1, 3), (1, 4)],
        8: [(2, 0), (2, 1), (2, 2), (2, 3), (2, 4), ("finish", 0)],
    }
    return Plan(((0, 192, 192), (1, 0, 384), (2, 0, 384)), (), schedule, 2, vector=32)


def last_plan():
    order = [("vec", 0), *[("go", k) for k in range(5)], ("vec", 1), (0, 0), ("vec", 2), (0, 1)]
    order += [("vec", 3), (1, 0), (1, 1), (3, 0), (2, 0), (2, 1), (3, 1), (4, 0), (3, 2), (4, 1)]
    order += [(5, 0), (3, 3), (4, 2), (5, 1), (6, 0), (3, 4), ("vec", 4), (4, 3), (5, 2), (6, 1)]
    order += [(3, 5), (4, 4), (5, 3), (6, 2), (3, 6), (4, 5), (5, 4), (6, 3), (4, 6), (5, 5)]
    order += [(6, 4), ("vec", 5), (5, 6), (6, 5), (6, 6)]
    return Plan(((0, 0, 288), (1, 0, 96)), (5,), order, 3, onward=True, vector=8)


def unpack_kernel(feed_ref, first_ref, last_ref, vec_ref, bias_ref, *outs):
    (
        e_in, e_out, e_bias, e_norm, e_expand, e_expand_bias, e_shrink, e_shrink_bias,
        s_in, s_out, c_in, c_out, d_bias, d_norm, d_expand, d_expand_bias, d_shrink, d_shrink_bias,
    ) = outs
    rows = e_out.shape[0]

    def rows_of(ref, at, count=1):
        return wide(ref[at * rows : (at + count) * rows, :])

    for i in range(4):
        part = slice(i * WIDTH, (i + 1) * WIDTH)
        d_expand[:, part] = rows_of(feed_ref, i)
        e_expand[:, part] = rows_of(last_ref, 2 + i)
    d_shrink[...] = rows_of(feed_ref, 4, 4)
    for i in range(3):
        c_in[i] = rows_of(first_ref, i)
        e_in[i] = rows_of(last_ref, 10 + i)
    c_out[...] = rows_of(first_ref, 3)
    s_in[0] = rows_of(first_ref, 4)
    s_in[1] = rows_of(first_ref, 5)
    s_in[2] = rows_of(last_ref, 0)
    s_out[...] = rows_of(last_ref, 1)
    e_shrink[...] = rows_of(last_ref, 6, 4)
    e_out[...] = rows_of(last_ref, 13)
    me = lax.axis_index("dp")
    mine = pltpu.roll(vec_ref[...], WIDTH - me * rows, 1)
    e_bias[0:2] = pltpu.roll(bias_ref[...], WIDTH - me * rows, 1)[0:2, 0:rows]
    e_bias[2:3] = mine[2:3, 0:rows]
    e_norm[0] = mine[3:5, 0:rows]
    e_norm[1] = mine[5:7, 0:rows]
    e_shrink_bias[...] = mine[11:12, 0:rows]
    d_bias[...] = mine[12:18, 0:rows]
    for i in range(3):
        d_norm[i] = mine[18 + 2 * i : 20 + 2 * i, 0:rows]
    d_shrink_bias[...] = mine[28:29, 0:rows]
    for at, to in ((7, e_expand_bias), (24, d_expand_bias)):
        row = jnp.zeros((1, WIDTH), wide_type)
        for i in range(4):
            row = jnp.where(me // 2 == i, vec_ref[at + i : at + i + 1, :], row)
        to[...] = jnp.where(me % 2 == 0, row[:, : WIDTH // 2], row[:, WIDTH // 2 :])


def unpack(feed, first, last, vector, biases):
    rows, width = WIDTH // 8, WIDTH
    square, cube = (rows, width), (3, rows, width)
    wide_one, tall_one = (rows, 4 * width), (4 * rows, width)
    shapes = [
        cube, square, (3, rows), (2, 2, rows), wide_one, (1, 4 * rows), tall_one, (1, rows),
        cube, square, cube, square, (6, rows), (3, 2, rows), wide_one, (1, 4 * rows), tall_one,
        (1, rows),
    ]
    here = pl.BlockSpec(memory_space=VMEM)
    return pl.pallas_call(
        unpack_kernel,
        in_specs=[here] * 5,
        out_specs=[here] * len(shapes),
        out_shape=[like(shape, wide_type) for shape in shapes],
        compiler_params=params(),
        cost_estimate=cost(1e7, 1.3e7),
        name="unpack",
    )(feed, first, last, vector, biases)


def sum_whole(grads):
    parts = lax.axis_size("dp")
    packed = []
    for grad in grads:
        count, rows, columns = grad.shape
        cut = grad.reshape(count, parts, rows // parts, columns // WIDTH, WIDTH)
        packed.append(cut.transpose(1, 0, 3, 2, 4).reshape(parts, -1, WIDTH))
    shard = lax.psum_scatter(jnp.concatenate(packed, 1), "dp", scatter_dimension=0, tiled=True)[0]
    total = wide(lax.psum(shard, "section"))
    outs, at = [], 0
    for grad in grads:
        count, rows, columns = grad.shape
        size = grad.size // parts // WIDTH
        cut = total[at : at + size].reshape(count, columns // WIDTH, rows // parts, WIDTH)
        outs.append(cut.transpose(0, 2, 1, 3).reshape(count * rows // parts, columns))
        at += size
    return outs


def beside(shard):
    rows = shard.shape[0] // 4
    return shard.reshape(4, rows, WIDTH).transpose(1, 0, 2).reshape(rows, 4 * WIDTH)


def sum_any(grads, d_feed, vectors):
    e_in, e_out, e_expand, e_shrink, s_all, c_in, c_out = sum_whole([grad[0] for grad in grads])
    d_feed = wide(lax.psum(d_feed, "section"))
    d_expand, d_shrink = d_feed[: d_feed.shape[0] // 2], d_feed[d_feed.shape[0] // 2 :]
    flat = lax.psum(jnp.concatenate([v.reshape(-1) for v in vectors]), ("dp", "section"))
    parts, mine = lax.axis_size("dp"), lax.axis_index("dp")
    outs, at = [], 0
    for v in vectors:
        whole = flat[at : at + v.size].reshape(v.shape)
        at += v.size
        size = v.shape[-1] // parts
        outs.append(lax.dynamic_slice_in_dim(whole, mine * size, size, v.ndim - 1))
    rows = WIDTH // parts
    return (
        e_in.reshape(3, rows, WIDTH),
        e_out,
        outs[0],
        outs[1],
        beside(e_expand),
        outs[2],
        e_shrink,
        outs[3],
        s_all[: 3 * rows].reshape(3, rows, WIDTH),
        s_all[3 * rows :],
        c_in.reshape(3, rows, WIDTH),
        c_out,
        outs[4],
        outs[5],
        beside(d_expand),
        outs[6],
        d_shrink,
        outs[7],
    )


def on_device(
    encoder_input,
    decoder_input,
    cotangent,
    pool_table,
    retrieved,
    decoder_lengths,
    encoder_inward,
    encoder_outward,
    encoder_biases,
    encoder_norms,
    encoder_expand,
    encoder_expand_bias,
    encoder_shrink,
    encoder_shrink_bias,
    self_inward,
    self_outward,
    cross_inward,
    cross_outward,
    decoder_biases,
    decoder_norms,
    decoder_expand,
    decoder_expand_bias,
    decoder_shrink,
    decoder_shrink_bias,
):
    x = encoder_input[0]
    half_way = lax.axis_size("section") // 2
    queries = decoder_input.shape[1]
    topk = retrieved.shape[2]
    rows_low = shifted(jnp.concatenate([decoder_input[0], cotangent[0]], 0), "section", -half_way)
    y, grad = rows_low[:queries], rows_low[queries:]
    lengths_row = jnp.pad(decoder_lengths[0], ((0, 0), (0, topk - decoder_lengths.shape[2])))
    integers = shifted(
        jnp.concatenate([retrieved[0], pool_table[0, 0].reshape(-1, topk), lengths_row], 0),
        "section",
        -half_way,
    )
    slots = integers[:queries]
    table = integers[queries:-1].reshape(-1)
    lengths = integers[-1, : decoder_lengths.shape[2]]
    owners = pool_table.shape[2]

    qkv, context, context_low, stats, mixed = encoder_attend(
        x, encoder_inward, encoder_outward, encoder_biases
    )
    hidden, slope, summed, states = encoder_feed(
        mixed,
        encoder_norms,
        encoder_expand,
        encoder_expand_bias,
        encoder_shrink,
        encoder_shrink_bias,
    )
    picked = pick_rows(table, states).reshape(owners, -1, WIDTH)
    pooled = lax.all_to_all(picked, "dp", split_axis=0, concat_axis=0, tiled=True)
    pooled = pooled.reshape(-1, WIDTH)

    mask_across, mask_down = slot_mask(slots, pooled.shape[0])
    self_qkv, self_context, self_mixed, cross_q = self_forward(
        lengths, y, self_inward, self_outward, decoder_biases, decoder_norms, cross_inward
    )
    kv, cross_context, cross_stats = cross_forward(
        pooled, cross_q, mask_across, cross_inward, decoder_biases
    )
    (out, joined_back, dc, mid_vec, mid_expand), d_feed, d_cross_out = middle(
        self_mixed,
        cross_context,
        cross_outward,
        decoder_biases,
        decoder_norms,
        decoder_expand,
        decoder_expand_bias,
        decoder_shrink,
        decoder_shrink_bias,
        grad,
    )
    d_feed = lax.psum_scatter(d_feed, "dp", scatter_dimension=0, tiled=True)[0]
    dkv, dq, cross_vec, dpool = cross_back(
        kv, cross_q, cross_context, dc, cross_stats, mask_down, cross_inward
    )
    returned = lax.all_to_all(
        dpool.reshape(owners, -1, WIDTH), "dp", split_axis=0, concat_axis=0, tiled=True
    )
    d_cross_in = cross_grads(pooled, dkv, self_mixed, dq, decoder_norms)
    (dy, self_vec), d_self = self_back(
        lengths,
        y,
        self_mixed,
        joined_back,
        dq,
        self_qkv,
        self_context,
        self_inward,
        self_outward,
        cross_inward,
        decoder_norms,
    )
    states_back = spread_rows(table, returned.reshape(-1, WIDTH), x.shape[0])

    hosts = paired()
    plan = feed_plan([like(out.shape, out.dtype), like(dy.shape, dy.dtype)]) if hosts else None
    pairs = (d_cross_in, d_cross_out, d_self)
    guests = [pair[k] for k in range(2) for pair in pairs] + [out, dy] if hosts else []
    (dmix, feed_vec, feed_expand), (e_expand, e_shrink, e_out), from_feed = encoder_feed_back(
        states_back,
        summed,
        mixed,
        hidden,
        slope,
        context_low,
        encoder_norms,
        encoder_expand,
        encoder_shrink,
        plan,
        guests,
    )
    if hosts:
        decoder_out, decoder_grad = from_feed[1:]
    else:
        decoder_out = shifted(out, "section", half_way)
        decoder_grad = shifted(dy, "section", half_way)
    rest = [
        jnp.concatenate([jnp.zeros((2, WIDTH), wide_type), feed_vec[5:6]], 0),
        jnp.stack([feed_vec[3:5], feed_vec[0:2]]),
        feed_expand[0],
        feed_vec[2],
        jnp.concatenate([self_vec[3:5], self_vec[2:3], cross_vec[0:2], mid_vec[5:6]], 0),
        jnp.stack([self_vec[0:2], mid_vec[3:5], mid_vec[0:2]]),
        mid_expand[0],
        mid_vec[2],
    ]
    plan = attend_plan() if hosts else None
    if hosts:
        guests = [pair[k] for k in range(2) for pair in (d_self, e_expand, e_shrink)]
        flat = jnp.concatenate([v.reshape(-1) for v in rest])
        flat = jnp.pad(flat, (0, 32 * WIDTH - flat.size)).reshape(32, WIDTH)
        guests.append(flat)
        early, dmix = lax.optimization_barrier(((d_feed, from_feed[0]), dmix))
        early = lax.psum(early, "section")
    (dx, attend_vec), e_in, from_attend = encoder_attend_back(
        dmix, x, qkv, context, stats, encoder_inward, encoder_outward, plan, guests
    )
    if hosts:
        last, vector = last_sums(last_plan(), (e_in, e_out), from_attend[:1], attend_vec)
        results = unpack(*early, last, from_attend[1], vector)
        results = [r[0] if n in (5, 7, 15, 17) else r for n, r in enumerate(results)]
    else:
        results = sum_any(
            [e_in, e_out, e_expand, e_shrink, d_self, d_cross_in, d_cross_out],
            d_feed,
            [rest[0] + jnp.pad(attend_vec[0:2], ((0, 1), (0, 0)))] + rest[1:],
        )
    return (decoder_out[None], dx[None], decoder_grad[None], *results)


def solution(mesh):
    in_specs = (
        P("section", "dp", None),
        P("section", "dp", None),
        P("section", "dp", None),
        P("section", "dp", None, None),
        P("section", "dp", None),
        P("section", "dp", None),
        P(),
        P(),
        P(),
        P(),
        P(),
        P(),
        P(),
        P(),
        P(),
        P(),
        P(),
        P(),
        P(),
        P(),
        P(),
        P(),
        P(),
        P(),
    )
    out_specs = (
        P("section", "dp", None),
        P("section", "dp", None),
        P("section", "dp", None),
        P(None, "dp", None),
        P("dp", None),
        P(None, "dp"),
        P(None, None, "dp"),
        P("dp", None),
        P("dp"),
        P("dp", None),
        P("dp"),
        P(None, "dp", None),
        P("dp", None),
        P(None, "dp", None),
        P("dp", None),
        P(None, "dp"),
        P(None, None, "dp"),
        P("dp", None),
        P("dp"),
        P("dp", None),
        P("dp"),
    )
    return jax.shard_map(
        on_device, mesh=mesh, in_specs=in_specs, out_specs=out_specs, check_vma=False
    )
```
